32 devices in a mesh: wide: 8 (over z, y), narrow: 4 (over x, core).
Axes of the slice: x: 2, y: 2, z: 4, core: 2. Of those that a mesh axis runs over, the one named last changes fastest.
Arguments:
- target_slot: int32 [1024], replicated, may hold values from 0 to 1023, as said below
- fields: bfloat16 [1024, 8, 4096], P(('wide', 'narrow')), as said below
Outputs:
- migrated: bfloat16 [1024, 8, 4096], P(('wide', 'narrow'))
- pressure: float32 [64, 512, 128], P('narrow', 'wide')
The draws below stay inside these ranges and needn't reach their ends.
Inputs may be any that keep to these rules, and one draw needn't show every extreme that they name: `target_slot`: A permutation of the patches. Owner w * 4 + n holds patches w * 4 + n times 32 onward, old and new. From one owner to any owner go at most 2 patches, and exactly 2 for some pairs in every draw; every owner receives exactly 32 patches. `fields`: fields 0, 1, 2 are velocity components along the three dimensions, field 3 is the density, between 0.6 and 8.1; the others are carried quantities.
All inputs are finite; a program needn't handle non-finite values.
Results may differ from the reference program's by a relative error of at most 0.0014.
Values may be sent and summed in bfloat16 or wider, within the bound.
A program may use at most 128 MiB of HBM per device.

```python
import jax
import jax.numpy as jnp
from jax import lax

PATCH = 16
NF = 8
BXP = 1
BYP = 4
BZP = 8
LEVELS = 3
BOTTOM = 16
OWNERS = 32
P_DEV = 32
PATCHES = 1024
CZ = 128
NX = 64
NY = 512
N_WIDE = 8
N_NARROW = 4


def slot_table(key):
    base = jax.random.fold_in(key, 11)
    subkeys = jax.random.split(base, 4)
    inward = jax.random.permutation(subkeys[0], OWNERS)
    outward = jax.random.permutation(subkeys[1], OWNERS)
    local_order = jax.vmap(lambda subkey: jax.random.permutation(subkey, P_DEV))(jax.random.split(subkeys[2], OWNERS))
    placing = jax.vmap(lambda subkey: jax.random.permutation(subkey, P_DEV))(jax.random.split(subkeys[3], OWNERS))
    offset = local_order // 2 % OWNERS
    destination = outward[(inward[:, None] + offset) % OWNERS]
    within = placing[destination, local_order]
    return (destination * P_DEV + within).reshape(-1).astype(jnp.int32)


def draw_target_slot(key, part):
    return slot_table(key)


def draw_fields(key, part):
    subkeys = jax.random.split(jax.random.fold_in(key, 23), 5)
    cells = PATCH ** 3
    velocity = jnp.clip(jax.random.normal(subkeys[1], (PATCHES, 3, cells), jnp.float32), -4.0, 4.0)
    density = jnp.exp(jax.random.uniform(subkeys[3], (PATCHES, 1, cells), jnp.float32, jnp.log(0.6), jnp.log(8.0)))
    carried = jnp.clip(jax.random.normal(subkeys[4], (PATCHES, NF - 4, cells), jnp.float32), -4.0, 4.0)
    return jnp.concatenate([velocity, density, carried], axis=1).astype(jnp.bfloat16)


def setup_inputs(seed: int = 0) -> dict:
    seeds = jax.random.split(jax.random.key(seed), 3)
    return {
        "target_slot": draw_target_slot(jax.random.fold_in(seeds[2], 71), 0),
        "fields": draw_fields(jax.random.fold_in(seeds[2], 71), 0),
    }


DAMPING = 0.8


def neighbours(values, direction):
    length = values.shape[direction]
    zero_plane = jnp.zeros_like(lax.slice_in_dim(values, 0, 1, axis=direction))
    lower_side = jnp.concatenate([zero_plane, lax.slice_in_dim(values, 0, length - 1, axis=direction)], direction)
    upper_side = jnp.concatenate([lax.slice_in_dim(values, 1, length, axis=direction), zero_plane], direction)
    return lower_side, upper_side


def face_along(density, direction):
    zero_plane = jnp.zeros_like(lax.slice_in_dim(density, 0, 1, axis=direction))
    padded = jnp.concatenate([zero_plane, density, zero_plane], direction)
    length = padded.shape[direction]
    return 2.0 / (lax.slice_in_dim(padded, 0, length - 1, axis=direction) + lax.slice_in_dim(padded, 1, length, axis=direction))


def split_faces(face, direction):
    length = face.shape[direction]
    return lax.slice_in_dim(face, 0, length - 1, axis=direction), lax.slice_in_dim(face, 1, length, axis=direction)


def apply_padded(values, face_set, level_scale):
    running = None
    for direction in range(3):
        lower_side, upper_side = neighbours(values, direction)
        low_face, high_face = split_faces(face_set[direction], direction)
        face_term = high_face * (values - upper_side) + low_face * (values - lower_side)
        running = face_term if running is None else running + face_term
    return level_scale * running


def diagonal_of(face_set, level_scale):
    running = None
    for direction in range(3):
        low_face, high_face = split_faces(face_set[direction], direction)
        face_term = low_face + high_face
        running = face_term if running is None else running + face_term
    return level_scale * running


def coarsen_faces(face_set):
    face_x, face_y, face_z = face_set
    picked = face_x[::2]
    coarse_x = picked.reshape(picked.shape[0], picked.shape[1] // 2, 2, picked.shape[2] // 2, 2).mean(axis=(2, 4))
    picked = face_y[:, ::2]
    coarse_y = picked.reshape(picked.shape[0] // 2, 2, picked.shape[1], picked.shape[2] // 2, 2).mean(axis=(1, 4))
    picked = face_z[:, :, ::2]
    coarse_z = picked.reshape(picked.shape[0] // 2, 2, picked.shape[1] // 2, 2, picked.shape[2]).mean(axis=(1, 3))
    return coarse_x, coarse_y, coarse_z


def restrict_mean(values):
    shape = values.shape
    return values.reshape(shape[0] // 2, 2, shape[1] // 2, 2, shape[2] // 2, 2).mean(axis=(1, 3, 5))


def prolong(values):
    return jnp.repeat(jnp.repeat(jnp.repeat(values, 2, axis=0), 2, axis=1), 2, axis=2)


def sweep_padded(values, source_term, face_set, diagonal, level_scale):
    return values + DAMPING * (source_term - apply_padded(values, face_set, level_scale)) / diagonal


def bottom_solve(source_term, face_set, level_scale):
    diagonal = diagonal_of(face_set, level_scale)

    def one_sweep(sweep_index, current):
        return sweep_padded(current, source_term, face_set, diagonal, level_scale)

    return lax.fori_loop(0, BOTTOM, one_sweep, jnp.zeros_like(source_term))


def project(grid_fields):
    velocity_x, velocity_y, velocity_z, density = grid_fields[0], grid_fields[1], grid_fields[2], grid_fields[3]
    face_set = tuple(face_along(density, direction) for direction in range(3))
    differences = []
    for direction, component in enumerate((velocity_x, velocity_y, velocity_z)):
        lower_side, upper_side = neighbours(component, direction)
        differences.append(upper_side - lower_side)
    source_term = -0.5 * ((differences[0] + differences[1]) + differences[2])
    stored = []
    for level_index in range(LEVELS):
        level_scale = 0.25 ** level_index
        diagonal = diagonal_of(face_set, level_scale)
        values = DAMPING * source_term / diagonal
        values = sweep_padded(values, source_term, face_set, diagonal, level_scale)
        residual = source_term - apply_padded(values, face_set, level_scale)
        stored.append((values, source_term, face_set, diagonal, level_scale))
        source_term = restrict_mean(residual)
        face_set = coarsen_faces(face_set)
    level_scale = 0.25 ** LEVELS
    slab_width = source_term.shape[1] // N_WIDE
    pieces = []
    for group_index in range(N_WIDE):
        start_row = group_index * slab_width
        slab_faces = (face_set[0][:, start_row:start_row + slab_width],
                      face_set[1][:, start_row:start_row + slab_width + 1],
                      face_set[2][:, start_row:start_row + slab_width])
        pieces.append(bottom_solve(source_term[:, start_row:start_row + slab_width], slab_faces, level_scale))
    correction = jnp.concatenate(pieces, 1)
    for level_index in reversed(range(LEVELS)):
        values, source_term, face_set, diagonal, level_scale = stored[level_index]
        values = values + prolong(correction)
        values = sweep_padded(values, source_term, face_set, diagonal, level_scale)
        values = sweep_padded(values, source_term, face_set, diagonal, level_scale)
        correction = values
    return correction


def reference(target_slot, fields):
    migrated = jnp.zeros_like(fields).at[target_slot].set(fields)
    solve_part = migrated[:, :4].reshape(N_WIDE, N_NARROW, BXP, BYP, BZP, 4, PATCH, PATCH, PATCH)
    grid_fields = jnp.transpose(solve_part, (5, 1, 2, 6, 0, 3, 7, 4, 8)).reshape(4, NX, NY, CZ).astype(jnp.float32)
    pressure = project(grid_fields)
    return migrated, pressure
```

```python
import functools

import jax
import jax.numpy as jnp
from jax import lax
from jax.experimental import pallas as pl
from jax.experimental.pallas import tpu as pltpu
from jax.sharding import PartitionSpec as P

PATCH = 16
BYP = 4
BZP = 8
LEVELS = 3
BOTTOM = 16
DAMPING = 0.8
KEEP = 1.0 - DAMPING
SOLVED = 4
CAPACITY = 2
PER_OWNER = 32
X0 = PATCH
Y0 = PATCH * BYP
Z = PATCH * BZP
PAD = 8
EDGE = 4
HX = 2
HALO = (4, 2, 1)
FIELD_HALO = (3, 2, 2, 5)
HALO_PLANES = sum(FIELD_HALO)
CORNER = max(FIELD_HALO)
MESH = pl.DeviceIdType.MESH
VMEM_LIMIT = 60 * 1024 * 1024
SHARES = (2, 3, 4, 2, 2, 2, 2, 2, 2, 10)
OUT_GROUP = 8
SIDES = tuple((dx, dy) for dx in (-1, 0, 1) for dy in (-1, 0, 1) if dx or dy)


def dims(level):
    return X0 >> level, Y0 >> level


def solve_kernel(
    n_wide,
    n_narrow,
    target_ref,
    fields_ref,
    migrated_ref,
    pressure_ref,
    target,
    fields,
    solved,
    carried,
    arrived,
    moved,
    merged,
    pressure,
    send_index_v,
    receive_index_v,
    send_index,
    receive_index,
    turn,
    tmp,
    grids,
    sent_x,
    got_x,
    sent_y,
    got_y,
    sent_c,
    got_c,
    iterates,
    sent_rows,
    got_rows,
    face_x,
    face_y,
    face_zl,
    face_zh,
    inner_zl,
    inner_zh,
    diag,
    weight,
    source,
    answer,
    gather_faces,
    gather_source,
    coef,
    send_sem,
    recv_sem,
    gsend_sem,
    grecv_sem,
    carry_send_sem,
    carry_recv_sem,
    solved_send_sem,
    solved_recv_sem,
    local_sem,
    out_sem,
):
    wide = lax.axis_index("wide")
    narrow = lax.axis_index("narrow")
    owners = n_wide * n_narrow
    me = wide * n_narrow + narrow
    low = {-1: narrow > 0, 1: narrow < n_narrow - 1, 0: None}
    side_y = {-1: wide > 0, 1: wide < n_wide - 1, 0: None}

    def has(side):
        dx, dy = side
        if dx == 0:
            return side_y[dy]
        if dy == 0:
            return low[dx]
        return jnp.logical_and(low[dx], side_y[dy])

    def peer(side):
        return (wide + side[1], narrow + side[0])

    def back(side):
        return (-side[0], -side[1])

    others = [(wide, lax.rem(narrow + d, n_narrow)) for d in range(1, n_narrow)]

    target_copy = pltpu.make_async_copy(target_ref, target, local_sem.at[0])
    target_copy.start()
    fields_copy = pltpu.make_async_copy(fields_ref, fields, local_sem.at[1])
    fields_copy.start()

    def partner(k):
        distance = jnp.where(lax.rem(k, 2) == 1, owners // 2 + k // 2, k // 2)
        owner = jnp.bitwise_xor(me, distance)
        return owner, (owner // n_narrow, lax.rem(owner, n_narrow))

    barrier = pltpu.get_barrier_semaphore()

    def greet(k, carry):
        _, device = partner(k)
        pl.semaphore_signal(barrier, inc=1, device_id=device, device_id_type=MESH)
        return carry

    lax.fori_loop(1, owners, greet, 0)

    target_copy.wait()
    segments = Z // PER_OWNER
    own_row = target[pl.ds(me // segments, 1), :]
    lane_d = lax.broadcasted_iota(jnp.int32, (owners, Z), 1)
    owner_d = lax.broadcasted_iota(jnp.int32, (owners, Z), 0)
    mine = jnp.logical_and(
        lane_d // PER_OWNER == lax.rem(me, segments), own_row // PER_OWNER == owner_d
    )
    place = lax.rem(lane_d, PER_OWNER)
    low_place = jnp.min(jnp.where(mine, place, PER_OWNER - 1), axis=1, keepdims=True)
    high_place = jnp.max(jnp.where(mine, place, 0), axis=1, keepdims=True)
    send_index_v[0] = jnp.broadcast_to(low_place, (owners, Z))
    send_index_v[1] = jnp.broadcast_to(high_place, (owners, Z))
    index_copy = pltpu.make_async_copy(send_index_v, send_index, local_sem.at[2])
    index_copy.start()

    table = target[...]
    t_rows = table.shape[0]
    t_lane = lax.broadcasted_iota(jnp.int32, (t_rows, Z), 1)
    t_owner = lax.broadcasted_iota(jnp.int32, (t_rows, Z), 0) * segments + t_lane // PER_OWNER
    t_place = lax.rem(t_lane, PER_OWNER)
    seen = jnp.where(table // PER_OWNER == me, 1, 0)
    step = 1
    while step < PER_OWNER:
        seen = jnp.maximum(seen, jnp.where(t_place >= step, pltpu.roll(seen, step, 1), 0))
        step *= 2
    rank = jnp.where(t_place >= 1, pltpu.roll(seen, 1, 1), 0)
    slot = t_owner * CAPACITY + rank
    for q in range(PER_OWNER):
        hit = jnp.where(table == me * PER_OWNER + q, slot, 0)
        receive_index_v[q : q + 1, :] = jnp.max(hit, axis=0, keepdims=True)
    slots_q = jnp.max(receive_index_v[...], axis=1, keepdims=True)
    receive_index_v[...] = jnp.broadcast_to(slots_q, (PER_OWNER, Z))
    receive_copy = pltpu.make_async_copy(receive_index_v, receive_index, local_sem.at[3])
    receive_copy.start()

    index_copy.wait()
    fields_copy.wait()
    pl.semaphore_wait(barrier, owners - 1)

    def block(owner):
        return pl.ds(owner * CAPACITY, CAPACITY)

    def bulk(packed, landed, send, recv, k, incoming=False):
        owner, device = partner(k)
        return pltpu.make_async_remote_copy(
            src_ref=packed.at[block(me if incoming else owner)],
            dst_ref=landed.at[block(owner if incoming else me)],
            send_sem=send.at[k],
            recv_sem=recv.at[k],
            device_id=device,
            device_id_type=MESH,
        )

    solved_bulk = functools.partial(bulk, solved, arrived, solved_send_sem, solved_recv_sem)
    carried_bulk = functools.partial(bulk, carried, moved, carry_send_sem, carry_recv_sem)

    def pack_solved(k, carry):
        owner, _ = partner(k)
        for r in range(CAPACITY):
            solved[owner * CAPACITY + r] = fields[send_index[r, owner, 0], :SOLVED]
        solved_bulk(k).start()
        return carry

    def pack_carried(k, carry):
        owner, _ = partner(k)
        for r in range(CAPACITY):
            carried[owner * CAPACITY + r] = fields[send_index[r, owner, 0], SOLVED:]
        return carry

    lax.fori_loop(1, owners, pack_solved, 0)
    for r in range(CAPACITY):
        patch = fields[send_index[r, me, 0]]
        arrived[me * CAPACITY + r] = patch[:SOLVED]
        moved[me * CAPACITY + r] = patch[SOLVED:]
    lax.fori_loop(1, owners, pack_carried, 0)

    bounds = [
        1 + (owners - 1) * sum(SHARES[:k]) // sum(SHARES) for k in range(len(SHARES) + 1)
    ]
    pushed = []

    def push():
        turn_now = len(pushed)
        pushed.append(turn_now)
        if bounds[turn_now] == bounds[turn_now + 1]:
            return

        def begin(k, carry):
            carried_bulk(k).start()
            return carry

        lax.fori_loop(bounds[turn_now], bounds[turn_now + 1], begin, 0)

    for level in range(LEVELS):
        X, Y = dims(level)
        p = iterates[level]
        for e in (2,) if level == 0 else (0, 2):

            @pl.when(jnp.logical_not(low[-1]))
            def _(p=p, e=e, Y=Y):
                p[e, :HX] = jnp.zeros((HX, Y + 2 * PAD, Z), jnp.float32)

            @pl.when(jnp.logical_not(low[1]))
            def _(p=p, e=e, X=X, Y=Y):
                p[e, HX + X :] = jnp.zeros((HX, Y + 2 * PAD, Z), jnp.float32)

            @pl.when(jnp.logical_not(side_y[-1]))
            def _(p=p, e=e, X=X, Y=Y):
                p[e, :, :PAD] = jnp.zeros((X + 2 * HX, PAD, Z), jnp.float32)

            @pl.when(jnp.logical_not(side_y[1]))
            def _(p=p, e=e, X=X, Y=Y):
                p[e, :, PAD + Y :] = jnp.zeros((X + 2 * HX, PAD, Z), jnp.float32)

    receive_copy.wait()

    def solved_arrive(k, carry):
        solved_bulk(k, incoming=True).wait_recv()
        return carry

    lax.fori_loop(1, owners, solved_arrive, 0)
    push()

    lane = lax.broadcasted_iota(jnp.int32, (8, Z), 1)
    block_lane = lane // PATCH
    lower_bits = [(block_lane // s) % 2 == 1 for s in (1, 2, 4)]

    def to_grid(step, carry):
        b = step // X0
        i = step % X0
        at = pl.multiple_of(i * 2 * Z, 2 * Z)
        rows = []
        for c in range(BZP):
            both = arrived[receive_index[b * BZP + c, 0], :, pl.ds(at, 2 * Z)].astype(
                jnp.float32
            )
            rows.append(jnp.concatenate([both[:, :Z], both[:, Z:]], axis=0))
        for bit, s in zip(lower_bits, (1, 2, 4)):
            new = list(rows)
            for c in range(BZP):
                if c & s == 0:
                    lower, upper = rows[c], rows[c + s]
                    new[c] = jnp.where(bit, pltpu.roll(upper, PATCH * s, 1), lower)
                    new[c + s] = jnp.where(bit, upper, pltpu.roll(lower, Z - PATCH * s, 1))
            rows = new
        for j in range(8):
            turn[8 * j : 8 * j + 8, :] = rows[j]
        for half in range(2):
            y = pl.multiple_of(b * PATCH + half * 8, 8)
            for f, ref in enumerate(grids):
                values = turn[pl.ds(half * SOLVED + f, 8, stride=8), :]
                ref[i + FIELD_HALO[f], pl.ds(PAD + y, 8), :] = values
        return carry

    lax.fori_loop(0, BYP * X0, to_grid, 0, unroll=8)

    def known(side, values):
        return jnp.where(has(side), values.astype(jnp.float32), 0.0)

    planes = []
    for f, h in enumerate(FIELD_HALO):
        planes += [(f, h, j) for j in range(h)]
    for n, (f, h, j) in enumerate(planes):
        for side, x in ((0, j), (1, X0 - h + j)):
            sent_x[side, n] = grids[f][h + x, PAD : PAD + Y0, :].astype(jnp.bfloat16)
    at_row = lax.broadcasted_iota(jnp.int32, (PAD, Z), 0)

    def end_rows(end, x):
        y = (0, Y0 - PAD)[end]
        u, v, w, r = (
            grids[f][h + x, PAD + y : PAD + y + PAD, :] for f, h in enumerate(FIELD_HALO)
        )
        if end == 0:
            uvw = jnp.where(
                at_row < 2, u, jnp.where(at_row < 5, pltpu.roll(v, 2, 0), pltpu.roll(w, 5, 0))
            )
        else:
            uvw = jnp.where(
                at_row > 5, u, jnp.where(at_row > 2, pltpu.roll(v, 6, 0), pltpu.roll(w, 3, 0))
            )
        return r.astype(jnp.bfloat16), uvw.astype(jnp.bfloat16)

    def keep_rows(end, x, uvw, r):
        y = (0, PAD + Y0)[end]
        u, v, w = (
            (uvw, pltpu.roll(uvw, 2, 0), pltpu.roll(uvw, 5, 0)),
            (uvw, pltpu.roll(uvw, 6, 0), pltpu.roll(uvw, 3, 0)),
        )[end]
        for f, values in enumerate((u, v, w, r)):
            h = FIELD_HALO[f]
            if -h <= x < X0 + h:
                grids[f][h + x, y : y + PAD, :] = values

    for end in range(2):
        for i in range(X0):
            sent_y[end, i], sent_y[end, X0 + i] = end_rows(end, i)
        for j in range(CORNER):
            for side, x in ((0, j), (1, X0 - CORNER + j)):
                (
                    sent_c[2 * side + end, j],
                    sent_c[2 * side + end, CORNER + j],
                ) = end_rows(end, x)

    def field_refs(side):
        dx, dy = side
        if dy == 0:
            return sent_x.at[(dx + 1) // 2], got_x.at[(1 - dx) // 2]
        if dx == 0:
            return sent_y.at[(dy + 1) // 2], got_y.at[(1 - dy) // 2]
        return sent_c.at[dx + 1 + (dy + 1) // 2], got_c.at[1 - dx + (1 - dy) // 2]

    def level_refs(level, e):
        X, Y = dims(level)
        p = iterates[level]

        def refs(side):
            dx, dy = side
            if dx == 0:
                which = e // 2
                return (
                    sent_rows[level].at[which, (dy + 1) // 2],
                    got_rows[level].at[which, (1 - dy) // 2],
                )
            h = HX if dy == 0 else 1
            src_x, dst_x, n_x = {
                -1: (HX, HX + X, h),
                0: (HX, HX, X),
                1: (HX + X - h, HX - h, h),
            }[dx]
            src_y, dst_y, n_y = {
                -1: (PAD, PAD + Y, PAD),
                0: (PAD, PAD, Y),
                1: (Y, 0, PAD),
            }[dy]
            return (
                p.at[e, pl.ds(src_x, n_x), pl.ds(src_y, n_y)],
                p.at[e, pl.ds(dst_x, n_x), pl.ds(dst_y, n_y)],
            )

        return refs

    def pack_rows(level, e):
        X, Y = dims(level)
        p = iterates[level]
        for end, y, first_row in ((0, PAD, 0), (1, Y, 6)):
            for g in range(X // 4):
                tile = None
                for k in range(4):
                    rows = p[e, HX + 4 * g + k, y : y + PAD, :]
                    shift = (2 * k - first_row) % PAD
                    rows = pltpu.roll(rows, shift, 0) if shift else rows
                    tile = rows if tile is None else jnp.where(at_row >= 2 * k, rows, tile)
                sent_rows[level][e // 2, end, g] = tile

    def unpack_rows(level, e):
        X, Y = dims(level)
        p = iterates[level]
        for end, y, first_row in ((0, 0, 6), (1, PAD + Y, 0)):
            for g in range(X // 4):
                tile = known((0, 2 * end - 1), got_rows[level][e // 2, end, g])
                for k in range(4):
                    shift = (first_row - 2 * k) % PAD
                    p[e, HX + 4 * g + k, y : y + PAD, :] = (
                        pltpu.roll(tile, shift, 0) if shift else tile
                    )

    drains = []

    def level_exchange(level, e, move):
        pack_rows(level, e)
        exchange(level_refs(level, e), move)
        unpack_rows(level, e)

    def exchange(refs, move):
        def copy(side, incoming=False):
            src, dst = refs(back(side) if incoming else side)
            return pltpu.make_async_remote_copy(
                src_ref=src,
                dst_ref=dst,
                send_sem=send_sem.at[move, SIDES.index(side)],
                recv_sem=recv_sem.at[move, SIDES.index(side if incoming else back(side))],
                device_id=peer(side),
                device_id_type=MESH,
            )

        def each(act):
            for side in SIDES:

                @pl.when(has(side))
                def _(side=side):
                    act(side)

        each(lambda side: copy(side).start())
        push()
        each(lambda side: copy(side, incoming=True).wait_recv())
        drains.append(lambda: each(lambda side: copy(side).wait_send()))

    exchange(field_refs, 0)

    for n, (f, h, j) in enumerate(planes):
        for dx, x in ((-1, j), (1, h + X0 + j)):
            at = (dx + 1) // 2
            grids[f][x, PAD : PAD + Y0, :] = known((dx, 0), got_x[at, n])
    for end, dy in ((0, -1), (1, 1)):
        for i in range(X0):
            r, uvw = (known((0, dy), got_y[end, k * X0 + i]) for k in range(2))
            keep_rows(end, i, uvw, r)
        for j in range(CORNER):
            for side, dx, x in ((0, -1, j - CORNER), (1, 1, X0 + j)):
                r, uvw = (
                    known((dx, dy), got_c[2 * side + end, k * CORNER + j]) for k in range(2)
                )
                keep_rows(end, x, uvw, r)

    def lanes(values):
        return lax.broadcasted_iota(jnp.int32, values.shape, 1)

    def z_low(values, step):
        return jnp.where(lanes(values) < step, 0.0, pltpu.roll(values, step, 1))

    def z_high(values, step):
        return jnp.where(lanes(values) >= Z - step, 0.0, pltpu.roll(values, Z - step, 1))

    def keep_inner(level, i, zl, zh):
        step = 1 << level
        inner_zl[level][i] = jnp.where(lanes(zl) < step, 0.0, zl)
        inner_zh[level][i] = jnp.where(lanes(zh) >= Z - step, 0.0, zh)

    push()
    grid_u, grid_v, grid_w, grid_r = grids
    rows0 = Y0 + 2 * EDGE
    win0 = pl.ds(PAD - EDGE, rows0)

    def face(a, b):
        return 2.0 / jnp.maximum(a + b, 0.5)

    def faces(i, carry):
        here = grid_r[i + 1, win0, :]
        face_x[0][i] = face(grid_r[i, win0, :], here)
        face_y[0][i, :rows0, :] = face(grid_r[i + 1, pl.ds(PAD - EDGE - 1, rows0), :], here)
        last = PAD + EDGE + Y0
        face_y[0][i, rows0 : rows0 + EDGE, :] = face(
            grid_r[i + 1, last - 1 : last + EDGE - 1, :], grid_r[i + 1, last : last + EDGE, :]
        )
        zl, zh = face(z_low(here, 1), here), face(z_high(here, 1), here)
        face_zl[0][i] = zl
        face_zh[0][i] = zh
        keep_inner(0, i, zl, zh)
        return carry

    n_faces = X0 + 2 * HALO[0]
    lax.fori_loop(0, n_faces, faces, 0, unroll=4)
    face_x[0][n_faces] = face(grid_r[n_faces, win0, :], grid_r[n_faces + 1, win0, :])

    def inside_rows(level):
        Y = dims(level)[1]
        at = lax.broadcasted_iota(jnp.int32, (Y + 2 * EDGE, Z), 0)
        return jnp.logical_and(
            jnp.logical_or(side_y[-1], at >= EDGE), jnp.logical_or(side_y[1], at < EDGE + Y)
        )

    def weigh(level, i):
        X, Y = dims(level)
        h, rows = HALO[level], Y + 2 * EDGE
        total = face_x[level][i] + face_x[level][i + 1]
        total += face_y[level][i, :rows, :] + face_y[level][i, pl.ds(1, rows), :]
        total += face_zl[level][i] + face_zh[level][i]
        inside = jnp.logical_and(
            jnp.logical_or(low[-1], i >= h), jnp.logical_or(low[1], i < h + X)
        )
        w = jnp.where(jnp.logical_and(inside_rows(level), inside), DAMPING / total, 0.0)
        diag[level][i] = total
        weight[level][i] = w
        return w

    def first(j, carry):
        w = weigh(0, j + HALO[0] - HX)
        wz = grid_w[j + FIELD_HALO[2] - HX, win0, :]
        u_at, v_at = j + FIELD_HALO[0] - HX, j + FIELD_HALO[1] - HX
        du = grid_u[u_at + 1, win0, :] - grid_u[u_at - 1, win0, :]
        dv = (
            grid_v[v_at, pl.ds(PAD - EDGE + 1, rows0), :]
            - grid_v[v_at, pl.ds(PAD - EDGE - 1, rows0), :]
        )
        b = -0.5 * ((du + dv) + (z_high(wz, 1) - z_low(wz, 1)))
        source[0][j] = b
        iterates[0][0, j, win0, :] = w * b
        return carry

    lax.fori_loop(0, X0 + 2 * HX, first, 0, unroll=4)

    def z_bit(values, level):
        return (lanes(values) // (1 << level)) % 2 == 1

    def z_pair(values, level):
        step = 1 << level
        return values + jnp.where(
            z_bit(values, level), pltpu.roll(values, step, 1), pltpu.roll(values, Z - step, 1)
        )

    def z_even(values, level):
        return jnp.where(z_bit(values, level), pltpu.roll(values, 1 << level, 1), values)

    def z_odd(values, level):
        return jnp.where(z_bit(values, level), values, pltpu.roll(values, Z - (1 << level), 1))

    def coarse_faces(level, base, start, count, more=0):
        even = pl.ds(start, count, stride=2)
        even_y = pl.ds(start, count + more, stride=2)
        odd = pl.ds(start + 1, count, stride=2)
        after = pl.ds(start + 2, count, stride=2)
        fx, fy, zl, zh = (f[level] for f in (face_x, face_y, face_zl, face_zh))

        def cx(x):
            i = base + 2 * x
            return 0.25 * z_pair(fx[i, even, :] + fx[i, odd, :], level)

        def cy(x, rows):
            i = base + 2 * x
            return 0.25 * z_pair(fy[i, rows, :] + fy[i + 1, rows, :], level)

        def four(f, x):
            i = base + 2 * x
            return 0.25 * (
                (f[i, even, :] + f[i, odd, :]) + (f[i + 1, even, :] + f[i + 1, odd, :])
            )

        return (
            cx,
            lambda x: cy(x, even_y),
            lambda x: cy(x, after),
            lambda x: z_even(four(zl, x), level),
            lambda x: z_odd(four(zh, x), level),
        )

    for level in range(LEVELS - 1):
        X, Y = dims(level + 1)
        count = Y + EDGE
        n_planes = X + 2 * HALO[level + 1]
        cx, cyl, _, czl, czh = coarse_faces(level, 0, 0, count, more=1)
        rows = pl.ds(EDGE // 2, count)

        def coarsen(i, carry, level=level, rows=rows, count=count, cx=cx, cyl=cyl, czl=czl, czh=czh):
            face_x[level + 1][i, rows, :] = cx(i)
            face_y[level + 1][i, pl.ds(EDGE // 2, count + 1), :] = cyl(i)
            zl, zh = czl(i), czh(i)
            face_zl[level + 1][i, rows, :] = zl
            face_zh[level + 1][i, rows, :] = zh
            step = 1 << (level + 1)
            inner_zl[level + 1][i, rows, :] = jnp.where(lanes(zl) < step, 0.0, zl)
            inner_zh[level + 1][i, rows, :] = jnp.where(lanes(zh) >= Z - step, 0.0, zh)
            return carry

        lax.fori_loop(0, n_planes, coarsen, 0, unroll=3)
        face_x[level + 1][n_planes, rows, :] = cx(n_planes)

        def weigh_plane(i, carry, level=level):
            weigh(level + 1, i)
            return carry

        lax.fori_loop(0, n_planes, weigh_plane, 0, unroll=3)

    X, Y = dims(LEVELS)
    cx, cyl, cyh, czl, czh = coarse_faces(LEVELS - 1, HALO[LEVELS - 1], EDGE, Y)
    for x in range(X + 1):
        gather_faces[narrow, x] = cx(x)
    for x in range(X):
        for k, part in enumerate((cyl, cyh, czl, czh)):
            gather_faces[narrow, X + 1 + k * X + x] = part(x)

    def gather(ref, which):
        def copy(d, incoming=False):
            came = lax.rem(narrow + n_narrow - d, n_narrow) if incoming else narrow
            return pltpu.make_async_remote_copy(
                src_ref=ref.at[narrow],
                dst_ref=ref.at[came],
                send_sem=gsend_sem.at[which, d - 1],
                recv_sem=grecv_sem.at[which, d - 1],
                device_id=others[d - 1],
                device_id_type=MESH,
            )

        def start():
            for d in range(1, n_narrow):
                copy(d).start()

        def finish():
            for d in range(1, n_narrow):
                copy(d, incoming=True).wait_recv()

        def drain():
            for d in range(1, n_narrow):
                copy(d).wait_send()

        return start, finish, drain

    face_start, face_finish, face_drain = gather(gather_faces, 0)
    source_start, source_finish, source_drain = gather(gather_source, 1)
    face_start()

    def neighbour_sum(level, e, x, own):
        Y = dims(level)[1]
        p = iterates[level]
        step = 1 << level
        edge = 0 if own else EDGE
        start, rows = PAD - edge, Y + 2 * edge
        at = pl.ds(EDGE - edge, rows)
        i, j = x + HALO[level], x + HX
        here = p[e, j, pl.ds(start, rows), :]
        total = (
            face_x[level][i, at, :] * p[e, j - 1, pl.ds(start, rows), :]
            + face_x[level][i + 1, at, :] * p[e, j + 1, pl.ds(start, rows), :]
        )
        total += face_y[level][i, at, :] * p[e, j, pl.ds(start - 1, rows), :]
        total += face_y[level][i, pl.ds(EDGE - edge + 1, rows), :] * p[
            e, j, pl.ds(start + 1, rows), :
        ]
        total += inner_zl[level][i, at, :] * pltpu.roll(here, step, 1)
        total += inner_zh[level][i, at, :] * pltpu.roll(here, Z - step, 1)
        return here, total

    def sweep(level, e, x, own):
        Y = dims(level)[1]
        edge = 0 if own else EDGE
        here, total = neighbour_sum(level, e, x, own)
        w = weight[level][x + HALO[level], pl.ds(EDGE - edge, Y + 2 * edge), :]
        if e == 0:
            return (1.0 + KEEP) * here + w * total
        start = iterates[level][0, x + HX, pl.ds(PAD - edge, Y + 2 * edge), :]
        return (KEEP * here + start) + w * total

    def wide_sweep(level, e):
        X, Y = dims(level)

        def plane(j, carry):
            iterates[level][e + 1, j + HX - 1, pl.ds(PAD - EDGE, Y + 2 * EDGE), :] = sweep(
                level, e, j - 1, False
            )
            return carry

        lax.fori_loop(0, X + 2, plane, 0, unroll=3 if level == 0 else 2)

    for level in range(LEVELS):
        X, Y = dims(level)
        if level > 0:
            level_exchange(level, 0, level)
        wide_sweep(level, 0)
        h, half, last = HALO[level], Y // 2, level + 1 == LEVELS
        own_rows = pl.ds(EDGE, Y)

        def restrict(x, carry, level=level, Y=Y, h=h, half=half, last=last, own_rows=own_rows):
            both = None
            for k in range(2):
                fine = 2 * x + k
                here, total = neighbour_sum(level, 1, fine, True)
                b = source[0][fine + HX, own_rows, :] if level == 0 else source[level][fine]
                left = (b - diag[level][fine + h, own_rows, :] * here) + total
                both = left if both is None else both + left
            tmp[:Y, :] = both
            summed = (
                tmp[pl.ds(0, half, stride=2), :] + tmp[pl.ds(1, half, stride=2), :]
            )
            summed = 0.5 * z_pair(summed, level)
            if last:
                gather_source[narrow, x] = summed
            else:
                source[level + 1][x] = summed
                w = weight[level + 1][x + HALO[level + 1], pl.ds(EDGE, half), :]
                iterates[level + 1][0, x + HX, pl.ds(PAD, half), :] = w * summed
            return carry

        if last:
            for x in range(X // 2):
                restrict(x, 0)
        else:
            lax.fori_loop(0, X // 2, restrict, 0, unroll=4)

    source_start()
    push()
    face_finish()
    source_finish()
    X, Y = dims(LEVELS)
    step = 1 << LEVELS
    row = lax.broadcasted_iota(jnp.int32, (Y, Z), 0)
    col = lax.broadcasted_iota(jnp.int32, (Y, Z), 1)
    for n in range(n_narrow):
        for x in range(X):
            fxl, fxh = gather_faces[n, x], gather_faces[n, x + 1]
            fyl, fyh, fzl, fzh = (gather_faces[n, X + 1 + k * X + x] for k in range(4))
            total = ((fxl + fxh) + (fyl + fyh)) + (fzl + fzh)
            w = DAMPING / total
            at = n * X + x
            coef[0, at] = w * fxl
            coef[1, at] = w * fxh
            coef[2, at] = jnp.where(row == 0, 0.0, w * fyl)
            coef[3, at] = jnp.where(row == Y - 1, 0.0, w * fyh)
            coef[4, at] = jnp.where(col < step, 0.0, w * fzl)
            coef[5, at] = jnp.where(col >= Z - step, 0.0, w * fzh)
            coef[6, at] = w * gather_source[n, x]

    zero_plane = jnp.zeros((1, Y, Z), jnp.float32)

    def bottom(k, cur):
        new = KEEP * cur + coef[6]
        new += coef[0] * jnp.concatenate([zero_plane, cur[:-1]], axis=0)
        new += coef[1] * jnp.concatenate([cur[1:], zero_plane], axis=0)
        new += coef[2] * pltpu.roll(cur, 1, 1)
        new += coef[3] * pltpu.roll(cur, Y - 1, 1)
        new += coef[4] * pltpu.roll(cur, step, 2)
        new += coef[5] * pltpu.roll(cur, Z - step, 2)
        return new

    push()
    coef[7] = lax.fori_loop(0, BOTTOM - 1, bottom, coef[6], unroll=15)
    for x in range(X):
        answer[LEVELS][x] = coef[7, narrow * X + x]

    for level in reversed(range(LEVELS)):
        X, Y = dims(level)
        half = Y // 2

        def raised(x, carry, level=level, Y=Y, half=half):
            e = answer[level + 1][x // 2]
            tmp[pl.ds(0, half, stride=2), :] = e
            tmp[pl.ds(1, half, stride=2), :] = e
            iterates[level][2, x + HX, PAD : PAD + Y, :] = (
                iterates[level][1, x + HX, PAD : PAD + Y, :] + tmp[:Y, :]
            )
            return carry

        lax.fori_loop(0, X, raised, 0, unroll=4)
        level_exchange(level, 2, LEVELS + level)
        wide_sweep(level, 2)
        result = pressure if level == 0 else answer[level]

        def close(x, carry, level=level, result=result):
            result[x] = sweep(level, 3, x, True)
            return carry

        lax.fori_loop(0, X, close, 0, unroll=4)

    assert len(pushed) == len(SHARES)
    pressure_copy = pltpu.make_async_copy(pressure, pressure_ref, local_sem.at[4])
    pressure_copy.start()

    def merge_solved(q, carry):
        merged[q, :SOLVED] = arrived[receive_index[q, 0]]
        return carry

    lax.fori_loop(0, PER_OWNER, merge_solved, 0, unroll=4)

    def carried_arrive(k, carry):
        carried_bulk(k, incoming=True).wait_recv()
        return carry

    lax.fori_loop(1, owners, carried_arrive, 0)

    def out_copy(g):
        group = pl.ds(g * OUT_GROUP, OUT_GROUP)
        return pltpu.make_async_copy(merged.at[group], migrated_ref.at[group], out_sem.at[g])

    for g in range(PER_OWNER // OUT_GROUP):

        def merge_carried(q, carry):
            merged[q, SOLVED:] = moved[receive_index[q, 0]]
            return carry

        lax.fori_loop(g * OUT_GROUP, (g + 1) * OUT_GROUP, merge_carried, 0, unroll=4)
        out_copy(g).start()

    def end(k, carry):
        carried_bulk(k).wait_send()
        solved_bulk(k).wait_send()
        return carry

    lax.fori_loop(1, owners, end, 0)
    face_drain()
    source_drain()
    for drain in drains:
        drain()
    pressure_copy.wait()
    for g in range(PER_OWNER // OUT_GROUP):
        out_copy(g).wait()


def f32(*shape):
    return pltpu.VMEM(shape, jnp.float32)


def bf16(*shape):
    return pltpu.VMEM(shape, jnp.bfloat16)


def call_solve(n_wide, n_narrow, table, fields):
    per_owner, n_fields, cells = fields.shape
    owners = n_wide * n_narrow
    slots = owners * CAPACITY
    X3, Y3 = dims(LEVELS)
    levels = [(level, *dims(level)) for level in range(LEVELS)]
    faces = [f32(X + 2 * HALO[l], Y + 2 * EDGE, Z) for l, X, Y in levels]
    moves = 2 * LEVELS
    packs = {
        "solved": bf16(slots, SOLVED, cells),
        "carried": bf16(slots, n_fields - SOLVED, cells),
    }
    dma = pltpu.SemaphoreType.DMA
    scratch = [
        pltpu.VMEM(table.shape, jnp.int32),
        bf16(*fields.shape),
        packs["solved"],
        packs["carried"],
        packs["solved"],
        packs["carried"],
        bf16(*fields.shape),
        f32(X0, Y0, Z),
        pltpu.VMEM((CAPACITY, owners, Z), jnp.int32),
        pltpu.VMEM((per_owner, Z), jnp.int32),
        pltpu.SMEM((CAPACITY, owners, Z), jnp.int32),
        pltpu.SMEM((per_owner, Z), jnp.int32),
        f32(64, Z),
        f32(Y0, Z),
        [f32(X0 + 2 * h, Y0 + 2 * PAD, Z) for h in FIELD_HALO],
        bf16(2, HALO_PLANES, Y0, Z),
        bf16(2, HALO_PLANES, Y0, Z),
        bf16(2, 2 * X0, PAD, Z),
        bf16(2, 2 * X0, PAD, Z),
        bf16(4, 2 * CORNER, PAD, Z),
        bf16(4, 2 * CORNER, PAD, Z),
        [f32(4, X + 2 * HX, Y + 2 * PAD, Z) for l, X, Y in levels],
        [f32(2, 2, X // 4, PAD, Z) for l, X, Y in levels],
        [f32(2, 2, X // 4, PAD, Z) for l, X, Y in levels],
        [f32(X + 2 * HALO[l] + 1, Y + 2 * EDGE, Z) for l, X, Y in levels],
        [f32(X + 2 * HALO[l], Y + 2 * EDGE + 8, Z) for l, X, Y in levels],
        faces,
        faces,
        faces,
        faces,
        faces,
        faces,
        [f32(X0 + 2 * HX, Y0 + 2 * EDGE, Z)] + [f32(X, Y, Z) for l, X, Y in levels[1:]],
        [f32(*dims(level), Z) for level in range(LEVELS + 1)],
        f32(n_narrow, 5 * X3 + 1, Y3, Z),
        f32(n_narrow, X3, Y3, Z),
        f32(8, n_narrow * X3, Y3, Z),
        dma((moves, 8)),
        dma((moves, 8)),
        dma((2, n_narrow - 1)),
        dma((2, n_narrow - 1)),
        dma((owners,)),
        dma((owners,)),
        dma((owners,)),
        dma((owners,)),
        dma((5,)),
        dma((per_owner // OUT_GROUP,)),
    ]
    anywhere = pl.BlockSpec(memory_space=pl.ANY)
    return pl.pallas_call(
        functools.partial(solve_kernel, n_wide, n_narrow),
        out_shape=(
            jax.ShapeDtypeStruct(fields.shape, fields.dtype),
            jax.ShapeDtypeStruct((X0, Y0, Z), jnp.float32),
        ),
        in_specs=[anywhere, anywhere],
        out_specs=(anywhere, anywhere),
        scratch_shapes=scratch,
        compiler_params=pltpu.CompilerParams(
            collective_id=0, has_side_effects=True, vmem_limit_bytes=VMEM_LIMIT
        ),
        cost_estimate=pl.CostEstimate(
            flops=200_000_000, bytes_accessed=200_000_000, transcendentals=0
        ),
    )(table, fields)


def shards(n_wide, n_narrow, target_slot, fields):
    return call_solve(n_wide, n_narrow, target_slot.reshape(-1, Z), fields)


def solution(mesh):
    body = functools.partial(shards, mesh.shape["wide"], mesh.shape["narrow"])
    in_specs = (P(), P(("wide", "narrow"), None, None))
    out_specs = (P(("wide", "narrow"), None, None), P("narrow", "wide", None))
    return jax.shard_map(body, mesh=mesh, in_specs=in_specs, out_specs=out_specs, check_vma=False)
```

```python
import functools

import jax
import jax.numpy as jnp
from jax import lax
from jax.experimental import pallas as pl
from jax.experimental.pallas import tpu as pltpu
from jax.sharding import PartitionSpec as P

PATCH = 16
BYP = 4
BZP = 8
LEVELS = 3
BOTTOM = 16
DAMPING = 0.8
KEEP = 1.0 - DAMPING
SOLVED = 4
CAPACITY = 2
PER_OWNER = 32
X0 = PATCH
Y0 = PATCH * BYP
Z = PATCH * BZP
PAD = 8
EDGE = 4
HX = (2, 3, 2)
ROWS = (2, 4, 2)
CORNER_PLANES = (1, 3, 1)
HALO = (4, 2, 1)
FIELD_HALO = (3, 2, 2, 5)
HALO_PLANES = sum(FIELD_HALO)
CORNER = max(FIELD_HALO)
MESH = pl.DeviceIdType.MESH
SHARES = (1, 1, 2, 1, 1, 1, 1, 1, 7)
OUT_GROUP = 8
PIECES = 8
SIDES = tuple((dx, dy) for dx in (-1, 0, 1) for dy in (-1, 0, 1) if dx or dy)


def dims(level):
    return X0 >> level, Y0 >> level


def solve_kernel(
    n_wide,
    n_narrow,
    target_ref,
    fields_ref,
    migrated_ref,
    pressure_ref,
    target,
    fields,
    solved,
    carried,
    arrived,
    moved,
    merged,
    pressure,
    send_index_v,
    receive_index_v,
    send_index,
    receive_index,
    turn,
    tmp,
    grids,
    sent_x,
    got_x,
    sent_y,
    got_y,
    sent_c,
    got_c,
    iterates,
    sent_rows,
    got_rows,
    face_x,
    face_y,
    face_zl,
    face_zh,
    inner_zl,
    inner_zh,
    diag,
    weight,
    source,
    answer,
    near_answer,
    gather_faces,
    gather_source,
    coef,
    send_sem,
    recv_sem,
    gsend_sem,
    grecv_sem,
    carry_send_sem,
    carry_recv_sem,
    solved_send_sem,
    solved_recv_sem,
    local_sem,
    out_sem,
):
    wide = lax.axis_index("wide")
    narrow = lax.axis_index("narrow")
    owners = n_wide * n_narrow
    me = wide * n_narrow + narrow
    low = {-1: narrow > 0, 1: narrow < n_narrow - 1, 0: None}
    side_y = {-1: wide > 0, 1: wide < n_wide - 1, 0: None}

    def has(side):
        dx, dy = side
        if dx == 0:
            return side_y[dy]
        if dy == 0:
            return low[dx]
        return jnp.logical_and(low[dx], side_y[dy])

    def peer(side):
        return (wide + side[1], narrow + side[0])

    def back(side):
        return (-side[0], -side[1])

    others = [(wide, lax.rem(narrow + d, n_narrow)) for d in range(1, n_narrow)]

    target_copy = pltpu.make_async_copy(target_ref, target, local_sem.at[0])
    target_copy.start()
    fields_copy = pltpu.make_async_copy(fields_ref, fields, local_sem.at[1])
    fields_copy.start()

    def at_distance(distance):
        owner = jnp.bitwise_xor(me, distance)
        return owner, (owner // n_narrow, lax.rem(owner, n_narrow))

    def partner(k):
        return at_distance(jnp.where(lax.rem(k, 2) == 1, owners // 2 + k // 2, k // 2))

    barrier = pltpu.get_barrier_semaphore()

    def greet(k, carry):
        _, device = partner(k)
        pl.semaphore_signal(barrier, inc=1, device_id=device, device_id_type=MESH)
        return carry

    lax.fori_loop(1, owners, greet, 0)

    target_copy.wait()
    segments = Z // PER_OWNER
    own_row = target[pl.ds(me // segments, 1), :]
    lane_d = lax.broadcasted_iota(jnp.int32, (owners, Z), 1)
    owner_d = lax.broadcasted_iota(jnp.int32, (owners, Z), 0)
    mine = jnp.logical_and(
        lane_d // PER_OWNER == lax.rem(me, segments), own_row // PER_OWNER == owner_d
    )
    place = lax.rem(lane_d, PER_OWNER)
    low_place = jnp.min(jnp.where(mine, place, PER_OWNER - 1), axis=1, keepdims=True)
    high_place = jnp.max(jnp.where(mine, place, 0), axis=1, keepdims=True)
    send_index_v[0] = jnp.broadcast_to(low_place, (owners, Z))
    send_index_v[1] = jnp.broadcast_to(high_place, (owners, Z))
    index_copy = pltpu.make_async_copy(send_index_v, send_index, local_sem.at[2])
    index_copy.start()

    table = target[...]
    t_rows = table.shape[0]
    t_lane = lax.broadcasted_iota(jnp.int32, (t_rows, Z), 1)
    t_owner = lax.broadcasted_iota(jnp.int32, (t_rows, Z), 0) * segments + t_lane // PER_OWNER
    t_place = lax.rem(t_lane, PER_OWNER)
    seen = jnp.where(table // PER_OWNER == me, 1, 0)
    step = 1
    while step < PER_OWNER:
        seen = jnp.maximum(seen, jnp.where(t_place >= step, pltpu.roll(seen, step, 1), 0))
        step *= 2
    rank = jnp.where(t_place >= 1, pltpu.roll(seen, 1, 1), 0)
    slot = t_owner * CAPACITY + rank
    for q in range(PER_OWNER):
        hit = jnp.where(table == me * PER_OWNER + q, slot, 0)
        receive_index_v[q : q + 1, :] = jnp.max(hit, axis=0, keepdims=True)
    slots_q = jnp.max(receive_index_v[...], axis=1, keepdims=True)
    receive_index_v[...] = jnp.broadcast_to(slots_q, (PER_OWNER, Z))
    receive_copy = pltpu.make_async_copy(receive_index_v, receive_index, local_sem.at[3])
    receive_copy.start()

    index_copy.wait()
    fields_copy.wait()
    pl.semaphore_wait(barrier, owners - 1)

    def block(owner):
        return pl.ds(owner * CAPACITY, CAPACITY)

    def bulk(whom, packed, landed, send, recv, k, incoming=False):
        owner, device = whom(k)
        return pltpu.make_async_remote_copy(
            src_ref=packed.at[block(me if incoming else owner)],
            dst_ref=landed.at[block(owner if incoming else me)],
            send_sem=send.at[k],
            recv_sem=recv.at[k],
            device_id=device,
            device_id_type=MESH,
        )

    solved_bulk = functools.partial(bulk, partner, solved, arrived, solved_send_sem, solved_recv_sem)
    carried_bulk = functools.partial(bulk, at_distance, carried, moved, carry_send_sem, carry_recv_sem)

    def pack_solved(k, carry):
        owner, _ = partner(k)
        for r in range(CAPACITY):
            solved[owner * CAPACITY + r] = fields[send_index[r, owner, 0], :SOLVED]
        solved_bulk(k).start()
        return carry

    def pack_carried(k, carry):
        owner, _ = at_distance(k)
        for r in range(CAPACITY):
            carried[owner * CAPACITY + r] = fields[send_index[r, owner, 0], SOLVED:]
        return carry

    lax.fori_loop(1, owners, pack_solved, 0)
    for r in range(CAPACITY):
        patch = fields[send_index[r, me, 0]]
        arrived[me * CAPACITY + r] = patch[:SOLVED]
        moved[me * CAPACITY + r] = patch[SOLVED:]
    lax.fori_loop(1, owners, pack_carried, 0)

    half_way = owners // 2
    bounds = [1] + [
        half_way + half_way * sum(SHARES[:k]) // sum(SHARES) for k in range(len(SHARES) + 1)
    ]
    pushed = []

    def push():
        turn_now = len(pushed)
        pushed.append(turn_now)
        if bounds[turn_now] == bounds[turn_now + 1]:
            return

        def begin(k, carry):
            carried_bulk(k).start()
            return carry

        lax.fori_loop(bounds[turn_now], bounds[turn_now + 1], begin, 0)

    push()
    for level in range(LEVELS):
        X, Y = dims(level)
        p = iterates[level]
        hx = HX[level]
        for e in (2,) if level == 0 else (0, 2):

            @pl.when(jnp.logical_not(low[-1]))
            def _(p=p, e=e, Y=Y, hx=hx):
                p[e, :hx] = jnp.zeros((hx, Y + 2 * PAD, Z), jnp.float32)

            @pl.when(jnp.logical_not(low[1]))
            def _(p=p, e=e, X=X, Y=Y, hx=hx):
                p[e, hx + X :] = jnp.zeros((hx, Y + 2 * PAD, Z), jnp.float32)

            @pl.when(jnp.logical_not(side_y[-1]))
            def _(p=p, e=e, X=X, Y=Y, hx=hx):
                p[e, :, :PAD] = jnp.zeros((X + 2 * hx, PAD, Z), jnp.float32)

            @pl.when(jnp.logical_not(side_y[1]))
            def _(p=p, e=e, X=X, Y=Y, hx=hx):
                p[e, :, PAD + Y :] = jnp.zeros((X + 2 * hx, PAD, Z), jnp.float32)

    receive_copy.wait()

    def solved_arrive(k, carry):
        solved_bulk(k, incoming=True).wait_recv()
        return carry

    lax.fori_loop(1, owners, solved_arrive, 0)
    push()

    lane = lax.broadcasted_iota(jnp.int32, (8, Z), 1)
    block_lane = lane // PATCH
    lower_bits = [(block_lane // s) % 2 == 1 for s in (1, 2, 4)]

    def to_grid(step, carry):
        b = step // X0
        i = step % X0
        at = pl.multiple_of(i * 2 * Z, 2 * Z)
        rows = []
        for c in range(BZP):
            both = arrived[receive_index[b * BZP + c, 0], :, pl.ds(at, 2 * Z)].astype(
                jnp.float32
            )
            rows.append(jnp.concatenate([both[:, :Z], both[:, Z:]], axis=0))
        for bit, s in zip(lower_bits, (1, 2, 4)):
            new = list(rows)
            for c in range(BZP):
                if c & s == 0:
                    lower, upper = rows[c], rows[c + s]
                    new[c] = jnp.where(bit, pltpu.roll(upper, PATCH * s, 1), lower)
                    new[c + s] = jnp.where(bit, upper, pltpu.roll(lower, Z - PATCH * s, 1))
            rows = new
        for j in range(8):
            turn[8 * j : 8 * j + 8, :] = rows[j]
        for half in range(2):
            y = pl.multiple_of(b * PATCH + half * 8, 8)
            for f, ref in enumerate(grids):
                values = turn[pl.ds(half * SOLVED + f, 8, stride=8), :]
                ref[i + FIELD_HALO[f], pl.ds(PAD + y, 8), :] = values
        return carry

    lax.fori_loop(0, BYP * X0, to_grid, 0, unroll=8)

    def known(side, values):
        return jnp.where(has(side), values.astype(jnp.float32), 0.0)

    planes = []
    for f, h in enumerate(FIELD_HALO):
        planes += [(f, h, j) for j in range(h)]
    for n, (f, h, j) in enumerate(planes):
        for side, x in ((0, j), (1, X0 - h + j)):
            sent_x[side, n] = grids[f][h + x, PAD : PAD + Y0, :].astype(jnp.bfloat16)
    at_row = lax.broadcasted_iota(jnp.int32, (PAD, Z), 0)

    def end_rows(end, x):
        y = (0, Y0 - PAD)[end]
        u, v, w, r = (
            grids[f][h + x, PAD + y : PAD + y + PAD, :] for f, h in enumerate(FIELD_HALO)
        )
        if end == 0:
            uvw = jnp.where(
                at_row < 2, u, jnp.where(at_row < 5, pltpu.roll(v, 2, 0), pltpu.roll(w, 5, 0))
            )
        else:
            uvw = jnp.where(
                at_row > 5, u, jnp.where(at_row > 2, pltpu.roll(v, 6, 0), pltpu.roll(w, 3, 0))
            )
        return r.astype(jnp.bfloat16), uvw.astype(jnp.bfloat16)

    def keep_rows(end, x, uvw, r):
        y = (0, PAD + Y0)[end]
        u, v, w = (
            (uvw, pltpu.roll(uvw, 2, 0), pltpu.roll(uvw, 5, 0)),
            (uvw, pltpu.roll(uvw, 6, 0), pltpu.roll(uvw, 3, 0)),
        )[end]
        for f, values in enumerate((u, v, w, r)):
            h = FIELD_HALO[f]
            if -h <= x < X0 + h:
                grids[f][h + x, y : y + PAD, :] = values

    for end in range(2):
        for i in range(X0):
            sent_y[end, i], sent_y[end, X0 + i] = end_rows(end, i)
        for j in range(CORNER):
            for side, x in ((0, j), (1, X0 - CORNER + j)):
                (
                    sent_c[2 * side + end, j],
                    sent_c[2 * side + end, CORNER + j],
                ) = end_rows(end, x)

    def field_refs(side):
        dx, dy = side
        if dy == 0:
            return sent_x.at[(dx + 1) // 2], got_x.at[(1 - dx) // 2]
        if dx == 0:
            return sent_y.at[(dy + 1) // 2], got_y.at[(1 - dy) // 2]
        return sent_c.at[dx + 1 + (dy + 1) // 2], got_c.at[1 - dx + (1 - dy) // 2]

    def level_refs(level, e, into):
        X, Y = dims(level)
        p = iterates[level]
        hx = HX[level]

        def refs(side):
            dx, dy = side
            if dx == 0:
                which = into // 2
                return (
                    sent_rows[level].at[which, (dy + 1) // 2],
                    got_rows[level].at[which, (1 - dy) // 2],
                )
            h = hx if dy == 0 else CORNER_PLANES[level]
            src_x, dst_x, n_x = {
                -1: (hx, hx + X, h),
                0: (hx, hx, X),
                1: (hx + X - h, hx - h, h),
            }[dx]
            src_y, dst_y, n_y = {
                -1: (PAD, PAD + Y, PAD),
                0: (PAD, PAD, Y),
                1: (Y, 0, PAD),
            }[dy]
            return (
                p.at[e, pl.ds(src_x, n_x), pl.ds(src_y, n_y)],
                p.at[into, pl.ds(dst_x, n_x), pl.ds(dst_y, n_y)],
            )

        return refs

    def pack_rows(level, e, into):
        X, Y = dims(level)
        p, n = iterates[level], ROWS[level]
        per = PAD // n
        for end, y, first_row in ((0, PAD, 0), (1, Y, PAD - n)):
            for g in range(X // per):
                tile = None
                for k in range(per):
                    rows = p[e, HX[level] + per * g + k, y : y + PAD, :]
                    shift = (n * k - first_row) % PAD
                    rows = pltpu.roll(rows, shift, 0) if shift else rows
                    tile = rows if tile is None else jnp.where(at_row >= n * k, rows, tile)
                sent_rows[level][into // 2, end, g] = tile

    def unpack_rows(level, into):
        X, Y = dims(level)
        p, n = iterates[level], ROWS[level]
        per = PAD // n
        for end, y, first_row in ((0, 0, PAD - n), (1, PAD + Y, 0)):
            for g in range(X // per):
                tile = known((0, 2 * end - 1), got_rows[level][into // 2, end, g])
                for k in range(per):
                    shift = (first_row - n * k) % PAD
                    p[into, HX[level] + per * g + k, y : y + PAD, :] = (
                        pltpu.roll(tile, shift, 0) if shift else tile
                    )

    drains = []

    def exchange(refs, move):
        def copy(side, incoming=False):
            src, dst = refs(back(side) if incoming else side)
            return pltpu.make_async_remote_copy(
                src_ref=src,
                dst_ref=dst,
                send_sem=send_sem.at[move, SIDES.index(side)],
                recv_sem=recv_sem.at[move, SIDES.index(side if incoming else back(side))],
                device_id=peer(side),
                device_id_type=MESH,
            )

        def each(act):
            for side in SIDES:

                @pl.when(has(side))
                def _(side=side):
                    act(side)

        drains.append(lambda: each(lambda side: copy(side).wait_send()))
        return (
            lambda: each(lambda side: copy(side).start()),
            lambda: each(lambda side: copy(side, incoming=True).wait_recv()),
        )

    def level_exchange(level, e, into, move):
        pack_rows(level, e, into)
        start, arrive = exchange(level_refs(level, e, into), move)
        start()

        def finish():
            arrive()
            unpack_rows(level, into)

        return finish

    def lanes(values):
        return lax.broadcasted_iota(jnp.int32, values.shape, 1)

    def z_low(values, step):
        return jnp.where(lanes(values) < step, 0.0, pltpu.roll(values, step, 1))

    def z_high(values, step):
        return jnp.where(lanes(values) >= Z - step, 0.0, pltpu.roll(values, Z - step, 1))

    def keep_inner(level, i, at, zl, zh):
        step = 1 << level
        inner_zl[level][i, at, :] = jnp.where(lanes(zl) < step, 0.0, zl)
        inner_zh[level][i, at, :] = jnp.where(lanes(zh) >= Z - step, 0.0, zh)

    grid_u, grid_v, grid_w, grid_r = grids
    rows0 = Y0 + 2 * EDGE
    win0 = pl.ds(PAD - EDGE, rows0)

    def face(a, b):
        return 2.0 / jnp.maximum(a + b, 0.5)

    def faces(i, row=0, rows=rows0):
        at, start = pl.ds(row, rows), row + PAD - EDGE
        here = grid_r[i + 1, pl.ds(start, rows), :]
        face_x[0][i, at, :] = face(grid_r[i, pl.ds(start, rows), :], here)
        face_y[0][i, at, :] = face(grid_r[i + 1, pl.ds(start - 1, rows), :], here)
        if row + rows == rows0:
            last = PAD + EDGE + Y0
            face_y[0][i, rows0 : rows0 + EDGE, :] = face(
                grid_r[i + 1, last - 1 : last + EDGE - 1, :], grid_r[i + 1, last : last + EDGE, :]
            )
        zl, zh = face(z_low(here, 1), here), face(z_high(here, 1), here)
        face_zl[0][i, at, :] = zl
        face_zh[0][i, at, :] = zh
        keep_inner(0, i, at, zl, zh)

    def inside_rows(level, row, rows):
        Y = dims(level)[1]
        at = lax.broadcasted_iota(jnp.int32, (rows, Z), 0) + row
        return jnp.logical_and(
            jnp.logical_or(side_y[-1], at >= EDGE), jnp.logical_or(side_y[1], at < EDGE + Y)
        )

    def weigh(level, i, row=0, rows=None):
        X, Y = dims(level)
        h, rows = HALO[level], rows or Y + 2 * EDGE
        at = pl.ds(row, rows)
        total = face_x[level][i, at, :] + face_x[level][i + 1, at, :]
        total += face_y[level][i, at, :] + face_y[level][i, pl.ds(row + 1, rows), :]
        total += face_zl[level][i, at, :] + face_zh[level][i, at, :]
        inside = jnp.logical_and(
            jnp.logical_or(low[-1], i >= h), jnp.logical_or(low[1], i < h + X)
        )
        w = jnp.where(jnp.logical_and(inside_rows(level, row, rows), inside), DAMPING / total, 0.0)
        diag[level][i, at, :] = total
        weight[level][i, at, :] = w
        return w

    def first(j, row=0, rows=rows0):
        at, start = pl.ds(row, rows), row + PAD - EDGE
        mid = pl.ds(start, rows)
        w = weigh(0, j + HALO[0] - HX[0], row, rows)
        wz = grid_w[j + FIELD_HALO[2] - HX[0], mid, :]
        u_at, v_at = j + FIELD_HALO[0] - HX[0], j + FIELD_HALO[1] - HX[0]
        du = grid_u[u_at + 1, mid, :] - grid_u[u_at - 1, mid, :]
        dv = grid_v[v_at, pl.ds(start + 1, rows), :] - grid_v[v_at, pl.ds(start - 1, rows), :]
        b = -0.5 * ((du + dv) + (z_high(wz, 1) - z_low(wz, 1)))
        source[0][j, at, :] = b
        iterates[0][0, j, mid, :] = w * b

    def planes_of(act, low_j, high_j, edges_only=False, unroll=2):
        def one(j, carry):
            if edges_only:
                act(j, 0, PAD)
                act(j, rows0 - PAD, PAD)
            else:
                act(j)
            return carry

        lax.fori_loop(low_j, high_j, one, 0, unroll=unroll)

    n_faces, n_first = X0 + 2 * HALO[0], X0 + 2 * HX[0]
    face_from, face_to = HALO[0] + 1, HALO[0] + X0 - 1
    first_from, first_to = HX[0] + 1, HX[0] + X0 - 2
    field_start, field_arrive = exchange(field_refs, 0)
    field_start()
    push()
    planes_of(faces, face_from, face_to)
    planes_of(first, first_from, first_to)
    field_arrive()

    for n, (f, h, j) in enumerate(planes):
        for dx, x in ((-1, j), (1, h + X0 + j)):
            at = (dx + 1) // 2
            grids[f][x, PAD : PAD + Y0, :] = known((dx, 0), got_x[at, n])
    for end, dy in ((0, -1), (1, 1)):
        for i in range(X0):
            r, uvw = (known((0, dy), got_y[end, k * X0 + i]) for k in range(2))
            keep_rows(end, i, uvw, r)
        for j in range(CORNER):
            for side, dx, x in ((0, -1, j - CORNER), (1, 1, X0 + j)):
                r, uvw = (
                    known((dx, dy), got_c[2 * side + end, k * CORNER + j]) for k in range(2)
                )
                keep_rows(end, x, uvw, r)

    push()
    planes_of(faces, 0, face_from)
    planes_of(faces, face_to, n_faces)
    planes_of(faces, face_from, face_to, edges_only=True)
    face_x[0][n_faces] = face(grid_r[n_faces, win0, :], grid_r[n_faces + 1, win0, :])
    planes_of(first, 0, first_from, unroll=3)
    planes_of(first, first_to, n_first, unroll=4)
    planes_of(first, first_from, first_to, edges_only=True)

    def z_bit(values, level):
        return (lanes(values) // (1 << level)) % 2 == 1

    def z_pair(values, level):
        step = 1 << level
        return values + jnp.where(
            z_bit(values, level), pltpu.roll(values, step, 1), pltpu.roll(values, Z - step, 1)
        )

    def z_even(values, level):
        return jnp.where(z_bit(values, level), pltpu.roll(values, 1 << level, 1), values)

    def z_odd(values, level):
        return jnp.where(z_bit(values, level), values, pltpu.roll(values, Z - (1 << level), 1))

    def coarse_faces(level, base, start, count, more=0):
        even = pl.ds(start, count, stride=2)
        even_y = pl.ds(start, count + more, stride=2)
        odd = pl.ds(start + 1, count, stride=2)
        after = pl.ds(start + 2, count, stride=2)
        fx, fy, zl, zh = (f[level] for f in (face_x, face_y, face_zl, face_zh))

        def cx(x):
            i = base + 2 * x
            return 0.25 * z_pair(fx[i, even, :] + fx[i, odd, :], level)

        def cy(x, rows):
            i = base + 2 * x
            return 0.25 * z_pair(fy[i, rows, :] + fy[i + 1, rows, :], level)

        def four(f, x):
            i = base + 2 * x
            return 0.25 * (
                (f[i, even, :] + f[i, odd, :]) + (f[i + 1, even, :] + f[i + 1, odd, :])
            )

        return (
            cx,
            lambda x: cy(x, even_y),
            lambda x: cy(x, after),
            lambda x: z_even(four(zl, x), level),
            lambda x: z_odd(four(zh, x), level),
        )

    for level in range(LEVELS - 1):
        X, Y = dims(level + 1)
        count = Y + EDGE
        n_planes = X + 2 * HALO[level + 1]
        cx, cyl, _, czl, czh = coarse_faces(level, 0, 0, count, more=1)
        rows = pl.ds(EDGE // 2, count)

        def coarsen(i, carry, level=level, rows=rows, count=count, cx=cx, cyl=cyl, czl=czl, czh=czh):
            face_x[level + 1][i, rows, :] = cx(i)
            face_y[level + 1][i, pl.ds(EDGE // 2, count + 1), :] = cyl(i)
            zl, zh = czl(i), czh(i)
            face_zl[level + 1][i, rows, :] = zl
            face_zh[level + 1][i, rows, :] = zh
            step = 1 << (level + 1)
            inner_zl[level + 1][i, rows, :] = jnp.where(lanes(zl) < step, 0.0, zl)
            inner_zh[level + 1][i, rows, :] = jnp.where(lanes(zh) >= Z - step, 0.0, zh)
            return carry

        lax.fori_loop(0, n_planes, coarsen, 0, unroll=3)
        face_x[level + 1][n_planes, rows, :] = cx(n_planes)

        def weigh_plane(i, carry, level=level):
            weigh(level + 1, i)
            return carry

        lax.fori_loop(0, n_planes, weigh_plane, 0, unroll=3)

    X, Y = dims(LEVELS)
    cx, cyl, cyh, czl, czh = coarse_faces(LEVELS - 1, HALO[LEVELS - 1], EDGE, Y)
    for x in range(X + 1):
        gather_faces[narrow, x] = cx(x)
    for x in range(X):
        for k, part in enumerate((cyl, cyh, czl, czh)):
            gather_faces[narrow, X + 1 + k * X + x] = part(x)

    def gather(ref, which):
        def copy(d, incoming=False):
            came = lax.rem(narrow + n_narrow - d, n_narrow) if incoming else narrow
            return pltpu.make_async_remote_copy(
                src_ref=ref.at[narrow],
                dst_ref=ref.at[came],
                send_sem=gsend_sem.at[which, d - 1],
                recv_sem=grecv_sem.at[which, d - 1],
                device_id=others[d - 1],
                device_id_type=MESH,
            )

        def start():
            for d in range(1, n_narrow):
                copy(d).start()

        def finish():
            for d in range(1, n_narrow):
                copy(d, incoming=True).wait_recv()

        def drain():
            for d in range(1, n_narrow):
                copy(d).wait_send()

        return start, finish, drain

    face_start, face_finish, face_drain = gather(gather_faces, 0)
    source_start, source_finish, source_drain = gather(gather_source, 1)
    face_start()

    def neighbour_sum(level, e, x, own):
        Y = dims(level)[1]
        p = iterates[level]
        step = 1 << level
        edge = 0 if own else EDGE
        start, rows = PAD - edge, Y + 2 * edge
        at = pl.ds(EDGE - edge, rows)
        i, j = x + HALO[level], x + HX[level]
        here = p[e, j, pl.ds(start, rows), :]
        total = (
            face_x[level][i, at, :] * p[e, j - 1, pl.ds(start, rows), :]
            + face_x[level][i + 1, at, :] * p[e, j + 1, pl.ds(start, rows), :]
        )
        total += face_y[level][i, at, :] * p[e, j, pl.ds(start - 1, rows), :]
        total += face_y[level][i, pl.ds(EDGE - edge + 1, rows), :] * p[
            e, j, pl.ds(start + 1, rows), :
        ]
        total += inner_zl[level][i, at, :] * pltpu.roll(here, step, 1)
        total += inner_zh[level][i, at, :] * pltpu.roll(here, Z - step, 1)
        return here, total

    def sweep(level, e, x, own):
        Y = dims(level)[1]
        edge = 0 if own else EDGE
        here, total = neighbour_sum(level, e, x, own)
        w = weight[level][x + HALO[level], pl.ds(EDGE - edge, Y + 2 * edge), :]
        if e == 0:
            return (1.0 + KEEP) * here + w * total
        start = iterates[level][0, x + HX[level], pl.ds(PAD - edge, Y + 2 * edge), :]
        return (KEEP * here + start) + w * total

    def wide_sweep(level, e, halo):
        X, Y = dims(level)

        def plane(j, carry):
            x = j - halo
            iterates[level][e + 1, x + HX[level], pl.ds(PAD - EDGE, Y + 2 * EDGE), :] = sweep(
                level, e, x, False
            )
            return carry

        lax.fori_loop(0, X + 2 * halo, plane, 0, unroll=3 if X + 2 * halo == 18 else 2)

    finish_first = None
    for level in range(LEVELS):
        X, Y = dims(level)
        if level > 0:
            finish = level_exchange(level, 0, 0, level)
            push()
            finish()
        wide_sweep(level, 0, 1)
        if level == 0:
            finish_first = level_exchange(0, 1, 2, LEVELS)
        h, half, last = HALO[level], Y // 2, level + 1 == LEVELS
        own_rows = pl.ds(EDGE, Y)

        def restrict(x, carry, level=level, Y=Y, h=h, half=half, last=last, own_rows=own_rows):
            both = None
            for k in range(2):
                fine = 2 * x + k
                here, total = neighbour_sum(level, 1, fine, True)
                b = source[0][fine + HX[0], own_rows, :] if level == 0 else source[level][fine]
                left = (b - diag[level][fine + h, own_rows, :] * here) + total
                both = left if both is None else both + left
            tmp[:Y, :] = both
            summed = (
                tmp[pl.ds(0, half, stride=2), :] + tmp[pl.ds(1, half, stride=2), :]
            )
            summed = 0.5 * z_pair(summed, level)
            if last:
                gather_source[narrow, x] = summed
            else:
                source[level + 1][x] = summed
                w = weight[level + 1][x + HALO[level + 1], pl.ds(EDGE, half), :]
                iterates[level + 1][0, x + HX[level + 1], pl.ds(PAD, half), :] = w * summed
            return carry

        if last:
            for x in range(X // 2):
                restrict(x, 0)
        else:
            lax.fori_loop(0, X // 2, restrict, 0, unroll=4)

    source_start()
    push()
    face_finish()
    source_finish()
    X, Y = dims(LEVELS)
    step = 1 << LEVELS
    row = lax.broadcasted_iota(jnp.int32, (Y, Z), 0)
    col = lax.broadcasted_iota(jnp.int32, (Y, Z), 1)
    for n in range(n_narrow):
        for x in range(X):
            fxl, fxh = gather_faces[n, x], gather_faces[n, x + 1]
            fyl, fyh, fzl, fzh = (gather_faces[n, X + 1 + k * X + x] for k in range(4))
            total = ((fxl + fxh) + (fyl + fyh)) + (fzl + fzh)
            w = DAMPING / total
            at = n * X + x
            coef[0, at] = w * fxl
            coef[1, at] = w * fxh
            coef[2, at] = jnp.where(row == 0, 0.0, w * fyl)
            coef[3, at] = jnp.where(row == Y - 1, 0.0, w * fyh)
            coef[4, at] = jnp.where(col < step, 0.0, w * fzl)
            coef[5, at] = jnp.where(col >= Z - step, 0.0, w * fzh)
            coef[6, at] = w * gather_source[n, x]

    zero_plane = jnp.zeros((1, Y, Z), jnp.float32)

    def bottom(k, cur):
        new = KEEP * cur + coef[6]
        new += coef[0] * jnp.concatenate([zero_plane, cur[:-1]], axis=0)
        new += coef[1] * jnp.concatenate([cur[1:], zero_plane], axis=0)
        new += coef[2] * pltpu.roll(cur, 1, 1)
        new += coef[3] * pltpu.roll(cur, Y - 1, 1)
        new += coef[4] * pltpu.roll(cur, step, 2)
        new += coef[5] * pltpu.roll(cur, Z - step, 2)
        return new

    push()
    coef[7] = lax.fori_loop(0, BOTTOM - 1, bottom, coef[6], unroll=15)
    for x in range(X):
        answer[LEVELS][x] = coef[7, narrow * X + x]

    def repeat_rows(e, count):
        tmp[pl.ds(0, count, stride=2), :] = e
        tmp[pl.ds(1, count, stride=2), :] = e
        return tmp[: 2 * count, :]

    for level in reversed(range(1, LEVELS)):
        X, Y = dims(level)
        half = Y // 2

        def raised(x, carry, level=level, Y=Y, half=half):
            e = repeat_rows(answer[level + 1][x // 2], half)
            at = x + HX[level]
            iterates[level][2, at, PAD : PAD + Y, :] = (
                iterates[level][1, at, PAD : PAD + Y, :] + e
            )
            return carry

        lax.fori_loop(0, X, raised, 0, unroll=4)
        finish = level_exchange(level, 2, 2, LEVELS + level)
        push()
        finish()
        out_halo = 1 if level == 1 else 0
        wide_sweep(level, 2, 1 + out_halo)

        def close(j, carry, level=level, out_halo=out_halo):
            if out_halo:
                near_answer[j, pl.ds(PAD - EDGE, dims(level)[1] + 2 * EDGE), :] = sweep(
                    level, 3, j - out_halo, False
                )
            else:
                answer[level][j] = sweep(level, 3, j, True)
            return carry

        lax.fori_loop(0, X + 2 * out_halo, close, 0, unroll=2)

    for x in range(X0):
        iterates[0][2, x + HX[0], PAD : PAD + Y0, :] = iterates[0][1, x + HX[0], PAD : PAD + Y0, :]
    finish_first()
    coarse_rows = pl.ds(PAD - EDGE // 2, Y0 // 2 + EDGE)

    def raise_first(j, carry):
        e = repeat_rows(near_answer[j // 2, coarse_rows, :], Y0 // 2 + EDGE)
        iterates[0][2, j, win0, :] = iterates[0][2, j, win0, :] + e
        return carry

    lax.fori_loop(0, X0 + 2 * HX[0], raise_first, 0, unroll=4)
    wide_sweep(0, 2, 1)

    def close_first(x, carry):
        pressure[x] = sweep(0, 3, x, True)
        return carry

    lax.fori_loop(0, X0, close_first, 0, unroll=4)

    assert len(pushed) == len(SHARES) + 1
    pressure_copy = pltpu.make_async_copy(pressure, pressure_ref, local_sem.at[4])
    pressure_copy.start()

    def merge_solved(q, carry):
        merged[q, :SOLVED] = arrived[receive_index[q, 0]]
        return carry

    lax.fori_loop(0, PER_OWNER, merge_solved, 0, unroll=4)

    def carried_arrive(k, carry):
        carried_bulk(k, incoming=True).wait_recv()
        return carry

    lax.fori_loop(1, owners, carried_arrive, 0)

    def out_copy(g):
        group = pl.ds(g * OUT_GROUP, OUT_GROUP)
        return pltpu.make_async_copy(merged.at[group], migrated_ref.at[group], out_sem.at[g])

    for g in range(PER_OWNER // OUT_GROUP):

        def merge_carried(q, carry):
            merged[q, SOLVED:] = moved[receive_index[q, 0]]
            return carry

        lax.fori_loop(g * OUT_GROUP, (g + 1) * OUT_GROUP, merge_carried, 0, unroll=4)
        out_copy(g).start()

    def end(k, carry):
        carried_bulk(k).wait_send()
        solved_bulk(k).wait_send()
        return carry

    lax.fori_loop(1, owners, end, 0)
    face_drain()
    source_drain()
    for drain in drains:
        drain()
    pressure_copy.wait()
    for g in range(PER_OWNER // OUT_GROUP):
        out_copy(g).wait()


def f32(*shape):
    return pltpu.VMEM(shape, jnp.float32)


def bf16(*shape):
    return pltpu.VMEM(shape, jnp.bfloat16)


def call_solve(n_wide, n_narrow, table, fields):
    per_owner, n_fields, cells = fields.shape
    owners = n_wide * n_narrow
    slots = owners * CAPACITY
    X3, Y3 = dims(LEVELS)
    levels = [(level, *dims(level)) for level in range(LEVELS)]
    faces = [f32(X + 2 * HALO[l], Y + 2 * EDGE, Z) for l, X, Y in levels]
    moves = 2 * LEVELS
    packs = {
        "solved": bf16(slots, SOLVED, cells),
        "carried": bf16(slots, n_fields - SOLVED, cells),
    }
    dma = pltpu.SemaphoreType.DMA
    scratch = [
        pltpu.VMEM(table.shape, jnp.int32),
        bf16(*fields.shape),
        packs["solved"],
        packs["carried"],
        packs["solved"],
        packs["carried"],
        bf16(*fields.shape),
        f32(X0, Y0, Z),
        pltpu.VMEM((CAPACITY, owners, Z), jnp.int32),
        pltpu.VMEM((per_owner, Z), jnp.int32),
        pltpu.SMEM((CAPACITY, owners, Z), jnp.int32),
        pltpu.SMEM((per_owner, Z), jnp.int32),
        f32(64, Z),
        f32(Y0 + 2 * PAD, Z),
        [f32(X0 + 2 * h, Y0 + 2 * PAD, Z) for h in FIELD_HALO],
        bf16(2, HALO_PLANES, Y0, Z),
        bf16(2, HALO_PLANES, Y0, Z),
        bf16(2, 2 * X0, PAD, Z),
        bf16(2, 2 * X0, PAD, Z),
        bf16(4, 2 * CORNER, PAD, Z),
        bf16(4, 2 * CORNER, PAD, Z),
        [f32(4, X + 2 * HX[l], Y + 2 * PAD, Z) for l, X, Y in levels],
        [f32(2, 2, X * ROWS[l] // PAD, PAD, Z) for l, X, Y in levels],
        [f32(2, 2, X * ROWS[l] // PAD, PAD, Z) for l, X, Y in levels],
        [f32(X + 2 * HALO[l] + 1, Y + 2 * EDGE, Z) for l, X, Y in levels],
        [f32(X + 2 * HALO[l], Y + 2 * EDGE + 8, Z) for l, X, Y in levels],
        faces,
        faces,
        faces,
        faces,
        faces,
        faces,
        [f32(X0 + 2 * HX[0], Y0 + 2 * EDGE, Z)] + [f32(X, Y, Z) for l, X, Y in levels[1:]],
        [f32(*dims(level), Z) for level in range(LEVELS + 1)],
        f32(dims(1)[0] + 2, dims(1)[1] + 2 * PAD, Z),
        f32(n_narrow, 5 * X3 + 1, Y3, Z),
        f32(n_narrow, X3, Y3, Z),
        f32(8, n_narrow * X3, Y3, Z),
        dma((moves, 8)),
        dma((moves, 8)),
        dma((2, n_narrow - 1)),
        dma((2, n_narrow - 1)),
        dma((owners,)),
        dma((owners,)),
        dma((owners,)),
        dma((owners,)),
        dma((5,)),
        dma((per_owner // OUT_GROUP,)),
    ]
    anywhere = pl.BlockSpec(memory_space=pl.ANY)
    return pl.pallas_call(
        functools.partial(solve_kernel, n_wide, n_narrow),
        out_shape=(
            jax.ShapeDtypeStruct(fields.shape, fields.dtype),
            jax.ShapeDtypeStruct((X0, Y0, Z), jnp.float32),
        ),
        in_specs=[anywhere, anywhere],
        out_specs=(anywhere, anywhere),
        scratch_shapes=scratch,
        compiler_params=pltpu.CompilerParams(
            collective_id=0, has_side_effects=True, vmem_limit_bytes=min(60, 46 + owners // 8) * 1024 * 1024
        ),
        cost_estimate=pl.CostEstimate(
            flops=200_000_000, bytes_accessed=200_000_000, transcendentals=0
        ),
    )(table, fields)


def hand_over_kernel(migrated_ref, pressure_ref, migrated_out, pressure_out, sem):
    copies = []
    for n, (src, dst) in enumerate(((migrated_ref, migrated_out), (pressure_ref, pressure_out))):
        size = src.shape[0] // PIECES
        for g in range(PIECES):
            piece = pl.ds(g * size, size)
            copies.append(pltpu.make_async_copy(src.at[piece], dst.at[piece], sem.at[n, g]))
    for copy in copies:
        copy.start()
    for copy in copies:
        copy.wait()


def hand_over(migrated, pressure):
    anywhere = pl.BlockSpec(memory_space=pl.ANY)
    return pl.pallas_call(
        hand_over_kernel,
        out_shape=tuple(jax.ShapeDtypeStruct(a.shape, a.dtype) for a in (migrated, pressure)),
        in_specs=[anywhere, anywhere],
        out_specs=(anywhere, anywhere),
        scratch_shapes=[pltpu.SemaphoreType.DMA((2, PIECES))],
        compiler_params=pltpu.CompilerParams(vmem_limit_bytes=1024 * 1024),
    )(migrated, pressure)


def shards(n_wide, n_narrow, target_slot, fields):
    return hand_over(*call_solve(n_wide, n_narrow, target_slot.reshape(-1, Z), fields))


def solution(mesh):
    body = functools.partial(shards, mesh.shape["wide"], mesh.shape["narrow"])
    in_specs = (P(), P(("wide", "narrow"), None, None))
    out_specs = (P(("wide", "narrow"), None, None), P("narrow", "wide", None))
    return jax.shard_map(body, mesh=mesh, in_specs=in_specs, out_specs=out_specs, check_vma=False)
```

```python
import functools

import jax
import jax.numpy as jnp
from jax import lax
from jax.experimental import pallas as pl
from jax.experimental.pallas import tpu as pltpu
from jax.sharding import PartitionSpec as P

PATCH = 16
BYP = 4
BZP = 8
LEVELS = 3
BOTTOM = 16
DAMPING = 0.8
KEEP = 1.0 - DAMPING
SOLVED = 4
CAPACITY = 2
PER_OWNER = 32
X0 = PATCH
Y0 = PATCH * BYP
Z = PATCH * BZP
PAD = 8
EDGE = 4
HX = (2, 3, 2)
ROWS = (2, 4, 2)
CORNER_PLANES = (1, 3, 1)
HALO = (4, 2, 1)
FIELD_HALO = (3, 2, 2, 5)
HALO_PLANES = sum(FIELD_HALO)
CORNER = max(FIELD_HALO)
MESH = pl.DeviceIdType.MESH
FAR = (4, 0, 1, 2, 1, 1, 1, 1, 1, 4)
NEAR = (10, 0, 0, 0, 1, 1, 1, 1, 1, 0)
OUT_GROUP = 8
PIECES = 8
SIDES = tuple((dx, dy) for dx in (-1, 0, 1) for dy in (-1, 0, 1) if dx or dy)


def dims(level):
    return X0 >> level, Y0 >> level


def solve_kernel(
    n_wide,
    n_narrow,
    target_ref,
    fields_ref,
    migrated_ref,
    pressure_ref,
    target,
    fields,
    solved,
    carried,
    arrived,
    moved,
    merged,
    pressure,
    send_index_v,
    receive_index_v,
    send_index,
    receive_index,
    turn,
    tmp,
    grids,
    sent_x,
    got_x,
    sent_y,
    got_y,
    sent_c,
    got_c,
    iterates,
    sent_rows,
    got_rows,
    face_x,
    face_y,
    face_zl,
    face_zh,
    inner_zl,
    inner_zh,
    diag,
    weight,
    source,
    answer,
    near_answer,
    gather_faces,
    gather_source,
    coef,
    send_sem,
    recv_sem,
    gsend_sem,
    grecv_sem,
    carry_send_sem,
    carry_recv_sem,
    solved_send_sem,
    solved_recv_sem,
    local_sem,
    out_sem,
):
    wide = lax.axis_index("wide")
    narrow = lax.axis_index("narrow")
    owners = n_wide * n_narrow
    me = wide * n_narrow + narrow
    low = {-1: narrow > 0, 1: narrow < n_narrow - 1, 0: None}
    side_y = {-1: wide > 0, 1: wide < n_wide - 1, 0: None}

    def has(side):
        dx, dy = side
        if dx == 0:
            return side_y[dy]
        if dy == 0:
            return low[dx]
        return jnp.logical_and(low[dx], side_y[dy])

    def peer(side):
        return (wide + side[1], narrow + side[0])

    def back(side):
        return (-side[0], -side[1])

    others = [(wide, lax.rem(narrow + d, n_narrow)) for d in range(1, n_narrow)]

    target_copy = pltpu.make_async_copy(target_ref, target, local_sem.at[0])
    target_copy.start()
    fields_copy = pltpu.make_async_copy(fields_ref, fields, local_sem.at[1])
    fields_copy.start()

    def at_distance(distance):
        owner = jnp.bitwise_xor(me, distance)
        return owner, (owner // n_narrow, lax.rem(owner, n_narrow))

    def partner(k):
        return at_distance(jnp.where(lax.rem(k, 2) == 1, owners // 2 + k // 2, k // 2))

    barrier = pltpu.get_barrier_semaphore()

    def greet(k, carry):
        _, device = partner(k)
        pl.semaphore_signal(barrier, inc=1, device_id=device, device_id_type=MESH)
        return carry

    lax.fori_loop(1, owners, greet, 0)

    target_copy.wait()
    segments = Z // PER_OWNER
    own_row = target[pl.ds(me // segments, 1), :]
    lane_d = lax.broadcasted_iota(jnp.int32, (owners, Z), 1)
    owner_d = lax.broadcasted_iota(jnp.int32, (owners, Z), 0)
    mine = jnp.logical_and(
        lane_d // PER_OWNER == lax.rem(me, segments), own_row // PER_OWNER == owner_d
    )
    place = lax.rem(lane_d, PER_OWNER)
    low_place = jnp.min(jnp.where(mine, place, PER_OWNER - 1), axis=1, keepdims=True)
    high_place = jnp.max(jnp.where(mine, place, 0), axis=1, keepdims=True)
    send_index_v[0] = jnp.broadcast_to(low_place, (owners, Z))
    send_index_v[1] = jnp.broadcast_to(high_place, (owners, Z))
    index_copy = pltpu.make_async_copy(send_index_v, send_index, local_sem.at[2])
    index_copy.start()

    table = target[...]
    t_rows = table.shape[0]
    t_lane = lax.broadcasted_iota(jnp.int32, (t_rows, Z), 1)
    t_owner = lax.broadcasted_iota(jnp.int32, (t_rows, Z), 0) * segments + t_lane // PER_OWNER
    t_place = lax.rem(t_lane, PER_OWNER)
    seen = jnp.where(table // PER_OWNER == me, 1, 0)
    step = 1
    while step < PER_OWNER:
        seen = jnp.maximum(seen, jnp.where(t_place >= step, pltpu.roll(seen, step, 1), 0))
        step *= 2
    rank = jnp.where(t_place >= 1, pltpu.roll(seen, 1, 1), 0)
    slot = t_owner * CAPACITY + rank
    for q in range(PER_OWNER):
        hit = jnp.where(table == me * PER_OWNER + q, slot, 0)
        receive_index_v[q : q + 1, :] = jnp.max(hit, axis=0, keepdims=True)
    slots_q = jnp.max(receive_index_v[...], axis=1, keepdims=True)
    receive_index_v[...] = jnp.broadcast_to(slots_q, (PER_OWNER, Z))
    receive_copy = pltpu.make_async_copy(receive_index_v, receive_index, local_sem.at[3])
    receive_copy.start()

    index_copy.wait()
    fields_copy.wait()
    pl.semaphore_wait(barrier, owners - 1)

    def block(owner):
        return pl.ds(owner * CAPACITY, CAPACITY)

    def bulk(whom, packed, landed, send, recv, k, incoming=False):
        owner, device = whom(k)
        return pltpu.make_async_remote_copy(
            src_ref=packed.at[block(me if incoming else owner)],
            dst_ref=landed.at[block(owner if incoming else me)],
            send_sem=send.at[k],
            recv_sem=recv.at[k],
            device_id=device,
            device_id_type=MESH,
        )

    solved_bulk = functools.partial(bulk, partner, solved, arrived, solved_send_sem, solved_recv_sem)
    carried_bulk = functools.partial(bulk, at_distance, carried, moved, carry_send_sem, carry_recv_sem)

    def pack_solved(k, carry):
        owner, _ = partner(k)
        for r in range(CAPACITY):
            solved[owner * CAPACITY + r] = fields[send_index[r, owner, 0], :SOLVED]
        solved_bulk(k).start()
        return carry

    def pack_carried(k, carry):
        owner, _ = at_distance(k)
        for r in range(CAPACITY):
            carried[owner * CAPACITY + r] = fields[send_index[r, owner, 0], SOLVED:]
        return carry

    lax.fori_loop(1, owners, pack_solved, 0)
    for r in range(CAPACITY):
        patch = fields[send_index[r, me, 0]]
        arrived[me * CAPACITY + r] = patch[:SOLVED]
        moved[me * CAPACITY + r] = patch[SOLVED:]
    lax.fori_loop(1, owners, pack_carried, 0)

    half_way = owners // 2

    def cuts(shares, first, end):
        return [first + (end - first) * sum(shares[:k]) // sum(shares) for k in range(len(shares) + 1)]

    far = cuts(FAR, half_way, owners)
    near = cuts(NEAR, 1, half_way)
    pushed = []

    def begin(k, carry):
        carried_bulk(k).start()
        return carry

    def push():
        turn_now = len(pushed)
        pushed.append(turn_now)
        for bounds in (far, near):
            if bounds[turn_now] < bounds[turn_now + 1]:
                lax.fori_loop(bounds[turn_now], bounds[turn_now + 1], begin, 0)

    push()
    for level in range(LEVELS):
        X, Y = dims(level)
        p = iterates[level]
        hx = HX[level]
        for e in (2,) if level == 0 else (0, 2):

            @pl.when(jnp.logical_not(low[-1]))
            def _(p=p, e=e, Y=Y, hx=hx):
                p[e, :hx] = jnp.zeros((hx, Y + 2 * PAD, Z), jnp.float32)

            @pl.when(jnp.logical_not(low[1]))
            def _(p=p, e=e, X=X, Y=Y, hx=hx):
                p[e, hx + X :] = jnp.zeros((hx, Y + 2 * PAD, Z), jnp.float32)

            @pl.when(jnp.logical_not(side_y[-1]))
            def _(p=p, e=e, X=X, Y=Y, hx=hx):
                p[e, :, :PAD] = jnp.zeros((X + 2 * hx, PAD, Z), jnp.float32)

            @pl.when(jnp.logical_not(side_y[1]))
            def _(p=p, e=e, X=X, Y=Y, hx=hx):
                p[e, :, PAD + Y :] = jnp.zeros((X + 2 * hx, PAD, Z), jnp.float32)

    receive_copy.wait()

    def solved_arrive(k, carry):
        solved_bulk(k, incoming=True).wait_recv()
        return carry

    lax.fori_loop(1, owners, solved_arrive, 0)
    push()

    lane = lax.broadcasted_iota(jnp.int32, (8, Z), 1)
    block_lane = lane // PATCH
    lower_bits = [(block_lane // s) % 2 == 1 for s in (1, 2, 4)]

    def to_grid(step, carry):
        b = step // X0
        i = step % X0
        at = pl.multiple_of(i * 2 * Z, 2 * Z)
        rows = []
        for c in range(BZP):
            both = arrived[receive_index[b * BZP + c, 0], :, pl.ds(at, 2 * Z)].astype(
                jnp.float32
            )
            rows.append(jnp.concatenate([both[:, :Z], both[:, Z:]], axis=0))
        for bit, s in zip(lower_bits, (1, 2, 4)):
            new = list(rows)
            for c in range(BZP):
                if c & s == 0:
                    lower, upper = rows[c], rows[c + s]
                    new[c] = jnp.where(bit, pltpu.roll(upper, PATCH * s, 1), lower)
                    new[c + s] = jnp.where(bit, upper, pltpu.roll(lower, Z - PATCH * s, 1))
            rows = new
        for j in range(8):
            turn[8 * j : 8 * j + 8, :] = rows[j]
        for half in range(2):
            y = pl.multiple_of(b * PATCH + half * 8, 8)
            for f, ref in enumerate(grids):
                values = turn[pl.ds(half * SOLVED + f, 8, stride=8), :]
                ref[i + FIELD_HALO[f], pl.ds(PAD + y, 8), :] = values
        return carry

    lax.fori_loop(0, BYP * X0, to_grid, 0, unroll=8)

    def known(side, values):
        return jnp.where(has(side), values.astype(jnp.float32), 0.0)

    planes = []
    for f, h in enumerate(FIELD_HALO):
        planes += [(f, h, j) for j in range(h)]
    for n, (f, h, j) in enumerate(planes):
        for side, x in ((0, j), (1, X0 - h + j)):
            sent_x[side, n] = grids[f][h + x, PAD : PAD + Y0, :].astype(jnp.bfloat16)
    at_row = lax.broadcasted_iota(jnp.int32, (PAD, Z), 0)

    def end_rows(end, x):
        y = (0, Y0 - PAD)[end]
        u, v, w, r = (
            grids[f][h + x, PAD + y : PAD + y + PAD, :] for f, h in enumerate(FIELD_HALO)
        )
        if end == 0:
            uvw = jnp.where(
                at_row < 2, u, jnp.where(at_row < 5, pltpu.roll(v, 2, 0), pltpu.roll(w, 5, 0))
            )
        else:
            uvw = jnp.where(
                at_row > 5, u, jnp.where(at_row > 2, pltpu.roll(v, 6, 0), pltpu.roll(w, 3, 0))
            )
        return r.astype(jnp.bfloat16), uvw.astype(jnp.bfloat16)

    def keep_rows(end, x, uvw, r):
        y = (0, PAD + Y0)[end]
        u, v, w = (
            (uvw, pltpu.roll(uvw, 2, 0), pltpu.roll(uvw, 5, 0)),
            (uvw, pltpu.roll(uvw, 6, 0), pltpu.roll(uvw, 3, 0)),
        )[end]
        for f, values in enumerate((u, v, w, r)):
            h = FIELD_HALO[f]
            if -h <= x < X0 + h:
                grids[f][h + x, y : y + PAD, :] = values

    for end in range(2):
        for i in range(X0):
            sent_y[end, i], sent_y[end, X0 + i] = end_rows(end, i)
        for j in range(CORNER):
            for side, x in ((0, j), (1, X0 - CORNER + j)):
                (
                    sent_c[2 * side + end, j],
                    sent_c[2 * side + end, CORNER + j],
                ) = end_rows(end, x)

    def field_refs(side):
        dx, dy = side
        if dy == 0:
            return sent_x.at[(dx + 1) // 2], got_x.at[(1 - dx) // 2]
        if dx == 0:
            return sent_y.at[(dy + 1) // 2], got_y.at[(1 - dy) // 2]
        return sent_c.at[dx + 1 + (dy + 1) // 2], got_c.at[1 - dx + (1 - dy) // 2]

    def level_refs(level, e, into):
        X, Y = dims(level)
        p = iterates[level]
        hx = HX[level]

        def refs(side):
            dx, dy = side
            if dx == 0:
                which = into // 2
                return (
                    sent_rows[level].at[which, (dy + 1) // 2],
                    got_rows[level].at[which, (1 - dy) // 2],
                )
            h = hx if dy == 0 else CORNER_PLANES[level]
            src_x, dst_x, n_x = {
                -1: (hx, hx + X, h),
                0: (hx, hx, X),
                1: (hx + X - h, hx - h, h),
            }[dx]
            src_y, dst_y, n_y = {
                -1: (PAD, PAD + Y, PAD),
                0: (PAD, PAD, Y),
                1: (Y, 0, PAD),
            }[dy]
            return (
                p.at[e, pl.ds(src_x, n_x), pl.ds(src_y, n_y)],
                p.at[into, pl.ds(dst_x, n_x), pl.ds(dst_y, n_y)],
            )

        return refs

    def pack_rows(level, e, into):
        X, Y = dims(level)
        p, n = iterates[level], ROWS[level]
        per = PAD // n
        for end, y, first_row in ((0, PAD, 0), (1, Y, PAD - n)):
            for g in range(X // per):
                tile = None
                for k in range(per):
                    rows = p[e, HX[level] + per * g + k, y : y + PAD, :]
                    shift = (n * k - first_row) % PAD
                    rows = pltpu.roll(rows, shift, 0) if shift else rows
                    tile = rows if tile is None else jnp.where(at_row >= n * k, rows, tile)
                sent_rows[level][into // 2, end, g] = tile

    def unpack_rows(level, into):
        X, Y = dims(level)
        p, n = iterates[level], ROWS[level]
        per = PAD // n
        for end, y, first_row in ((0, 0, PAD - n), (1, PAD + Y, 0)):
            for g in range(X // per):
                tile = known((0, 2 * end - 1), got_rows[level][into // 2, end, g])
                for k in range(per):
                    shift = (first_row - n * k) % PAD
                    p[into, HX[level] + per * g + k, y : y + PAD, :] = (
                        pltpu.roll(tile, shift, 0) if shift else tile
                    )

    drains = []

    def exchange(refs, move):
        def copy(side, incoming=False):
            src, dst = refs(back(side) if incoming else side)
            return pltpu.make_async_remote_copy(
                src_ref=src,
                dst_ref=dst,
                send_sem=send_sem.at[move, SIDES.index(side)],
                recv_sem=recv_sem.at[move, SIDES.index(side if incoming else back(side))],
                device_id=peer(side),
                device_id_type=MESH,
            )

        def each(act):
            for side in SIDES:

                @pl.when(has(side))
                def _(side=side):
                    act(side)

        drains.append(lambda: each(lambda side: copy(side).wait_send()))
        return (
            lambda: each(lambda side: copy(side).start()),
            lambda: each(lambda side: copy(side, incoming=True).wait_recv()),
        )

    def level_exchange(level, e, into, move):
        pack_rows(level, e, into)
        start, arrive = exchange(level_refs(level, e, into), move)
        start()

        def finish():
            arrive()
            unpack_rows(level, into)

        return finish

    def lanes(values):
        return lax.broadcasted_iota(jnp.int32, values.shape, 1)

    def z_low(values, step):
        return jnp.where(lanes(values) < step, 0.0, pltpu.roll(values, step, 1))

    def z_high(values, step):
        return jnp.where(lanes(values) >= Z - step, 0.0, pltpu.roll(values, Z - step, 1))

    def keep_inner(level, i, at, zl, zh):
        step = 1 << level
        inner_zl[level][i, at, :] = jnp.where(lanes(zl) < step, 0.0, zl)
        inner_zh[level][i, at, :] = jnp.where(lanes(zh) >= Z - step, 0.0, zh)

    grid_u, grid_v, grid_w, grid_r = grids
    rows0 = Y0 + 2 * EDGE
    win0 = pl.ds(PAD - EDGE, rows0)

    def face(a, b):
        return 2.0 / jnp.maximum(a + b, 0.5)

    def faces(i, row=0, rows=rows0):
        at, start = pl.ds(row, rows), row + PAD - EDGE
        here = grid_r[i + 1, pl.ds(start, rows), :]
        face_x[0][i, at, :] = face(grid_r[i, pl.ds(start, rows), :], here)
        face_y[0][i, at, :] = face(grid_r[i + 1, pl.ds(start - 1, rows), :], here)
        if row + rows == rows0:
            last = PAD + EDGE + Y0
            face_y[0][i, rows0 : rows0 + EDGE, :] = face(
                grid_r[i + 1, last - 1 : last + EDGE - 1, :], grid_r[i + 1, last : last + EDGE, :]
            )
        zl, zh = face(z_low(here, 1), here), face(z_high(here, 1), here)
        face_zl[0][i, at, :] = zl
        face_zh[0][i, at, :] = zh
        keep_inner(0, i, at, zl, zh)

    def inside_rows(level, row, rows):
        Y = dims(level)[1]
        at = lax.broadcasted_iota(jnp.int32, (rows, Z), 0) + row
        return jnp.logical_and(
            jnp.logical_or(side_y[-1], at >= EDGE), jnp.logical_or(side_y[1], at < EDGE + Y)
        )

    def weigh(level, i, row=0, rows=None):
        X, Y = dims(level)
        h, rows = HALO[level], rows or Y + 2 * EDGE
        at = pl.ds(row, rows)
        total = face_x[level][i, at, :] + face_x[level][i + 1, at, :]
        total += face_y[level][i, at, :] + face_y[level][i, pl.ds(row + 1, rows), :]
        total += face_zl[level][i, at, :] + face_zh[level][i, at, :]
        inside = jnp.logical_and(
            jnp.logical_or(low[-1], i >= h), jnp.logical_or(low[1], i < h + X)
        )
        w = jnp.where(jnp.logical_and(inside_rows(level, row, rows), inside), DAMPING / total, 0.0)
        diag[level][i, at, :] = total
        weight[level][i, at, :] = w
        return w

    def first(j, row=0, rows=rows0):
        at, start = pl.ds(row, rows), row + PAD - EDGE
        mid = pl.ds(start, rows)
        w = weigh(0, j + HALO[0] - HX[0], row, rows)
        wz = grid_w[j + FIELD_HALO[2] - HX[0], mid, :]
        u_at, v_at = j + FIELD_HALO[0] - HX[0], j + FIELD_HALO[1] - HX[0]
        du = grid_u[u_at + 1, mid, :] - grid_u[u_at - 1, mid, :]
        dv = grid_v[v_at, pl.ds(start + 1, rows), :] - grid_v[v_at, pl.ds(start - 1, rows), :]
        b = -0.5 * ((du + dv) + (z_high(wz, 1) - z_low(wz, 1)))
        source[0][j, at, :] = b
        iterates[0][0, j, mid, :] = w * b

    def planes_of(act, low_j, high_j, edges_only=False, unroll=2):
        def one(j, carry):
            if edges_only:
                act(j, 0, PAD)
                act(j, rows0 - PAD, PAD)
            else:
                act(j)
            return carry

        lax.fori_loop(low_j, high_j, one, 0, unroll=unroll)

    n_faces, n_first = X0 + 2 * HALO[0], X0 + 2 * HX[0]
    face_from, face_to = HALO[0] + 1, HALO[0] + X0 - 1
    first_from, first_to = HX[0] + 1, HX[0] + X0 - 2
    field_start, field_arrive = exchange(field_refs, 0)
    field_start()
    push()

    def solved_end(k, carry):
        solved_bulk(k).wait_send()
        return carry

    lax.fori_loop(1, owners, solved_end, 0, unroll=False)
    planes_of(faces, face_from, face_to)
    planes_of(first, first_from, first_to)
    field_arrive()

    for n, (f, h, j) in enumerate(planes):
        for dx, x in ((-1, j), (1, h + X0 + j)):
            at = (dx + 1) // 2
            grids[f][x, PAD : PAD + Y0, :] = known((dx, 0), got_x[at, n])
    for end, dy in ((0, -1), (1, 1)):
        for i in range(X0):
            r, uvw = (known((0, dy), got_y[end, k * X0 + i]) for k in range(2))
            keep_rows(end, i, uvw, r)
        for j in range(CORNER):
            for side, dx, x in ((0, -1, j - CORNER), (1, 1, X0 + j)):
                r, uvw = (
                    known((dx, dy), got_c[2 * side + end, k * CORNER + j]) for k in range(2)
                )
                keep_rows(end, x, uvw, r)

    push()
    planes_of(faces, 0, face_from)
    planes_of(faces, face_to, n_faces)
    planes_of(faces, face_from, face_to, edges_only=True)
    face_x[0][n_faces] = face(grid_r[n_faces, win0, :], grid_r[n_faces + 1, win0, :])
    planes_of(first, 0, first_from, unroll=3)
    planes_of(first, first_to, n_first, unroll=4)
    planes_of(first, first_from, first_to, edges_only=True)

    def z_bit(values, level):
        return (lanes(values) // (1 << level)) % 2 == 1

    def z_pair(values, level):
        step = 1 << level
        return values + jnp.where(
            z_bit(values, level), pltpu.roll(values, step, 1), pltpu.roll(values, Z - step, 1)
        )

    def z_even(values, level):
        return jnp.where(z_bit(values, level), pltpu.roll(values, 1 << level, 1), values)

    def z_odd(values, level):
        return jnp.where(z_bit(values, level), values, pltpu.roll(values, Z - (1 << level), 1))

    def coarse_faces(level, base, start, count, more=0):
        even = pl.ds(start, count, stride=2)
        even_y = pl.ds(start, count + more, stride=2)
        odd = pl.ds(start + 1, count, stride=2)
        after = pl.ds(start + 2, count, stride=2)
        fx, fy, zl, zh = (f[level] for f in (face_x, face_y, face_zl, face_zh))

        def cx(x):
            i = base + 2 * x
            return 0.25 * z_pair(fx[i, even, :] + fx[i, odd, :], level)

        def cy(x, rows):
            i = base + 2 * x
            return 0.25 * z_pair(fy[i, rows, :] + fy[i + 1, rows, :], level)

        def four(f, x):
            i = base + 2 * x
            return 0.25 * (
                (f[i, even, :] + f[i, odd, :]) + (f[i + 1, even, :] + f[i + 1, odd, :])
            )

        return (
            cx,
            lambda x: cy(x, even_y),
            lambda x: cy(x, after),
            lambda x: z_even(four(zl, x), level),
            lambda x: z_odd(four(zh, x), level),
        )

    for level in range(LEVELS - 1):
        X, Y = dims(level + 1)
        count = Y + EDGE
        n_planes = X + 2 * HALO[level + 1]
        cx, cyl, _, czl, czh = coarse_faces(level, 0, 0, count, more=1)
        rows = pl.ds(EDGE // 2, count)

        def coarsen(i, carry, level=level, rows=rows, count=count, cx=cx, cyl=cyl, czl=czl, czh=czh):
            face_x[level + 1][i, rows, :] = cx(i)
            face_y[level + 1][i, pl.ds(EDGE // 2, count + 1), :] = cyl(i)
            zl, zh = czl(i), czh(i)
            face_zl[level + 1][i, rows, :] = zl
            face_zh[level + 1][i, rows, :] = zh
            step = 1 << (level + 1)
            inner_zl[level + 1][i, rows, :] = jnp.where(lanes(zl) < step, 0.0, zl)
            inner_zh[level + 1][i, rows, :] = jnp.where(lanes(zh) >= Z - step, 0.0, zh)
            return carry

        lax.fori_loop(0, n_planes, coarsen, 0, unroll=3)
        face_x[level + 1][n_planes, rows, :] = cx(n_planes)

        def weigh_plane(i, carry, level=level):
            weigh(level + 1, i)
            return carry

        lax.fori_loop(0, n_planes, weigh_plane, 0, unroll=3)

    X, Y = dims(LEVELS)
    cx, cyl, cyh, czl, czh = coarse_faces(LEVELS - 1, HALO[LEVELS - 1], EDGE, Y)
    for x in range(X + 1):
        gather_faces[narrow, x] = cx(x)
    for x in range(X):
        for k, part in enumerate((cyl, cyh, czl, czh)):
            gather_faces[narrow, X + 1 + k * X + x] = part(x)

    def gather(ref, which):
        def copy(d, incoming=False):
            came = lax.rem(narrow + n_narrow - d, n_narrow) if incoming else narrow
            return pltpu.make_async_remote_copy(
                src_ref=ref.at[narrow],
                dst_ref=ref.at[came],
                send_sem=gsend_sem.at[which, d - 1],
                recv_sem=grecv_sem.at[which, d - 1],
                device_id=others[d - 1],
                device_id_type=MESH,
            )

        def start():
            for d in range(1, n_narrow):
                copy(d).start()

        def finish():
            for d in range(1, n_narrow):
                copy(d, incoming=True).wait_recv()

        def drain():
            for d in range(1, n_narrow):
                copy(d).wait_send()

        return start, finish, drain

    face_start, face_finish, face_drain = gather(gather_faces, 0)
    source_start, source_finish, source_drain = gather(gather_source, 1)
    face_start()

    def neighbour_sum(level, e, x, own):
        Y = dims(level)[1]
        p = iterates[level]
        step = 1 << level
        edge = 0 if own else EDGE
        start, rows = PAD - edge, Y + 2 * edge
        at = pl.ds(EDGE - edge, rows)
        i, j = x + HALO[level], x + HX[level]
        here = p[e, j, pl.ds(start, rows), :]
        total = (
            face_x[level][i, at, :] * p[e, j - 1, pl.ds(start, rows), :]
            + face_x[level][i + 1, at, :] * p[e, j + 1, pl.ds(start, rows), :]
        )
        total += face_y[level][i, at, :] * p[e, j, pl.ds(start - 1, rows), :]
        total += face_y[level][i, pl.ds(EDGE - edge + 1, rows), :] * p[
            e, j, pl.ds(start + 1, rows), :
        ]
        total += inner_zl[level][i, at, :] * pltpu.roll(here, step, 1)
        total += inner_zh[level][i, at, :] * pltpu.roll(here, Z - step, 1)
        return here, total

    def sweep(level, e, x, own):
        Y = dims(level)[1]
        edge = 0 if own else EDGE
        here, total = neighbour_sum(level, e, x, own)
        w = weight[level][x + HALO[level], pl.ds(EDGE - edge, Y + 2 * edge), :]
        if e == 0:
            return (1.0 + KEEP) * here + w * total
        start = iterates[level][0, x + HX[level], pl.ds(PAD - edge, Y + 2 * edge), :]
        return (KEEP * here + start) + w * total

    def wide_sweep(level, e, halo):
        X, Y = dims(level)

        def plane(j, carry):
            x = j - halo
            iterates[level][e + 1, x + HX[level], pl.ds(PAD - EDGE, Y + 2 * EDGE), :] = sweep(
                level, e, x, False
            )
            return carry

        lax.fori_loop(0, X + 2 * halo, plane, 0, unroll=3 if X + 2 * halo == 18 else 2)

    finish_first = None
    for level in range(LEVELS):
        X, Y = dims(level)
        if level > 0:
            finish = level_exchange(level, 0, 0, level)
            push()
            finish()
        wide_sweep(level, 0, 1)
        if level == 0:
            finish_first = level_exchange(0, 1, 2, LEVELS)
        h, half, last = HALO[level], Y // 2, level + 1 == LEVELS
        own_rows = pl.ds(EDGE, Y)

        def restrict(x, carry, level=level, Y=Y, h=h, half=half, last=last, own_rows=own_rows):
            both = None
            for k in range(2):
                fine = 2 * x + k
                here, total = neighbour_sum(level, 1, fine, True)
                b = source[0][fine + HX[0], own_rows, :] if level == 0 else source[level][fine]
                left = (b - diag[level][fine + h, own_rows, :] * here) + total
                both = left if both is None else both + left
            tmp[:Y, :] = both
            summed = (
                tmp[pl.ds(0, half, stride=2), :] + tmp[pl.ds(1, half, stride=2), :]
            )
            summed = 0.5 * z_pair(summed, level)
            if last:
                gather_source[narrow, x] = summed
            else:
                source[level + 1][x] = summed
                w = weight[level + 1][x + HALO[level + 1], pl.ds(EDGE, half), :]
                iterates[level + 1][0, x + HX[level + 1], pl.ds(PAD, half), :] = w * summed
            return carry

        if last:
            for x in range(X // 2):
                restrict(x, 0)
        else:
            lax.fori_loop(0, X // 2, restrict, 0, unroll=4)

    source_start()
    push()
    face_finish()
    source_finish()
    X, Y = dims(LEVELS)
    step = 1 << LEVELS
    row = lax.broadcasted_iota(jnp.int32, (Y, Z), 0)
    col = lax.broadcasted_iota(jnp.int32, (Y, Z), 1)
    for n in range(n_narrow):
        for x in range(X):
            fxl, fxh = gather_faces[n, x], gather_faces[n, x + 1]
            fyl, fyh, fzl, fzh = (gather_faces[n, X + 1 + k * X + x] for k in range(4))
            total = ((fxl + fxh) + (fyl + fyh)) + (fzl + fzh)
            w = DAMPING / total
            at = n * X + x
            coef[0, at] = w * fxl
            coef[1, at] = w * fxh
            coef[2, at] = jnp.where(row == 0, 0.0, w * fyl)
            coef[3, at] = jnp.where(row == Y - 1, 0.0, w * fyh)
            coef[4, at] = jnp.where(col < step, 0.0, w * fzl)
            coef[5, at] = jnp.where(col >= Z - step, 0.0, w * fzh)
            coef[6, at] = w * gather_source[n, x]

    zero_plane = jnp.zeros((1, Y, Z), jnp.float32)

    def bottom(k, cur):
        new = KEEP * cur + coef[6]
        new += coef[0] * jnp.concatenate([zero_plane, cur[:-1]], axis=0)
        new += coef[1] * jnp.concatenate([cur[1:], zero_plane], axis=0)
        new += coef[2] * pltpu.roll(cur, 1, 1)
        new += coef[3] * pltpu.roll(cur, Y - 1, 1)
        new += coef[4] * pltpu.roll(cur, step, 2)
        new += coef[5] * pltpu.roll(cur, Z - step, 2)
        return new

    push()
    coef[7] = lax.fori_loop(0, BOTTOM - 1, bottom, coef[6], unroll=15)
    for x in range(X):
        answer[LEVELS][x] = coef[7, narrow * X + x]

    def repeat_rows(e, count):
        tmp[pl.ds(0, count, stride=2), :] = e
        tmp[pl.ds(1, count, stride=2), :] = e
        return tmp[: 2 * count, :]

    for level in reversed(range(1, LEVELS)):
        X, Y = dims(level)
        half = Y // 2

        def raised(x, carry, level=level, Y=Y, half=half):
            e = repeat_rows(answer[level + 1][x // 2], half)
            at = x + HX[level]
            iterates[level][2, at, PAD : PAD + Y, :] = (
                iterates[level][1, at, PAD : PAD + Y, :] + e
            )
            return carry

        lax.fori_loop(0, X, raised, 0, unroll=4)
        finish = level_exchange(level, 2, 2, LEVELS + level)
        push()
        finish()
        out_halo = 1 if level == 1 else 0
        wide_sweep(level, 2, 1 + out_halo)

        def close(j, carry, level=level, out_halo=out_halo):
            if out_halo:
                near_answer[j, pl.ds(PAD - EDGE, dims(level)[1] + 2 * EDGE), :] = sweep(
                    level, 3, j - out_halo, False
                )
            else:
                answer[level][j] = sweep(level, 3, j, True)
            return carry

        lax.fori_loop(0, X + 2 * out_halo, close, 0, unroll=2)

    for x in range(X0):
        iterates[0][2, x + HX[0], PAD : PAD + Y0, :] = iterates[0][1, x + HX[0], PAD : PAD + Y0, :]
    finish_first()
    coarse_rows = pl.ds(PAD - EDGE // 2, Y0 // 2 + EDGE)

    def raise_first(j, carry):
        e = repeat_rows(near_answer[j // 2, coarse_rows, :], Y0 // 2 + EDGE)
        iterates[0][2, j, win0, :] = iterates[0][2, j, win0, :] + e
        return carry

    lax.fori_loop(0, X0 + 2 * HX[0], raise_first, 0, unroll=4)
    wide_sweep(0, 2, 1)

    def close_first(x, carry):
        pressure[x] = sweep(0, 3, x, True)
        return carry

    lax.fori_loop(0, X0, close_first, 0, unroll=4)

    assert len(pushed) == len(FAR)
    pressure_copy = pltpu.make_async_copy(pressure, pressure_ref, local_sem.at[4])
    pressure_copy.start()

    def merge_solved(q, carry):
        merged[q, :SOLVED] = arrived[receive_index[q, 0]]
        return carry

    lax.fori_loop(0, PER_OWNER, merge_solved, 0, unroll=4)
    face_drain()
    source_drain()
    for drain in drains:
        drain()
    pressure_copy.wait()

    def carried_end(k, carry):
        carried_bulk(k).wait_send()
        carried_bulk(k, incoming=True).wait_recv()
        return carry

    lax.fori_loop(1, owners, carried_end, 0)

    def out_copy(g):
        group = pl.ds(g * OUT_GROUP, OUT_GROUP)
        return pltpu.make_async_copy(merged.at[group], migrated_ref.at[group], out_sem.at[g])

    for g in range(PER_OWNER // OUT_GROUP):

        def merge_carried(q, carry):
            merged[q, SOLVED:] = moved[receive_index[q, 0]]
            return carry

        lax.fori_loop(g * OUT_GROUP, (g + 1) * OUT_GROUP, merge_carried, 0, unroll=4)
        out_copy(g).start()

    for g in range(PER_OWNER // OUT_GROUP):
        out_copy(g).wait()


def f32(*shape):
    return pltpu.VMEM(shape, jnp.float32)


def bf16(*shape):
    return pltpu.VMEM(shape, jnp.bfloat16)


def call_solve(n_wide, n_narrow, table, fields):
    per_owner, n_fields, cells = fields.shape
    owners = n_wide * n_narrow
    slots = owners * CAPACITY
    X3, Y3 = dims(LEVELS)
    levels = [(level, *dims(level)) for level in range(LEVELS)]
    faces = [f32(X + 2 * HALO[l], Y + 2 * EDGE, Z) for l, X, Y in levels]
    moves = 2 * LEVELS
    packs = {
        "solved": bf16(slots, SOLVED, cells),
        "carried": bf16(slots, n_fields - SOLVED, cells),
    }
    dma = pltpu.SemaphoreType.DMA
    scratch = [
        pltpu.VMEM(table.shape, jnp.int32),
        bf16(*fields.shape),
        packs["solved"],
        packs["carried"],
        packs["solved"],
        packs["carried"],
        bf16(*fields.shape),
        f32(X0, Y0, Z),
        pltpu.VMEM((CAPACITY, owners, Z), jnp.int32),
        pltpu.VMEM((per_owner, Z), jnp.int32),
        pltpu.SMEM((CAPACITY, owners, Z), jnp.int32),
        pltpu.SMEM((per_owner, Z), jnp.int32),
        f32(64, Z),
        f32(Y0 + 2 * PAD, Z),
        [f32(X0 + 2 * h, Y0 + 2 * PAD, Z) for h in FIELD_HALO],
        bf16(2, HALO_PLANES, Y0, Z),
        bf16(2, HALO_PLANES, Y0, Z),
        bf16(2, 2 * X0, PAD, Z),
        bf16(2, 2 * X0, PAD, Z),
        bf16(4, 2 * CORNER, PAD, Z),
        bf16(4, 2 * CORNER, PAD, Z),
        [f32(4, X + 2 * HX[l], Y + 2 * PAD, Z) for l, X, Y in levels],
        [f32(2, 2, X * ROWS[l] // PAD, PAD, Z) for l, X, Y in levels],
        [f32(2, 2, X * ROWS[l] // PAD, PAD, Z) for l, X, Y in levels],
        [f32(X + 2 * HALO[l] + 1, Y + 2 * EDGE, Z) for l, X, Y in levels],
        [f32(X + 2 * HALO[l], Y + 2 * EDGE + 8, Z) for l, X, Y in levels],
        faces,
        faces,
        faces,
        faces,
        faces,
        faces,
        [f32(X0 + 2 * HX[0], Y0 + 2 * EDGE, Z)] + [f32(X, Y, Z) for l, X, Y in levels[1:]],
        [f32(*dims(level), Z) for level in range(LEVELS + 1)],
        f32(dims(1)[0] + 2, dims(1)[1] + 2 * PAD, Z),
        f32(n_narrow, 5 * X3 + 1, Y3, Z),
        f32(n_narrow, X3, Y3, Z),
        f32(8, n_narrow * X3, Y3, Z),
        dma((moves, 8)),
        dma((moves, 8)),
        dma((2, n_narrow - 1)),
        dma((2, n_narrow - 1)),
        dma((owners,)),
        dma((owners,)),
        dma((owners,)),
        dma((owners,)),
        dma((5,)),
        dma((per_owner // OUT_GROUP,)),
    ]
    anywhere = pl.BlockSpec(memory_space=pl.ANY)
    return pl.pallas_call(
        functools.partial(solve_kernel, n_wide, n_narrow),
        out_shape=(
            jax.ShapeDtypeStruct(fields.shape, fields.dtype),
            jax.ShapeDtypeStruct((X0, Y0, Z), jnp.float32),
        ),
        in_specs=[anywhere, anywhere],
        out_specs=(anywhere, anywhere),
        scratch_shapes=scratch,
        compiler_params=pltpu.CompilerParams(
            collective_id=0, has_side_effects=True, vmem_limit_bytes=min(60, 46 + owners // 8) * 1024 * 1024
        ),
        cost_estimate=pl.CostEstimate(
            flops=200_000_000, bytes_accessed=200_000_000, transcendentals=0
        ),
    )(table, fields)


def hand_over_kernel(migrated_ref, pressure_ref, migrated_out, pressure_out, sem):
    copies = []
    for n, (src, dst) in enumerate(((migrated_ref, migrated_out), (pressure_ref, pressure_out))):
        size = src.shape[0] // PIECES
        for g in range(PIECES):
            piece = pl.ds(g * size, size)
            copies.append(pltpu.make_async_copy(src.at[piece], dst.at[piece], sem.at[n, g]))
    for copy in copies:
        copy.start()
    for copy in copies:
        copy.wait()


def hand_over(migrated, pressure):
    anywhere = pl.BlockSpec(memory_space=pl.ANY)
    return pl.pallas_call(
        hand_over_kernel,
        out_shape=tuple(jax.ShapeDtypeStruct(a.shape, a.dtype) for a in (migrated, pressure)),
        in_specs=[anywhere, anywhere],
        out_specs=(anywhere, anywhere),
        scratch_shapes=[pltpu.SemaphoreType.DMA((2, PIECES))],
        compiler_params=pltpu.CompilerParams(vmem_limit_bytes=1024 * 1024),
    )(migrated, pressure)


def shards(n_wide, n_narrow, target_slot, fields):
    return hand_over(*call_solve(n_wide, n_narrow, target_slot.reshape(-1, Z), fields))


def solution(mesh):
    body = functools.partial(shards, mesh.shape["wide"], mesh.shape["narrow"])
    in_specs = (P(), P(("wide", "narrow"), None, None))
    out_specs = (P(("wide", "narrow"), None, None), P("narrow", "wide", None))
    return jax.shard_map(body, mesh=mesh, in_specs=in_specs, out_specs=out_specs, check_vma=False)
```

```python
import functools

import jax
import jax.numpy as jnp
from jax import lax
from jax.experimental import pallas as pl
from jax.experimental.pallas import tpu as pltpu
from jax.sharding import PartitionSpec as P

PATCH = 16
BYP = 4
BZP = 8
LEVELS = 3
BOTTOM = 16
DAMPING = 0.8
KEEP = 1.0 - DAMPING
SOLVED = 4
CAPACITY = 2
PER_OWNER = 32
X0 = PATCH
Y0 = PATCH * BYP
Z = PATCH * BZP
PAD = 8
EDGE = 4
HX = (2, 3, 2)
ROWS = (2, 4, 2)
CORNER_PLANES = (1, 3, 1)
HALO = (4, 2, 1)
FIELD_HALO = (3, 2, 2, 5)
HALO_PLANES = sum(FIELD_HALO)
CORNER = max(FIELD_HALO)
MESH = pl.DeviceIdType.MESH
FAR = (5, 0, 1, 2, 1, 1, 1, 1, 1, 3)
NEAR = (9, 0, 0, 1, 1, 1, 1, 1, 1, 0)
OUT_GROUP = 8
PIECES = 8
SIDES = tuple((dx, dy) for dx in (-1, 0, 1) for dy in (-1, 0, 1) if dx or dy)


def dims(level):
    return X0 >> level, Y0 >> level


def solve_kernel(
    n_wide,
    n_narrow,
    target_ref,
    fields_ref,
    migrated_ref,
    pressure_ref,
    target,
    fields,
    solved,
    carried,
    arrived,
    moved,
    merged,
    pressure,
    send_index_v,
    receive_index_v,
    send_index,
    receive_index,
    turn,
    tmp,
    grids,
    sent_x,
    got_x,
    sent_y,
    got_y,
    sent_c,
    got_c,
    iterates,
    sent_rows,
    got_rows,
    face_x,
    face_y,
    face_zl,
    face_zh,
    inner_zl,
    inner_zh,
    diag,
    weight,
    source,
    answer,
    near_answer,
    gather_faces,
    gather_source,
    coef,
    send_sem,
    recv_sem,
    gsend_sem,
    grecv_sem,
    carry_send_sem,
    carry_recv_sem,
    solved_send_sem,
    solved_recv_sem,
    local_sem,
    out_sem,
):
    wide = lax.axis_index("wide")
    narrow = lax.axis_index("narrow")
    owners = n_wide * n_narrow
    me = wide * n_narrow + narrow
    low = {-1: narrow > 0, 1: narrow < n_narrow - 1, 0: None}
    side_y = {-1: wide > 0, 1: wide < n_wide - 1, 0: None}

    def has(side):
        dx, dy = side
        if dx == 0:
            return side_y[dy]
        if dy == 0:
            return low[dx]
        return jnp.logical_and(low[dx], side_y[dy])

    def peer(side):
        return (wide + side[1], narrow + side[0])

    def back(side):
        return (-side[0], -side[1])

    others = [(wide, lax.rem(narrow + d, n_narrow)) for d in range(1, n_narrow)]

    target_copy = pltpu.make_async_copy(target_ref, target, local_sem.at[0])
    target_copy.start()
    fields_copy = pltpu.make_async_copy(fields_ref, fields, local_sem.at[1])
    fields_copy.start()

    def at_distance(distance):
        owner = jnp.bitwise_xor(me, distance)
        return owner, (owner // n_narrow, lax.rem(owner, n_narrow))

    def partner(k):
        return at_distance(jnp.where(lax.rem(k, 2) == 1, owners // 2 + k // 2, k // 2))

    barrier = pltpu.get_barrier_semaphore()

    def greet(k, carry):
        _, device = partner(k)
        pl.semaphore_signal(barrier, inc=1, device_id=device, device_id_type=MESH)
        return carry

    lax.fori_loop(1, owners, greet, 0)

    target_copy.wait()
    segments = Z // PER_OWNER
    own_row = target[pl.ds(me // segments, 1), :]
    lane_d = lax.broadcasted_iota(jnp.int32, (owners, Z), 1)
    owner_d = lax.broadcasted_iota(jnp.int32, (owners, Z), 0)
    mine = jnp.logical_and(
        lane_d // PER_OWNER == lax.rem(me, segments), own_row // PER_OWNER == owner_d
    )
    place = lax.rem(lane_d, PER_OWNER)
    low_place = jnp.min(jnp.where(mine, place, PER_OWNER - 1), axis=1, keepdims=True)
    high_place = jnp.max(jnp.where(mine, place, 0), axis=1, keepdims=True)
    send_index_v[0] = jnp.broadcast_to(low_place, (owners, Z))
    send_index_v[1] = jnp.broadcast_to(high_place, (owners, Z))
    index_copy = pltpu.make_async_copy(send_index_v, send_index, local_sem.at[2])
    index_copy.start()

    table = target[...]
    t_rows = table.shape[0]
    t_lane = lax.broadcasted_iota(jnp.int32, (t_rows, Z), 1)
    t_owner = lax.broadcasted_iota(jnp.int32, (t_rows, Z), 0) * segments + t_lane // PER_OWNER
    t_place = lax.rem(t_lane, PER_OWNER)
    seen = jnp.where(table // PER_OWNER == me, 1, 0)
    step = 1
    while step < PER_OWNER:
        seen = jnp.maximum(seen, jnp.where(t_place >= step, pltpu.roll(seen, step, 1), 0))
        step *= 2
    rank = jnp.where(t_place >= 1, pltpu.roll(seen, 1, 1), 0)
    slot = t_owner * CAPACITY + rank
    for q in range(PER_OWNER):
        hit = jnp.where(table == me * PER_OWNER + q, slot, 0)
        receive_index_v[q : q + 1, :] = jnp.max(hit, axis=0, keepdims=True)
    slots_q = jnp.max(receive_index_v[...], axis=1, keepdims=True)
    receive_index_v[...] = jnp.broadcast_to(slots_q, (PER_OWNER, Z))
    receive_copy = pltpu.make_async_copy(receive_index_v, receive_index, local_sem.at[3])
    receive_copy.start()

    index_copy.wait()
    fields_copy.wait()
    pl.semaphore_wait(barrier, owners - 1)

    def block(owner):
        return pl.ds(owner * CAPACITY, CAPACITY)

    def bulk(whom, packed, landed, send, recv, k, incoming=False):
        owner, device = whom(k)
        return pltpu.make_async_remote_copy(
            src_ref=packed.at[block(me if incoming else owner)],
            dst_ref=landed.at[block(owner if incoming else me)],
            send_sem=send.at[k],
            recv_sem=recv.at[k],
            device_id=device,
            device_id_type=MESH,
        )

    solved_bulk = functools.partial(bulk, partner, solved, arrived, solved_send_sem, solved_recv_sem)
    carried_bulk = functools.partial(bulk, at_distance, carried, moved, carry_send_sem, carry_recv_sem)

    def pack_solved(k, carry):
        owner, _ = partner(k)
        for r in range(CAPACITY):
            solved[owner * CAPACITY + r] = fields[send_index[r, owner, 0], :SOLVED]
        solved_bulk(k).start()
        return carry

    def pack_carried(k, carry):
        owner, _ = at_distance(k)
        for r in range(CAPACITY):
            carried[owner * CAPACITY + r] = fields[send_index[r, owner, 0], SOLVED:]
        return carry

    lax.fori_loop(1, owners, pack_solved, 0)
    for r in range(CAPACITY):
        patch = fields[send_index[r, me, 0]]
        arrived[me * CAPACITY + r] = patch[:SOLVED]
        moved[me * CAPACITY + r] = patch[SOLVED:]
    lax.fori_loop(1, owners, pack_carried, 0)

    half_way = owners // 2

    def cuts(shares, first, end):
        return [first + (end - first) * sum(shares[:k]) // sum(shares) for k in range(len(shares) + 1)]

    far = cuts(FAR, half_way, owners)
    near = cuts(NEAR, 1, half_way)
    pushed = []

    def begin(k, carry):
        carried_bulk(k).start()
        return carry

    def push():
        turn_now = len(pushed)
        pushed.append(turn_now)
        for bounds in (near, far):
            if bounds[turn_now] < bounds[turn_now + 1]:
                lax.fori_loop(bounds[turn_now], bounds[turn_now + 1], begin, 0)

    push()
    for level in range(LEVELS):
        X, Y = dims(level)
        p = iterates[level]
        hx = HX[level]
        for e in (2,) if level == 0 else (0, 2):

            @pl.when(jnp.logical_not(low[-1]))
            def _(p=p, e=e, Y=Y, hx=hx):
                p[e, :hx] = jnp.zeros((hx, Y + 2 * PAD, Z), jnp.float32)

            @pl.when(jnp.logical_not(low[1]))
            def _(p=p, e=e, X=X, Y=Y, hx=hx):
                p[e, hx + X :] = jnp.zeros((hx, Y + 2 * PAD, Z), jnp.float32)

            @pl.when(jnp.logical_not(side_y[-1]))
            def _(p=p, e=e, X=X, Y=Y, hx=hx):
                p[e, :, :PAD] = jnp.zeros((X + 2 * hx, PAD, Z), jnp.float32)

            @pl.when(jnp.logical_not(side_y[1]))
            def _(p=p, e=e, X=X, Y=Y, hx=hx):
                p[e, :, PAD + Y :] = jnp.zeros((X + 2 * hx, PAD, Z), jnp.float32)

    receive_copy.wait()

    def solved_arrive(k, carry):
        solved_bulk(k, incoming=True).wait_recv()
        return carry

    lax.fori_loop(1, owners, solved_arrive, 0)
    push()

    lane = lax.broadcasted_iota(jnp.int32, (8, Z), 1)
    block_lane = lane // PATCH
    lower_bits = [(block_lane // s) % 2 == 1 for s in (1, 2, 4)]

    def to_grid(step, carry):
        b = step // X0
        i = step % X0
        at = pl.multiple_of(i * 2 * Z, 2 * Z)
        rows = []
        for c in range(BZP):
            both = arrived[receive_index[b * BZP + c, 0], :, pl.ds(at, 2 * Z)].astype(
                jnp.float32
            )
            rows.append(jnp.concatenate([both[:, :Z], both[:, Z:]], axis=0))
        for bit, s in zip(lower_bits, (1, 2, 4)):
            new = list(rows)
            for c in range(BZP):
                if c & s == 0:
                    lower, upper = rows[c], rows[c + s]
                    new[c] = jnp.where(bit, pltpu.roll(upper, PATCH * s, 1), lower)
                    new[c + s] = jnp.where(bit, upper, pltpu.roll(lower, Z - PATCH * s, 1))
            rows = new
        for j in range(8):
            turn[8 * j : 8 * j + 8, :] = rows[j]
        for half in range(2):
            y = pl.multiple_of(b * PATCH + half * 8, 8)
            for f, ref in enumerate(grids):
                values = turn[pl.ds(half * SOLVED + f, 8, stride=8), :]
                ref[i + FIELD_HALO[f], pl.ds(PAD + y, 8), :] = values
        return carry

    lax.fori_loop(0, BYP * X0, to_grid, 0, unroll=8)

    def known(side, values):
        return jnp.where(has(side), values.astype(jnp.float32), 0.0)

    planes = []
    for f, h in enumerate(FIELD_HALO):
        planes += [(f, h, j) for j in range(h)]
    for n, (f, h, j) in enumerate(planes):
        for side, x in ((0, j), (1, X0 - h + j)):
            sent_x[side, n] = grids[f][h + x, PAD : PAD + Y0, :].astype(jnp.bfloat16)
    at_row = lax.broadcasted_iota(jnp.int32, (PAD, Z), 0)

    def end_rows(end, x):
        y = (0, Y0 - PAD)[end]
        u, v, w, r = (
            grids[f][h + x, PAD + y : PAD + y + PAD, :] for f, h in enumerate(FIELD_HALO)
        )
        if end == 0:
            uvw = jnp.where(
                at_row < 2, u, jnp.where(at_row < 5, pltpu.roll(v, 2, 0), pltpu.roll(w, 5, 0))
            )
        else:
            uvw = jnp.where(
                at_row > 5, u, jnp.where(at_row > 2, pltpu.roll(v, 6, 0), pltpu.roll(w, 3, 0))
            )
        return r.astype(jnp.bfloat16), uvw.astype(jnp.bfloat16)

    def keep_rows(end, x, uvw, r):
        y = (0, PAD + Y0)[end]
        u, v, w = (
            (uvw, pltpu.roll(uvw, 2, 0), pltpu.roll(uvw, 5, 0)),
            (uvw, pltpu.roll(uvw, 6, 0), pltpu.roll(uvw, 3, 0)),
        )[end]
        for f, values in enumerate((u, v, w, r)):
            h = FIELD_HALO[f]
            if -h <= x < X0 + h:
                grids[f][h + x, y : y + PAD, :] = values

    for end in range(2):
        for i in range(X0):
            sent_y[end, i], sent_y[end, X0 + i] = end_rows(end, i)
        for j in range(CORNER):
            for side, x in ((0, j), (1, X0 - CORNER + j)):
                (
                    sent_c[2 * side + end, j],
                    sent_c[2 * side + end, CORNER + j],
                ) = end_rows(end, x)

    def field_refs(side):
        dx, dy = side
        if dy == 0:
            return sent_x.at[(dx + 1) // 2], got_x.at[(1 - dx) // 2]
        if dx == 0:
            return sent_y.at[(dy + 1) // 2], got_y.at[(1 - dy) // 2]
        return sent_c.at[dx + 1 + (dy + 1) // 2], got_c.at[1 - dx + (1 - dy) // 2]

    def level_refs(level, e, into):
        X, Y = dims(level)
        p = iterates[level]
        hx = HX[level]

        def refs(side):
            dx, dy = side
            if dx == 0:
                which = into // 2
                return (
                    sent_rows[level].at[which, (dy + 1) // 2],
                    got_rows[level].at[which, (1 - dy) // 2],
                )
            h = hx if dy == 0 else CORNER_PLANES[level]
            src_x, dst_x, n_x = {
                -1: (hx, hx + X, h),
                0: (hx, hx, X),
                1: (hx + X - h, hx - h, h),
            }[dx]
            src_y, dst_y, n_y = {
                -1: (PAD, PAD + Y, PAD),
                0: (PAD, PAD, Y),
                1: (Y, 0, PAD),
            }[dy]
            return (
                p.at[e, pl.ds(src_x, n_x), pl.ds(src_y, n_y)],
                p.at[into, pl.ds(dst_x, n_x), pl.ds(dst_y, n_y)],
            )

        return refs

    def pack_rows(level, e, into):
        X, Y = dims(level)
        p, n = iterates[level], ROWS[level]
        per = PAD // n
        for end, y, first_row in ((0, PAD, 0), (1, Y, PAD - n)):
            for g in range(X // per):
                tile = None
                for k in range(per):
                    rows = p[e, HX[level] + per * g + k, y : y + PAD, :]
                    shift = (n * k - first_row) % PAD
                    rows = pltpu.roll(rows, shift, 0) if shift else rows
                    tile = rows if tile is None else jnp.where(at_row >= n * k, rows, tile)
                sent_rows[level][into // 2, end, g] = tile

    def unpack_rows(level, into):
        X, Y = dims(level)
        p, n = iterates[level], ROWS[level]
        per = PAD // n
        for end, y, first_row in ((0, 0, PAD - n), (1, PAD + Y, 0)):
            for g in range(X // per):
                tile = known((0, 2 * end - 1), got_rows[level][into // 2, end, g])
                for k in range(per):
                    shift = (first_row - n * k) % PAD
                    p[into, HX[level] + per * g + k, y : y + PAD, :] = (
                        pltpu.roll(tile, shift, 0) if shift else tile
                    )

    drains = []

    def exchange(refs, move):
        def copy(side, incoming=False):
            src, dst = refs(back(side) if incoming else side)
            return pltpu.make_async_remote_copy(
                src_ref=src,
                dst_ref=dst,
                send_sem=send_sem.at[move, SIDES.index(side)],
                recv_sem=recv_sem.at[move, SIDES.index(side if incoming else back(side))],
                device_id=peer(side),
                device_id_type=MESH,
            )

        def each(act):
            for side in SIDES:

                @pl.when(has(side))
                def _(side=side):
                    act(side)

        drains.append(lambda: each(lambda side: copy(side).wait_send()))
        return (
            lambda: each(lambda side: copy(side).start()),
            lambda: each(lambda side: copy(side, incoming=True).wait_recv()),
        )

    def level_exchange(level, e, into, move):
        pack_rows(level, e, into)
        start, arrive = exchange(level_refs(level, e, into), move)
        start()

        def finish():
            arrive()
            unpack_rows(level, into)

        return finish

    def lanes(values):
        return lax.broadcasted_iota(jnp.int32, values.shape, 1)

    def z_low(values, step):
        return jnp.where(lanes(values) < step, 0.0, pltpu.roll(values, step, 1))

    def z_high(values, step):
        return jnp.where(lanes(values) >= Z - step, 0.0, pltpu.roll(values, Z - step, 1))

    def keep_inner(level, i, at, zl, zh):
        step = 1 << level
        inner_zl[level][i, at, :] = jnp.where(lanes(zl) < step, 0.0, zl)
        inner_zh[level][i, at, :] = jnp.where(lanes(zh) >= Z - step, 0.0, zh)

    grid_u, grid_v, grid_w, grid_r = grids
    rows0 = Y0 + 2 * EDGE
    win0 = pl.ds(PAD - EDGE, rows0)

    def face(a, b):
        return 2.0 / jnp.maximum(a + b, 0.5)

    def faces(i, row=0, rows=rows0):
        at, start = pl.ds(row, rows), row + PAD - EDGE
        here = grid_r[i + 1, pl.ds(start, rows), :]
        face_x[0][i, at, :] = face(grid_r[i, pl.ds(start, rows), :], here)
        face_y[0][i, at, :] = face(grid_r[i + 1, pl.ds(start - 1, rows), :], here)
        if row + rows == rows0:
            last = PAD + EDGE + Y0
            face_y[0][i, rows0 : rows0 + EDGE, :] = face(
                grid_r[i + 1, last - 1 : last + EDGE - 1, :], grid_r[i + 1, last : last + EDGE, :]
            )
        zl, zh = face(z_low(here, 1), here), face(z_high(here, 1), here)
        face_zl[0][i, at, :] = zl
        face_zh[0][i, at, :] = zh
        keep_inner(0, i, at, zl, zh)

    def inside_rows(level, row, rows):
        Y = dims(level)[1]
        at = lax.broadcasted_iota(jnp.int32, (rows, Z), 0) + row
        return jnp.logical_and(
            jnp.logical_or(side_y[-1], at >= EDGE), jnp.logical_or(side_y[1], at < EDGE + Y)
        )

    def weigh(level, i, row=0, rows=None):
        X, Y = dims(level)
        h, rows = HALO[level], rows or Y + 2 * EDGE
        at = pl.ds(row, rows)
        total = face_x[level][i, at, :] + face_x[level][i + 1, at, :]
        total += face_y[level][i, at, :] + face_y[level][i, pl.ds(row + 1, rows), :]
        total += face_zl[level][i, at, :] + face_zh[level][i, at, :]
        inside = jnp.logical_and(
            jnp.logical_or(low[-1], i >= h), jnp.logical_or(low[1], i < h + X)
        )
        w = jnp.where(jnp.logical_and(inside_rows(level, row, rows), inside), DAMPING / total, 0.0)
        diag[level][i, at, :] = total
        weight[level][i, at, :] = w
        return w

    def first(j, row=0, rows=rows0):
        at, start = pl.ds(row, rows), row + PAD - EDGE
        mid = pl.ds(start, rows)
        w = weigh(0, j + HALO[0] - HX[0], row, rows)
        wz = grid_w[j + FIELD_HALO[2] - HX[0], mid, :]
        u_at, v_at = j + FIELD_HALO[0] - HX[0], j + FIELD_HALO[1] - HX[0]
        du = grid_u[u_at + 1, mid, :] - grid_u[u_at - 1, mid, :]
        dv = grid_v[v_at, pl.ds(start + 1, rows), :] - grid_v[v_at, pl.ds(start - 1, rows), :]
        b = -0.5 * ((du + dv) + (z_high(wz, 1) - z_low(wz, 1)))
        source[0][j, at, :] = b
        iterates[0][0, j, mid, :] = w * b

    def planes_of(act, low_j, high_j, edges_only=False, unroll=2):
        def one(j, carry):
            if edges_only:
                act(j, 0, PAD)
                act(j, rows0 - PAD, PAD)
            else:
                act(j)
            return carry

        lax.fori_loop(low_j, high_j, one, 0, unroll=unroll)

    n_faces, n_first = X0 + 2 * HALO[0], X0 + 2 * HX[0]
    face_from, face_to = HALO[0] + 1, HALO[0] + X0 - 1
    first_from, first_to = HX[0] + 1, HX[0] + X0 - 2
    field_start, field_arrive = exchange(field_refs, 0)
    field_start()
    push()

    def solved_end(k, carry):
        solved_bulk(k).wait_send()
        return carry

    lax.fori_loop(1, owners, solved_end, 0, unroll=False)
    planes_of(faces, face_from, face_to)
    planes_of(first, first_from, first_to)
    field_arrive()

    for n, (f, h, j) in enumerate(planes):
        for dx, x in ((-1, j), (1, h + X0 + j)):
            at = (dx + 1) // 2
            grids[f][x, PAD : PAD + Y0, :] = known((dx, 0), got_x[at, n])
    for end, dy in ((0, -1), (1, 1)):
        for i in range(X0):
            r, uvw = (known((0, dy), got_y[end, k * X0 + i]) for k in range(2))
            keep_rows(end, i, uvw, r)
        for j in range(CORNER):
            for side, dx, x in ((0, -1, j - CORNER), (1, 1, X0 + j)):
                r, uvw = (
                    known((dx, dy), got_c[2 * side + end, k * CORNER + j]) for k in range(2)
                )
                keep_rows(end, x, uvw, r)

    push()
    planes_of(faces, 0, face_from)
    planes_of(faces, face_to, n_faces)
    planes_of(faces, face_from, face_to, edges_only=True)
    face_x[0][n_faces] = face(grid_r[n_faces, win0, :], grid_r[n_faces + 1, win0, :])
    planes_of(first, 0, first_from, unroll=3)
    planes_of(first, first_to, n_first, unroll=4)
    planes_of(first, first_from, first_to, edges_only=True)

    def z_bit(values, level):
        return (lanes(values) // (1 << level)) % 2 == 1

    def z_pair(values, level):
        step = 1 << level
        return values + jnp.where(
            z_bit(values, level), pltpu.roll(values, step, 1), pltpu.roll(values, Z - step, 1)
        )

    def z_even(values, level):
        return jnp.where(z_bit(values, level), pltpu.roll(values, 1 << level, 1), values)

    def z_odd(values, level):
        return jnp.where(z_bit(values, level), values, pltpu.roll(values, Z - (1 << level), 1))

    def coarse_faces(level, base, start, count, more=0):
        even = pl.ds(start, count, stride=2)
        even_y = pl.ds(start, count + more, stride=2)
        odd = pl.ds(start + 1, count, stride=2)
        after = pl.ds(start + 2, count, stride=2)
        fx, fy, zl, zh = (f[level] for f in (face_x, face_y, face_zl, face_zh))

        def cx(x):
            i = base + 2 * x
            return 0.25 * z_pair(fx[i, even, :] + fx[i, odd, :], level)

        def cy(x, rows):
            i = base + 2 * x
            return 0.25 * z_pair(fy[i, rows, :] + fy[i + 1, rows, :], level)

        def four(f, x):
            i = base + 2 * x
            return 0.25 * (
                (f[i, even, :] + f[i, odd, :]) + (f[i + 1, even, :] + f[i + 1, odd, :])
            )

        return (
            cx,
            lambda x: cy(x, even_y),
            lambda x: cy(x, after),
            lambda x: z_even(four(zl, x), level),
            lambda x: z_odd(four(zh, x), level),
        )

    for level in range(LEVELS - 1):
        X, Y = dims(level + 1)
        count = Y + EDGE
        n_planes = X + 2 * HALO[level + 1]
        cx, cyl, _, czl, czh = coarse_faces(level, 0, 0, count, more=1)
        rows = pl.ds(EDGE // 2, count)

        def coarsen(i, carry, level=level, rows=rows, count=count, cx=cx, cyl=cyl, czl=czl, czh=czh):
            face_x[level + 1][i, rows, :] = cx(i)
            face_y[level + 1][i, pl.ds(EDGE // 2, count + 1), :] = cyl(i)
            zl, zh = czl(i), czh(i)
            face_zl[level + 1][i, rows, :] = zl
            face_zh[level + 1][i, rows, :] = zh
            step = 1 << (level + 1)
            inner_zl[level + 1][i, rows, :] = jnp.where(lanes(zl) < step, 0.0, zl)
            inner_zh[level + 1][i, rows, :] = jnp.where(lanes(zh) >= Z - step, 0.0, zh)
            return carry

        lax.fori_loop(0, n_planes, coarsen, 0, unroll=3)
        face_x[level + 1][n_planes, rows, :] = cx(n_planes)

        def weigh_plane(i, carry, level=level):
            weigh(level + 1, i)
            return carry

        lax.fori_loop(0, n_planes, weigh_plane, 0, unroll=3)

    X, Y = dims(LEVELS)
    cx, cyl, cyh, czl, czh = coarse_faces(LEVELS - 1, HALO[LEVELS - 1], EDGE, Y)
    for x in range(X + 1):
        gather_faces[narrow, x] = cx(x)
    for x in range(X):
        for k, part in enumerate((cyl, cyh, czl, czh)):
            gather_faces[narrow, X + 1 + k * X + x] = part(x)

    def gather(ref, which):
        def copy(d, incoming=False):
            came = lax.rem(narrow + n_narrow - d, n_narrow) if incoming else narrow
            return pltpu.make_async_remote_copy(
                src_ref=ref.at[narrow],
                dst_ref=ref.at[came],
                send_sem=gsend_sem.at[which, d - 1],
                recv_sem=grecv_sem.at[which, d - 1],
                device_id=others[d - 1],
                device_id_type=MESH,
            )

        def start():
            for d in range(1, n_narrow):
                copy(d).start()

        def finish():
            for d in range(1, n_narrow):
                copy(d, incoming=True).wait_recv()

        def drain():
            for d in range(1, n_narrow):
                copy(d).wait_send()

        return start, finish, drain

    face_start, face_finish, face_drain = gather(gather_faces, 0)
    source_start, source_finish, source_drain = gather(gather_source, 1)
    face_start()

    def neighbour_sum(level, e, x, own):
        Y = dims(level)[1]
        p = iterates[level]
        step = 1 << level
        edge = 0 if own else EDGE
        start, rows = PAD - edge, Y + 2 * edge
        at = pl.ds(EDGE - edge, rows)
        i, j = x + HALO[level], x + HX[level]
        here = p[e, j, pl.ds(start, rows), :]
        total = (
            face_x[level][i, at, :] * p[e, j - 1, pl.ds(start, rows), :]
            + face_x[level][i + 1, at, :] * p[e, j + 1, pl.ds(start, rows), :]
        )
        total += face_y[level][i, at, :] * p[e, j, pl.ds(start - 1, rows), :]
        total += face_y[level][i, pl.ds(EDGE - edge + 1, rows), :] * p[
            e, j, pl.ds(start + 1, rows), :
        ]
        total += inner_zl[level][i, at, :] * pltpu.roll(here, step, 1)
        total += inner_zh[level][i, at, :] * pltpu.roll(here, Z - step, 1)
        return here, total

    def sweep(level, e, x, own):
        Y = dims(level)[1]
        edge = 0 if own else EDGE
        here, total = neighbour_sum(level, e, x, own)
        w = weight[level][x + HALO[level], pl.ds(EDGE - edge, Y + 2 * edge), :]
        if e == 0:
            return (1.0 + KEEP) * here + w * total
        start = iterates[level][0, x + HX[level], pl.ds(PAD - edge, Y + 2 * edge), :]
        return (KEEP * here + start) + w * total

    def wide_sweep(level, e, halo):
        X, Y = dims(level)

        def plane(j, carry):
            x = j - halo
            iterates[level][e + 1, x + HX[level], pl.ds(PAD - EDGE, Y + 2 * EDGE), :] = sweep(
                level, e, x, False
            )
            return carry

        lax.fori_loop(0, X + 2 * halo, plane, 0, unroll=3 if X + 2 * halo == 18 else 2)

    finish_first = None
    for level in range(LEVELS):
        X, Y = dims(level)
        if level > 0:
            finish = level_exchange(level, 0, 0, level)
            push()
            finish()
        wide_sweep(level, 0, 1)
        if level == 0:
            finish_first = level_exchange(0, 1, 2, LEVELS)
        h, half, last = HALO[level], Y // 2, level + 1 == LEVELS
        own_rows = pl.ds(EDGE, Y)

        def restrict(x, carry, level=level, Y=Y, h=h, half=half, last=last, own_rows=own_rows):
            both = None
            for k in range(2):
                fine = 2 * x + k
                here, total = neighbour_sum(level, 1, fine, True)
                b = source[0][fine + HX[0], own_rows, :] if level == 0 else source[level][fine]
                left = (b - diag[level][fine + h, own_rows, :] * here) + total
                both = left if both is None else both + left
            tmp[:Y, :] = both
            summed = (
                tmp[pl.ds(0, half, stride=2), :] + tmp[pl.ds(1, half, stride=2), :]
            )
            summed = 0.5 * z_pair(summed, level)
            if last:
                gather_source[narrow, x] = summed
            else:
                source[level + 1][x] = summed
                w = weight[level + 1][x + HALO[level + 1], pl.ds(EDGE, half), :]
                iterates[level + 1][0, x + HX[level + 1], pl.ds(PAD, half), :] = w * summed
            return carry

        if last:
            for x in range(X // 2):
                restrict(x, 0)
        else:
            lax.fori_loop(0, X // 2, restrict, 0, unroll=4)

    source_start()
    push()
    face_finish()
    source_finish()
    X, Y = dims(LEVELS)
    step = 1 << LEVELS
    row = lax.broadcasted_iota(jnp.int32, (Y, Z), 0)
    col = lax.broadcasted_iota(jnp.int32, (Y, Z), 1)
    for n in range(n_narrow):
        for x in range(X):
            fxl, fxh = gather_faces[n, x], gather_faces[n, x + 1]
            fyl, fyh, fzl, fzh = (gather_faces[n, X + 1 + k * X + x] for k in range(4))
            total = ((fxl + fxh) + (fyl + fyh)) + (fzl + fzh)
            w = DAMPING / total
            at = n * X + x
            coef[0, at] = w * fxl
            coef[1, at] = w * fxh
            coef[2, at] = jnp.where(row == 0, 0.0, w * fyl)
            coef[3, at] = jnp.where(row == Y - 1, 0.0, w * fyh)
            coef[4, at] = jnp.where(col < step, 0.0, w * fzl)
            coef[5, at] = jnp.where(col >= Z - step, 0.0, w * fzh)
            coef[6, at] = w * gather_source[n, x]

    zero_plane = jnp.zeros((1, Y, Z), jnp.float32)

    def bottom(k, cur):
        new = KEEP * cur + coef[6]
        new += coef[0] * jnp.concatenate([zero_plane, cur[:-1]], axis=0)
        new += coef[1] * jnp.concatenate([cur[1:], zero_plane], axis=0)
        new += coef[2] * pltpu.roll(cur, 1, 1)
        new += coef[3] * pltpu.roll(cur, Y - 1, 1)
        new += coef[4] * pltpu.roll(cur, step, 2)
        new += coef[5] * pltpu.roll(cur, Z - step, 2)
        return new

    push()
    coef[7] = lax.fori_loop(0, BOTTOM - 1, bottom, coef[6], unroll=15)
    for x in range(X):
        answer[LEVELS][x] = coef[7, narrow * X + x]

    def repeat_rows(e, count):
        tmp[pl.ds(0, count, stride=2), :] = e
        tmp[pl.ds(1, count, stride=2), :] = e
        return tmp[: 2 * count, :]

    for level in reversed(range(1, LEVELS)):
        X, Y = dims(level)
        half = Y // 2

        def raised(x, carry, level=level, Y=Y, half=half):
            e = repeat_rows(answer[level + 1][x // 2], half)
            at = x + HX[level]
            iterates[level][2, at, PAD : PAD + Y, :] = (
                iterates[level][1, at, PAD : PAD + Y, :] + e
            )
            return carry

        lax.fori_loop(0, X, raised, 0, unroll=4)
        finish = level_exchange(level, 2, 2, LEVELS + level)
        push()
        finish()
        out_halo = 1 if level == 1 else 0
        wide_sweep(level, 2, 1 + out_halo)

        def close(j, carry, level=level, out_halo=out_halo):
            if out_halo:
                near_answer[j, pl.ds(PAD - EDGE, dims(level)[1] + 2 * EDGE), :] = sweep(
                    level, 3, j - out_halo, False
                )
            else:
                answer[level][j] = sweep(level, 3, j, True)
            return carry

        lax.fori_loop(0, X + 2 * out_halo, close, 0, unroll=2)

    for x in range(X0):
        iterates[0][2, x + HX[0], PAD : PAD + Y0, :] = iterates[0][1, x + HX[0], PAD : PAD + Y0, :]
    finish_first()
    coarse_rows = pl.ds(PAD - EDGE // 2, Y0 // 2 + EDGE)

    def raise_first(j, carry):
        e = repeat_rows(near_answer[j // 2, coarse_rows, :], Y0 // 2 + EDGE)
        iterates[0][2, j, win0, :] = iterates[0][2, j, win0, :] + e
        return carry

    lax.fori_loop(0, X0 + 2 * HX[0], raise_first, 0, unroll=4)
    wide_sweep(0, 2, 1)

    def close_first(x, carry):
        pressure[x] = sweep(0, 3, x, True)
        return carry

    lax.fori_loop(0, X0, close_first, 0, unroll=4)

    assert len(pushed) == len(FAR)
    pressure_copy = pltpu.make_async_copy(pressure, pressure_ref, local_sem.at[4])
    pressure_copy.start()

    def merge_solved(q, carry):
        merged[q, :SOLVED] = arrived[receive_index[q, 0]]
        return carry

    lax.fori_loop(0, PER_OWNER, merge_solved, 0, unroll=4)
    face_drain()
    source_drain()
    for drain in drains:
        drain()
    pressure_copy.wait()

    def carried_end(k, carry):
        carried_bulk(k).wait_send()
        carried_bulk(k, incoming=True).wait_recv()
        return carry

    lax.fori_loop(1, owners, carried_end, 0)

    def out_copy(g):
        group = pl.ds(g * OUT_GROUP, OUT_GROUP)
        return pltpu.make_async_copy(merged.at[group], migrated_ref.at[group], out_sem.at[g])

    for g in range(PER_OWNER // OUT_GROUP):

        def merge_carried(q, carry):
            merged[q, SOLVED:] = moved[receive_index[q, 0]]
            return carry

        lax.fori_loop(g * OUT_GROUP, (g + 1) * OUT_GROUP, merge_carried, 0, unroll=4)
        out_copy(g).start()

    for g in range(PER_OWNER // OUT_GROUP):
        out_copy(g).wait()


def f32(*shape):
    return pltpu.VMEM(shape, jnp.float32)


def bf16(*shape):
    return pltpu.VMEM(shape, jnp.bfloat16)


def call_solve(n_wide, n_narrow, table, fields):
    per_owner, n_fields, cells = fields.shape
    owners = n_wide * n_narrow
    slots = owners * CAPACITY
    X3, Y3 = dims(LEVELS)
    levels = [(level, *dims(level)) for level in range(LEVELS)]
    faces = [f32(X + 2 * HALO[l], Y + 2 * EDGE, Z) for l, X, Y in levels]
    moves = 2 * LEVELS
    packs = {
        "solved": bf16(slots, SOLVED, cells),
        "carried": bf16(slots, n_fields - SOLVED, cells),
    }
    dma = pltpu.SemaphoreType.DMA
    scratch = [
        pltpu.VMEM(table.shape, jnp.int32),
        bf16(*fields.shape),
        packs["solved"],
        packs["carried"],
        packs["solved"],
        packs["carried"],
        bf16(*fields.shape),
        f32(X0, Y0, Z),
        pltpu.VMEM((CAPACITY, owners, Z), jnp.int32),
        pltpu.VMEM((per_owner, Z), jnp.int32),
        pltpu.SMEM((CAPACITY, owners, Z), jnp.int32),
        pltpu.SMEM((per_owner, Z), jnp.int32),
        f32(64, Z),
        f32(Y0 + 2 * PAD, Z),
        [f32(X0 + 2 * h, Y0 + 2 * PAD, Z) for h in FIELD_HALO],
        bf16(2, HALO_PLANES, Y0, Z),
        bf16(2, HALO_PLANES, Y0, Z),
        bf16(2, 2 * X0, PAD, Z),
        bf16(2, 2 * X0, PAD, Z),
        bf16(4, 2 * CORNER, PAD, Z),
        bf16(4, 2 * CORNER, PAD, Z),
        [f32(4, X + 2 * HX[l], Y + 2 * PAD, Z) for l, X, Y in levels],
        [f32(2, 2, X * ROWS[l] // PAD, PAD, Z) for l, X, Y in levels],
        [f32(2, 2, X * ROWS[l] // PAD, PAD, Z) for l, X, Y in levels],
        [f32(X + 2 * HALO[l] + 1, Y + 2 * EDGE, Z) for l, X, Y in levels],
        [f32(X + 2 * HALO[l], Y + 2 * EDGE + 8, Z) for l, X, Y in levels],
        faces,
        faces,
        faces,
        faces,
        faces,
        faces,
        [f32(X0 + 2 * HX[0], Y0 + 2 * EDGE, Z)] + [f32(X, Y, Z) for l, X, Y in levels[1:]],
        [f32(*dims(level), Z) for level in range(LEVELS + 1)],
        f32(dims(1)[0] + 2, dims(1)[1] + 2 * PAD, Z),
        f32(n_narrow, 5 * X3 + 1, Y3, Z),
        f32(n_narrow, X3, Y3, Z),
        f32(8, n_narrow * X3, Y3, Z),
        dma((moves, 8)),
        dma((moves, 8)),
        dma((2, n_narrow - 1)),
        dma((2, n_narrow - 1)),
        dma((owners,)),
        dma((owners,)),
        dma((owners,)),
        dma((owners,)),
        dma((5,)),
        dma((per_owner // OUT_GROUP,)),
    ]
    anywhere = pl.BlockSpec(memory_space=pl.ANY)
    return pl.pallas_call(
        functools.partial(solve_kernel, n_wide, n_narrow),
        out_shape=(
            jax.ShapeDtypeStruct(fields.shape, fields.dtype),
            jax.ShapeDtypeStruct((X0, Y0, Z), jnp.float32),
        ),
        in_specs=[anywhere, anywhere],
        out_specs=(anywhere, anywhere),
        scratch_shapes=scratch,
        compiler_params=pltpu.CompilerParams(
            collective_id=0, has_side_effects=True, vmem_limit_bytes=min(60, 46 + owners // 8) * 1024 * 1024
        ),
        cost_estimate=pl.CostEstimate(
            flops=200_000_000, bytes_accessed=200_000_000, transcendentals=0
        ),
    )(table, fields)


def hand_over_kernel(migrated_ref, pressure_ref, migrated_out, pressure_out, sem):
    copies = []
    for n, (src, dst) in enumerate(((migrated_ref, migrated_out), (pressure_ref, pressure_out))):
        size = src.shape[0] // PIECES
        for g in range(PIECES):
            piece = pl.ds(g * size, size)
            copies.append(pltpu.make_async_copy(src.at[piece], dst.at[piece], sem.at[n, g]))
    for copy in copies:
        copy.start()
    for copy in copies:
        copy.wait()


def hand_over(migrated, pressure):
    anywhere = pl.BlockSpec(memory_space=pl.ANY)
    return pl.pallas_call(
        hand_over_kernel,
        out_shape=tuple(jax.ShapeDtypeStruct(a.shape, a.dtype) for a in (migrated, pressure)),
        in_specs=[anywhere, anywhere],
        out_specs=(anywhere, anywhere),
        scratch_shapes=[pltpu.SemaphoreType.DMA((2, PIECES))],
        compiler_params=pltpu.CompilerParams(vmem_limit_bytes=1024 * 1024),
    )(migrated, pressure)


def shards(n_wide, n_narrow, target_slot, fields):
    return hand_over(*call_solve(n_wide, n_narrow, target_slot.reshape(-1, Z), fields))


def solution(mesh):
    body = functools.partial(shards, mesh.shape["wide"], mesh.shape["narrow"])
    in_specs = (P(), P(("wide", "narrow"), None, None))
    out_specs = (P(("wide", "narrow"), None, None), P("narrow", "wide", None))
    return jax.shard_map(body, mesh=mesh, in_specs=in_specs, out_specs=out_specs, check_vma=False)
```

```python
import functools

import jax
import jax.numpy as jnp
from jax import lax
from jax.experimental import pallas as pl
from jax.experimental.pallas import tpu as pltpu
from jax.sharding import PartitionSpec as P

PATCH = 16
BYP = 4
BZP = 8
LEVELS = 3
BOTTOM = 16
DAMPING = 0.8
KEEP = 1.0 - DAMPING
SOLVED = 4
CAPACITY = 2
PER_OWNER = 32
X0 = PATCH
Y0 = PATCH * BYP
Z = PATCH * BZP
PAD = 8
EDGE = 4
HX = (2, 3, 2)
ROWS = (2, 4, 2)
CORNER_PLANES = (1, 3, 1)
HALO = (4, 2, 1)
FIELD_HALO = (3, 2, 2, 5)
HALO_PLANES = sum(FIELD_HALO)
CORNER = max(FIELD_HALO)
MESH = pl.DeviceIdType.MESH
FAR = (5, 0, 1, 2, 1, 1, 1, 1, 1, 3)
NEAR = (9, 0, 0, 1, 1, 1, 1, 1, 1, 0)
PIECES = 8
SIDES = tuple((dx, dy) for dx in (-1, 0, 1) for dy in (-1, 0, 1) if dx or dy)


def dims(level):
    return X0 >> level, Y0 >> level


def solve_kernel(
    n_wide,
    n_narrow,
    target_ref,
    fields_ref,
    merged,
    pressure,
    target,
    fields,
    solved,
    carried,
    arrived,
    moved,
    send_index_v,
    receive_index_v,
    send_index,
    receive_index,
    turn,
    tmp,
    grids,
    sent_x,
    got_x,
    sent_y,
    got_y,
    sent_c,
    got_c,
    iterates,
    sent_rows,
    got_rows,
    face_x,
    face_y,
    face_zl,
    face_zh,
    inner_zl,
    inner_zh,
    diag,
    weight,
    source,
    answer,
    near_answer,
    gather_faces,
    gather_source,
    coef,
    send_sem,
    recv_sem,
    gsend_sem,
    grecv_sem,
    carry_send_sem,
    carry_recv_sem,
    solved_send_sem,
    solved_recv_sem,
    local_sem,
):
    wide = lax.axis_index("wide")
    narrow = lax.axis_index("narrow")
    owners = n_wide * n_narrow
    me = wide * n_narrow + narrow
    low = {-1: narrow > 0, 1: narrow < n_narrow - 1, 0: None}
    side_y = {-1: wide > 0, 1: wide < n_wide - 1, 0: None}

    def has(side):
        dx, dy = side
        if dx == 0:
            return side_y[dy]
        if dy == 0:
            return low[dx]
        return jnp.logical_and(low[dx], side_y[dy])

    def peer(side):
        return (wide + side[1], narrow + side[0])

    def back(side):
        return (-side[0], -side[1])

    others = [(wide, lax.rem(narrow + d, n_narrow)) for d in range(1, n_narrow)]

    target_copy = pltpu.make_async_copy(target_ref, target, local_sem.at[0])
    target_copy.start()
    fields_copy = pltpu.make_async_copy(fields_ref, fields, local_sem.at[1])
    fields_copy.start()

    def at_distance(distance):
        owner = jnp.bitwise_xor(me, distance)
        return owner, (owner // n_narrow, lax.rem(owner, n_narrow))

    def partner(k):
        return at_distance(jnp.where(lax.rem(k, 2) == 1, owners // 2 + k // 2, k // 2))

    barrier = pltpu.get_barrier_semaphore()

    def greet(k, carry):
        _, device = partner(k)
        pl.semaphore_signal(barrier, inc=1, device_id=device, device_id_type=MESH)
        return carry

    lax.fori_loop(1, owners, greet, 0)

    target_copy.wait()
    segments = Z // PER_OWNER
    own_row = target[pl.ds(me // segments, 1), :]
    lane_d = lax.broadcasted_iota(jnp.int32, (owners, Z), 1)
    owner_d = lax.broadcasted_iota(jnp.int32, (owners, Z), 0)
    mine = jnp.logical_and(
        lane_d // PER_OWNER == lax.rem(me, segments), own_row // PER_OWNER == owner_d
    )
    place = lax.rem(lane_d, PER_OWNER)
    low_place = jnp.min(jnp.where(mine, place, PER_OWNER - 1), axis=1, keepdims=True)
    high_place = jnp.max(jnp.where(mine, place, 0), axis=1, keepdims=True)
    send_index_v[0] = jnp.broadcast_to(low_place, (owners, Z))
    send_index_v[1] = jnp.broadcast_to(high_place, (owners, Z))
    index_copy = pltpu.make_async_copy(send_index_v, send_index, local_sem.at[2])
    index_copy.start()

    table = target[...]
    t_rows = table.shape[0]
    t_lane = lax.broadcasted_iota(jnp.int32, (t_rows, Z), 1)
    t_owner = lax.broadcasted_iota(jnp.int32, (t_rows, Z), 0) * segments + t_lane // PER_OWNER
    t_place = lax.rem(t_lane, PER_OWNER)
    seen = jnp.where(table // PER_OWNER == me, 1, 0)
    step = 1
    while step < PER_OWNER:
        seen = jnp.maximum(seen, jnp.where(t_place >= step, pltpu.roll(seen, step, 1), 0))
        step *= 2
    rank = jnp.where(t_place >= 1, pltpu.roll(seen, 1, 1), 0)
    slot = t_owner * CAPACITY + rank
    for q in range(PER_OWNER):
        hit = jnp.where(table == me * PER_OWNER + q, slot, 0)
        receive_index_v[q : q + 1, :] = jnp.max(hit, axis=0, keepdims=True)
    slots_q = jnp.max(receive_index_v[...], axis=1, keepdims=True)
    receive_index_v[...] = jnp.broadcast_to(slots_q, (PER_OWNER, Z))
    receive_copy = pltpu.make_async_copy(receive_index_v, receive_index, local_sem.at[3])
    receive_copy.start()

    index_copy.wait()
    fields_copy.wait()
    pl.semaphore_wait(barrier, owners - 1)

    def block(owner):
        return pl.ds(owner * CAPACITY, CAPACITY)

    def bulk(whom, packed, landed, send, recv, k, incoming=False):
        owner, device = whom(k)
        return pltpu.make_async_remote_copy(
            src_ref=packed.at[block(me if incoming else owner)],
            dst_ref=landed.at[block(owner if incoming else me)],
            send_sem=send.at[k],
            recv_sem=recv.at[k],
            device_id=device,
            device_id_type=MESH,
        )

    solved_bulk = functools.partial(bulk, partner, solved, arrived, solved_send_sem, solved_recv_sem)
    carried_bulk = functools.partial(bulk, at_distance, carried, moved, carry_send_sem, carry_recv_sem)

    def pack_solved(k, carry):
        owner, _ = partner(k)
        for r in range(CAPACITY):
            solved[owner * CAPACITY + r] = fields[send_index[r, owner, 0], :SOLVED]
        solved_bulk(k).start()
        return carry

    def pack_carried(k, carry):
        owner, _ = at_distance(k)
        for r in range(CAPACITY):
            carried[owner * CAPACITY + r] = fields[send_index[r, owner, 0], SOLVED:]
        return carry

    lax.fori_loop(1, owners, pack_solved, 0)
    for r in range(CAPACITY):
        patch = fields[send_index[r, me, 0]]
        arrived[me * CAPACITY + r] = patch[:SOLVED]
        moved[me * CAPACITY + r] = patch[SOLVED:]
    lax.fori_loop(1, owners, pack_carried, 0)

    half_way = owners // 2

    def cuts(shares, first, end):
        return [first + (end - first) * sum(shares[:k]) // sum(shares) for k in range(len(shares) + 1)]

    far = cuts(FAR, half_way, owners)
    near = cuts(NEAR, 1, half_way)
    pushed = []

    def begin(k, carry):
        carried_bulk(k).start()
        return carry

    def push():
        turn_now = len(pushed)
        pushed.append(turn_now)
        for bounds in (near, far):
            if bounds[turn_now] < bounds[turn_now + 1]:
                lax.fori_loop(bounds[turn_now], bounds[turn_now + 1], begin, 0)

    push()
    for level in range(LEVELS):
        X, Y = dims(level)
        p = iterates[level]
        hx = HX[level]
        for e in (2,) if level == 0 else (0, 2):

            @pl.when(jnp.logical_not(low[-1]))
            def _(p=p, e=e, Y=Y, hx=hx):
                p[e, :hx] = jnp.zeros((hx, Y + 2 * PAD, Z), jnp.float32)

            @pl.when(jnp.logical_not(low[1]))
            def _(p=p, e=e, X=X, Y=Y, hx=hx):
                p[e, hx + X :] = jnp.zeros((hx, Y + 2 * PAD, Z), jnp.float32)

            @pl.when(jnp.logical_not(side_y[-1]))
            def _(p=p, e=e, X=X, Y=Y, hx=hx):
                p[e, :, :PAD] = jnp.zeros((X + 2 * hx, PAD, Z), jnp.float32)

            @pl.when(jnp.logical_not(side_y[1]))
            def _(p=p, e=e, X=X, Y=Y, hx=hx):
                p[e, :, PAD + Y :] = jnp.zeros((X + 2 * hx, PAD, Z), jnp.float32)

    receive_copy.wait()

    def solved_arrive(k, carry):
        solved_bulk(k, incoming=True).wait_recv()
        return carry

    lax.fori_loop(1, owners, solved_arrive, 0)
    push()

    lane = lax.broadcasted_iota(jnp.int32, (8, Z), 1)
    block_lane = lane // PATCH
    lower_bits = [(block_lane // s) % 2 == 1 for s in (1, 2, 4)]

    def to_grid(step, carry):
        b = step // X0
        i = step % X0
        at = pl.multiple_of(i * 2 * Z, 2 * Z)
        rows = []
        for c in range(BZP):
            both = arrived[receive_index[b * BZP + c, 0], :, pl.ds(at, 2 * Z)].astype(
                jnp.float32
            )
            rows.append(jnp.concatenate([both[:, :Z], both[:, Z:]], axis=0))
        for bit, s in zip(lower_bits, (1, 2, 4)):
            new = list(rows)
            for c in range(BZP):
                if c & s == 0:
                    lower, upper = rows[c], rows[c + s]
                    new[c] = jnp.where(bit, pltpu.roll(upper, PATCH * s, 1), lower)
                    new[c + s] = jnp.where(bit, upper, pltpu.roll(lower, Z - PATCH * s, 1))
            rows = new
        for j in range(8):
            turn[8 * j : 8 * j + 8, :] = rows[j]
        for half in range(2):
            y = pl.multiple_of(b * PATCH + half * 8, 8)
            for f, ref in enumerate(grids):
                values = turn[pl.ds(half * SOLVED + f, 8, stride=8), :]
                ref[i + FIELD_HALO[f], pl.ds(PAD + y, 8), :] = values
        return carry

    lax.fori_loop(0, BYP * X0, to_grid, 0, unroll=8)

    def known(side, values):
        return jnp.where(has(side), values.astype(jnp.float32), 0.0)

    planes = []
    for f, h in enumerate(FIELD_HALO):
        planes += [(f, h, j) for j in range(h)]
    for n, (f, h, j) in enumerate(planes):
        for side, x in ((0, j), (1, X0 - h + j)):
            sent_x[side, n] = grids[f][h + x, PAD : PAD + Y0, :].astype(jnp.bfloat16)
    at_row = lax.broadcasted_iota(jnp.int32, (PAD, Z), 0)

    def end_rows(end, x):
        y = (0, Y0 - PAD)[end]
        u, v, w, r = (
            grids[f][h + x, PAD + y : PAD + y + PAD, :] for f, h in enumerate(FIELD_HALO)
        )
        if end == 0:
            uvw = jnp.where(
                at_row < 2, u, jnp.where(at_row < 5, pltpu.roll(v, 2, 0), pltpu.roll(w, 5, 0))
            )
        else:
            uvw = jnp.where(
                at_row > 5, u, jnp.where(at_row > 2, pltpu.roll(v, 6, 0), pltpu.roll(w, 3, 0))
            )
        return r.astype(jnp.bfloat16), uvw.astype(jnp.bfloat16)

    def keep_rows(end, x, uvw, r):
        y = (0, PAD + Y0)[end]
        u, v, w = (
            (uvw, pltpu.roll(uvw, 2, 0), pltpu.roll(uvw, 5, 0)),
            (uvw, pltpu.roll(uvw, 6, 0), pltpu.roll(uvw, 3, 0)),
        )[end]
        for f, values in enumerate((u, v, w, r)):
            h = FIELD_HALO[f]
            if -h <= x < X0 + h:
                grids[f][h + x, y : y + PAD, :] = values

    for end in range(2):
        for i in range(X0):
            sent_y[end, i], sent_y[end, X0 + i] = end_rows(end, i)
        for j in range(CORNER):
            for side, x in ((0, j), (1, X0 - CORNER + j)):
                (
                    sent_c[2 * side + end, j],
                    sent_c[2 * side + end, CORNER + j],
                ) = end_rows(end, x)

    def field_refs(side):
        dx, dy = side
        if dy == 0:
            return sent_x.at[(dx + 1) // 2], got_x.at[(1 - dx) // 2]
        if dx == 0:
            return sent_y.at[(dy + 1) // 2], got_y.at[(1 - dy) // 2]
        return sent_c.at[dx + 1 + (dy + 1) // 2], got_c.at[1 - dx + (1 - dy) // 2]

    def level_refs(level, e, into):
        X, Y = dims(level)
        p = iterates[level]
        hx = HX[level]

        def refs(side):
            dx, dy = side
            if dx == 0:
                which = into // 2
                return (
                    sent_rows[level].at[which, (dy + 1) // 2],
                    got_rows[level].at[which, (1 - dy) // 2],
                )
            h = hx if dy == 0 else CORNER_PLANES[level]
            src_x, dst_x, n_x = {
                -1: (hx, hx + X, h),
                0: (hx, hx, X),
                1: (hx + X - h, hx - h, h),
            }[dx]
            src_y, dst_y, n_y = {
                -1: (PAD, PAD + Y, PAD),
                0: (PAD, PAD, Y),
                1: (Y, 0, PAD),
            }[dy]
            return (
                p.at[e, pl.ds(src_x, n_x), pl.ds(src_y, n_y)],
                p.at[into, pl.ds(dst_x, n_x), pl.ds(dst_y, n_y)],
            )

        return refs

    def pack_rows(level, e, into):
        X, Y = dims(level)
        p, n = iterates[level], ROWS[level]
        per = PAD // n
        for end, y, first_row in ((0, PAD, 0), (1, Y, PAD - n)):
            for g in range(X // per):
                tile = None
                for k in range(per):
                    rows = p[e, HX[level] + per * g + k, y : y + PAD, :]
                    shift = (n * k - first_row) % PAD
                    rows = pltpu.roll(rows, shift, 0) if shift else rows
                    tile = rows if tile is None else jnp.where(at_row >= n * k, rows, tile)
                sent_rows[level][into // 2, end, g] = tile

    def unpack_rows(level, into):
        X, Y = dims(level)
        p, n = iterates[level], ROWS[level]
        per = PAD // n
        for end, y, first_row in ((0, 0, PAD - n), (1, PAD + Y, 0)):
            for g in range(X // per):
                tile = known((0, 2 * end - 1), got_rows[level][into // 2, end, g])
                for k in range(per):
                    shift = (first_row - n * k) % PAD
                    p[into, HX[level] + per * g + k, y : y + PAD, :] = (
                        pltpu.roll(tile, shift, 0) if shift else tile
                    )

    drains = []

    def exchange(refs, move):
        def copy(side, incoming=False):
            src, dst = refs(back(side) if incoming else side)
            return pltpu.make_async_remote_copy(
                src_ref=src,
                dst_ref=dst,
                send_sem=send_sem.at[move, SIDES.index(side)],
                recv_sem=recv_sem.at[move, SIDES.index(side if incoming else back(side))],
                device_id=peer(side),
                device_id_type=MESH,
            )

        def each(act):
            for side in SIDES:

                @pl.when(has(side))
                def _(side=side):
                    act(side)

        drains.append(lambda: each(lambda side: copy(side).wait_send()))
        return (
            lambda: each(lambda side: copy(side).start()),
            lambda: each(lambda side: copy(side, incoming=True).wait_recv()),
        )

    def level_exchange(level, e, into, move):
        pack_rows(level, e, into)
        start, arrive = exchange(level_refs(level, e, into), move)
        start()

        def finish():
            arrive()
            unpack_rows(level, into)

        return finish

    def lanes(values):
        return lax.broadcasted_iota(jnp.int32, values.shape, 1)

    def z_low(values, step):
        return jnp.where(lanes(values) < step, 0.0, pltpu.roll(values, step, 1))

    def z_high(values, step):
        return jnp.where(lanes(values) >= Z - step, 0.0, pltpu.roll(values, Z - step, 1))

    def keep_inner(level, i, at, zl, zh):
        step = 1 << level
        inner_zl[level][i, at, :] = jnp.where(lanes(zl) < step, 0.0, zl)
        inner_zh[level][i, at, :] = jnp.where(lanes(zh) >= Z - step, 0.0, zh)

    grid_u, grid_v, grid_w, grid_r = grids
    rows0 = Y0 + 2 * EDGE
    win0 = pl.ds(PAD - EDGE, rows0)

    def face(a, b):
        return 2.0 / jnp.maximum(a + b, 0.5)

    def faces(i, row=0, rows=rows0):
        at, start = pl.ds(row, rows), row + PAD - EDGE
        here = grid_r[i + 1, pl.ds(start, rows), :]
        face_x[0][i, at, :] = face(grid_r[i, pl.ds(start, rows), :], here)
        face_y[0][i, at, :] = face(grid_r[i + 1, pl.ds(start - 1, rows), :], here)
        if row + rows == rows0:
            last = PAD + EDGE + Y0
            face_y[0][i, rows0 : rows0 + EDGE, :] = face(
                grid_r[i + 1, last - 1 : last + EDGE - 1, :], grid_r[i + 1, last : last + EDGE, :]
            )
        zl, zh = face(z_low(here, 1), here), face(z_high(here, 1), here)
        face_zl[0][i, at, :] = zl
        face_zh[0][i, at, :] = zh
        keep_inner(0, i, at, zl, zh)

    def inside_rows(level, row, rows):
        Y = dims(level)[1]
        at = lax.broadcasted_iota(jnp.int32, (rows, Z), 0) + row
        return jnp.logical_and(
            jnp.logical_or(side_y[-1], at >= EDGE), jnp.logical_or(side_y[1], at < EDGE + Y)
        )

    def weigh(level, i, row=0, rows=None):
        X, Y = dims(level)
        h, rows = HALO[level], rows or Y + 2 * EDGE
        at = pl.ds(row, rows)
        total = face_x[level][i, at, :] + face_x[level][i + 1, at, :]
        total += face_y[level][i, at, :] + face_y[level][i, pl.ds(row + 1, rows), :]
        total += face_zl[level][i, at, :] + face_zh[level][i, at, :]
        inside = jnp.logical_and(
            jnp.logical_or(low[-1], i >= h), jnp.logical_or(low[1], i < h + X)
        )
        w = jnp.where(jnp.logical_and(inside_rows(level, row, rows), inside), DAMPING / total, 0.0)
        diag[level][i, at, :] = total
        weight[level][i, at, :] = w
        return w

    def first(j, row=0, rows=rows0):
        at, start = pl.ds(row, rows), row + PAD - EDGE
        mid = pl.ds(start, rows)
        w = weigh(0, j + HALO[0] - HX[0], row, rows)
        wz = grid_w[j + FIELD_HALO[2] - HX[0], mid, :]
        u_at, v_at = j + FIELD_HALO[0] - HX[0], j + FIELD_HALO[1] - HX[0]
        du = grid_u[u_at + 1, mid, :] - grid_u[u_at - 1, mid, :]
        dv = grid_v[v_at, pl.ds(start + 1, rows), :] - grid_v[v_at, pl.ds(start - 1, rows), :]
        b = -0.5 * ((du + dv) + (z_high(wz, 1) - z_low(wz, 1)))
        source[0][j, at, :] = b
        iterates[0][0, j, mid, :] = w * b

    def planes_of(act, low_j, high_j, edges_only=False, unroll=2):
        def one(j, carry):
            if edges_only:
                act(j, 0, PAD)
                act(j, rows0 - PAD, PAD)
            else:
                act(j)
            return carry

        lax.fori_loop(low_j, high_j, one, 0, unroll=unroll)

    n_faces, n_first = X0 + 2 * HALO[0], X0 + 2 * HX[0]
    face_from, face_to = HALO[0] + 1, HALO[0] + X0 - 1
    first_from, first_to = HX[0] + 1, HX[0] + X0 - 2
    field_start, field_arrive = exchange(field_refs, 0)
    field_start()
    push()

    def solved_end(k, carry):
        solved_bulk(k).wait_send()
        return carry

    lax.fori_loop(1, owners, solved_end, 0, unroll=False)
    planes_of(faces, face_from, face_to)
    planes_of(first, first_from, first_to)
    field_arrive()

    for n, (f, h, j) in enumerate(planes):
        for dx, x in ((-1, j), (1, h + X0 + j)):
            at = (dx + 1) // 2
            grids[f][x, PAD : PAD + Y0, :] = known((dx, 0), got_x[at, n])
    for end, dy in ((0, -1), (1, 1)):
        for i in range(X0):
            r, uvw = (known((0, dy), got_y[end, k * X0 + i]) for k in range(2))
            keep_rows(end, i, uvw, r)
        for j in range(CORNER):
            for side, dx, x in ((0, -1, j - CORNER), (1, 1, X0 + j)):
                r, uvw = (
                    known((dx, dy), got_c[2 * side + end, k * CORNER + j]) for k in range(2)
                )
                keep_rows(end, x, uvw, r)

    push()
    planes_of(faces, 0, face_from)
    planes_of(faces, face_to, n_faces)
    planes_of(faces, face_from, face_to, edges_only=True)
    face_x[0][n_faces] = face(grid_r[n_faces, win0, :], grid_r[n_faces + 1, win0, :])
    planes_of(first, 0, first_from, unroll=3)
    planes_of(first, first_to, n_first, unroll=4)
    planes_of(first, first_from, first_to, edges_only=True)

    def z_bit(values, level):
        return (lanes(values) // (1 << level)) % 2 == 1

    def z_pair(values, level):
        step = 1 << level
        return values + jnp.where(
            z_bit(values, level), pltpu.roll(values, step, 1), pltpu.roll(values, Z - step, 1)
        )

    def z_even(values, level):
        return jnp.where(z_bit(values, level), pltpu.roll(values, 1 << level, 1), values)

    def z_odd(values, level):
        return jnp.where(z_bit(values, level), values, pltpu.roll(values, Z - (1 << level), 1))

    def coarse_faces(level, base, start, count, more=0):
        even = pl.ds(start, count, stride=2)
        even_y = pl.ds(start, count + more, stride=2)
        odd = pl.ds(start + 1, count, stride=2)
        after = pl.ds(start + 2, count, stride=2)
        fx, fy, zl, zh = (f[level] for f in (face_x, face_y, face_zl, face_zh))

        def cx(x):
            i = base + 2 * x
            return 0.25 * z_pair(fx[i, even, :] + fx[i, odd, :], level)

        def cy(x, rows):
            i = base + 2 * x
            return 0.25 * z_pair(fy[i, rows, :] + fy[i + 1, rows, :], level)

        def four(f, x):
            i = base + 2 * x
            return 0.25 * (
                (f[i, even, :] + f[i, odd, :]) + (f[i + 1, even, :] + f[i + 1, odd, :])
            )

        return (
            cx,
            lambda x: cy(x, even_y),
            lambda x: cy(x, after),
            lambda x: z_even(four(zl, x), level),
            lambda x: z_odd(four(zh, x), level),
        )

    for level in range(LEVELS - 1):
        X, Y = dims(level + 1)
        count = Y + EDGE
        n_planes = X + 2 * HALO[level + 1]
        cx, cyl, _, czl, czh = coarse_faces(level, 0, 0, count, more=1)
        rows = pl.ds(EDGE // 2, count)

        def coarsen(i, carry, level=level, rows=rows, count=count, cx=cx, cyl=cyl, czl=czl, czh=czh):
            face_x[level + 1][i, rows, :] = cx(i)
            face_y[level + 1][i, pl.ds(EDGE // 2, count + 1), :] = cyl(i)
            zl, zh = czl(i), czh(i)
            face_zl[level + 1][i, rows, :] = zl
            face_zh[level + 1][i, rows, :] = zh
            step = 1 << (level + 1)
            inner_zl[level + 1][i, rows, :] = jnp.where(lanes(zl) < step, 0.0, zl)
            inner_zh[level + 1][i, rows, :] = jnp.where(lanes(zh) >= Z - step, 0.0, zh)
            return carry

        lax.fori_loop(0, n_planes, coarsen, 0, unroll=3)
        face_x[level + 1][n_planes, rows, :] = cx(n_planes)

        def weigh_plane(i, carry, level=level):
            weigh(level + 1, i)
            return carry

        lax.fori_loop(0, n_planes, weigh_plane, 0, unroll=3)

    X, Y = dims(LEVELS)
    cx, cyl, cyh, czl, czh = coarse_faces(LEVELS - 1, HALO[LEVELS - 1], EDGE, Y)
    for x in range(X + 1):
        gather_faces[narrow, x] = cx(x)
    for x in range(X):
        for k, part in enumerate((cyl, cyh, czl, czh)):
            gather_faces[narrow, X + 1 + k * X + x] = part(x)

    def gather(ref, which):
        def copy(d, incoming=False):
            came = lax.rem(narrow + n_narrow - d, n_narrow) if incoming else narrow
            return pltpu.make_async_remote_copy(
                src_ref=ref.at[narrow],
                dst_ref=ref.at[came],
                send_sem=gsend_sem.at[which, d - 1],
                recv_sem=grecv_sem.at[which, d - 1],
                device_id=others[d - 1],
                device_id_type=MESH,
            )

        def start():
            for d in range(1, n_narrow):
                copy(d).start()

        def finish():
            for d in range(1, n_narrow):
                copy(d, incoming=True).wait_recv()

        def drain():
            for d in range(1, n_narrow):
                copy(d).wait_send()

        return start, finish, drain

    face_start, face_finish, face_drain = gather(gather_faces, 0)
    source_start, source_finish, source_drain = gather(gather_source, 1)
    face_start()

    def neighbour_sum(level, e, x, own):
        Y = dims(level)[1]
        p = iterates[level]
        step = 1 << level
        edge = 0 if own else EDGE
        start, rows = PAD - edge, Y + 2 * edge
        at = pl.ds(EDGE - edge, rows)
        i, j = x + HALO[level], x + HX[level]
        here = p[e, j, pl.ds(start, rows), :]
        total = (
            face_x[level][i, at, :] * p[e, j - 1, pl.ds(start, rows), :]
            + face_x[level][i + 1, at, :] * p[e, j + 1, pl.ds(start, rows), :]
        )
        total += face_y[level][i, at, :] * p[e, j, pl.ds(start - 1, rows), :]
        total += face_y[level][i, pl.ds(EDGE - edge + 1, rows), :] * p[
            e, j, pl.ds(start + 1, rows), :
        ]
        total += inner_zl[level][i, at, :] * pltpu.roll(here, step, 1)
        total += inner_zh[level][i, at, :] * pltpu.roll(here, Z - step, 1)
        return here, total

    def sweep(level, e, x, own):
        Y = dims(level)[1]
        edge = 0 if own else EDGE
        here, total = neighbour_sum(level, e, x, own)
        w = weight[level][x + HALO[level], pl.ds(EDGE - edge, Y + 2 * edge), :]
        if e == 0:
            return (1.0 + KEEP) * here + w * total
        start = iterates[level][0, x + HX[level], pl.ds(PAD - edge, Y + 2 * edge), :]
        return (KEEP * here + start) + w * total

    def wide_sweep(level, e, halo):
        X, Y = dims(level)

        def plane(j, carry):
            x = j - halo
            iterates[level][e + 1, x + HX[level], pl.ds(PAD - EDGE, Y + 2 * EDGE), :] = sweep(
                level, e, x, False
            )
            return carry

        lax.fori_loop(0, X + 2 * halo, plane, 0, unroll=3 if X + 2 * halo == 18 else 2)

    finish_first = None
    for level in range(LEVELS):
        X, Y = dims(level)
        if level > 0:
            finish = level_exchange(level, 0, 0, level)
            push()
            finish()
        wide_sweep(level, 0, 1)
        if level == 0:
            finish_first = level_exchange(0, 1, 2, LEVELS)
        h, half, last = HALO[level], Y // 2, level + 1 == LEVELS
        own_rows = pl.ds(EDGE, Y)

        def restrict(x, carry, level=level, Y=Y, h=h, half=half, last=last, own_rows=own_rows):
            both = None
            for k in range(2):
                fine = 2 * x + k
                here, total = neighbour_sum(level, 1, fine, True)
                b = source[0][fine + HX[0], own_rows, :] if level == 0 else source[level][fine]
                left = (b - diag[level][fine + h, own_rows, :] * here) + total
                both = left if both is None else both + left
            tmp[:Y, :] = both
            summed = (
                tmp[pl.ds(0, half, stride=2), :] + tmp[pl.ds(1, half, stride=2), :]
            )
            summed = 0.5 * z_pair(summed, level)
            if last:
                gather_source[narrow, x] = summed
            else:
                source[level + 1][x] = summed
                w = weight[level + 1][x + HALO[level + 1], pl.ds(EDGE, half), :]
                iterates[level + 1][0, x + HX[level + 1], pl.ds(PAD, half), :] = w * summed
            return carry

        if last:
            for x in range(X // 2):
                restrict(x, 0)
        else:
            lax.fori_loop(0, X // 2, restrict, 0, unroll=4)

    source_start()
    push()
    face_finish()
    source_finish()
    X, Y = dims(LEVELS)
    step = 1 << LEVELS
    row = lax.broadcasted_iota(jnp.int32, (Y, Z), 0)
    col = lax.broadcasted_iota(jnp.int32, (Y, Z), 1)
    for n in range(n_narrow):
        for x in range(X):
            fxl, fxh = gather_faces[n, x], gather_faces[n, x + 1]
            fyl, fyh, fzl, fzh = (gather_faces[n, X + 1 + k * X + x] for k in range(4))
            total = ((fxl + fxh) + (fyl + fyh)) + (fzl + fzh)
            w = DAMPING / total
            at = n * X + x
            coef[0, at] = w * fxl
            coef[1, at] = w * fxh
            coef[2, at] = jnp.where(row == 0, 0.0, w * fyl)
            coef[3, at] = jnp.where(row == Y - 1, 0.0, w * fyh)
            coef[4, at] = jnp.where(col < step, 0.0, w * fzl)
            coef[5, at] = jnp.where(col >= Z - step, 0.0, w * fzh)
            coef[6, at] = w * gather_source[n, x]

    zero_plane = jnp.zeros((1, Y, Z), jnp.float32)

    def bottom(k, cur):
        new = KEEP * cur + coef[6]
        new += coef[0] * jnp.concatenate([zero_plane, cur[:-1]], axis=0)
        new += coef[1] * jnp.concatenate([cur[1:], zero_plane], axis=0)
        new += coef[2] * pltpu.roll(cur, 1, 1)
        new += coef[3] * pltpu.roll(cur, Y - 1, 1)
        new += coef[4] * pltpu.roll(cur, step, 2)
        new += coef[5] * pltpu.roll(cur, Z - step, 2)
        return new

    push()
    coef[7] = lax.fori_loop(0, BOTTOM - 1, bottom, coef[6], unroll=15)
    for x in range(X):
        answer[LEVELS][x] = coef[7, narrow * X + x]

    def repeat_rows(e, count):
        tmp[pl.ds(0, count, stride=2), :] = e
        tmp[pl.ds(1, count, stride=2), :] = e
        return tmp[: 2 * count, :]

    for level in reversed(range(1, LEVELS)):
        X, Y = dims(level)
        half = Y // 2

        def raised(x, carry, level=level, Y=Y, half=half):
            e = repeat_rows(answer[level + 1][x // 2], half)
            at = x + HX[level]
            iterates[level][2, at, PAD : PAD + Y, :] = (
                iterates[level][1, at, PAD : PAD + Y, :] + e
            )
            return carry

        lax.fori_loop(0, X, raised, 0, unroll=4)
        finish = level_exchange(level, 2, 2, LEVELS + level)
        push()
        finish()
        out_halo = 1 if level == 1 else 0
        wide_sweep(level, 2, 1 + out_halo)

        def close(j, carry, level=level, out_halo=out_halo):
            if out_halo:
                near_answer[j, pl.ds(PAD - EDGE, dims(level)[1] + 2 * EDGE), :] = sweep(
                    level, 3, j - out_halo, False
                )
            else:
                answer[level][j] = sweep(level, 3, j, True)
            return carry

        lax.fori_loop(0, X + 2 * out_halo, close, 0, unroll=2)

    for x in range(X0):
        iterates[0][2, x + HX[0], PAD : PAD + Y0, :] = iterates[0][1, x + HX[0], PAD : PAD + Y0, :]
    finish_first()
    coarse_rows = pl.ds(PAD - EDGE // 2, Y0 // 2 + EDGE)

    def raise_first(j, carry):
        e = repeat_rows(near_answer[j // 2, coarse_rows, :], Y0 // 2 + EDGE)
        iterates[0][2, j, win0, :] = iterates[0][2, j, win0, :] + e
        return carry

    lax.fori_loop(0, X0 + 2 * HX[0], raise_first, 0, unroll=4)
    wide_sweep(0, 2, 1)

    def close_first(x, carry):
        pressure[x] = sweep(0, 3, x, True)
        return carry

    lax.fori_loop(0, X0, close_first, 0, unroll=4)

    assert len(pushed) == len(FAR)

    def merge_solved(q, carry):
        merged[q, :SOLVED] = arrived[receive_index[q, 0]]
        return carry

    lax.fori_loop(0, PER_OWNER, merge_solved, 0, unroll=4)
    face_drain()
    source_drain()
    for drain in drains:
        drain()

    def carried_end(k, carry):
        carried_bulk(k).wait_send()
        carried_bulk(k, incoming=True).wait_recv()
        return carry

    lax.fori_loop(1, owners, carried_end, 0)

    def merge_carried(q, carry):
        merged[q, SOLVED:] = moved[receive_index[q, 0]]
        return carry

    lax.fori_loop(0, PER_OWNER, merge_carried, 0, unroll=8)


def f32(*shape):
    return pltpu.VMEM(shape, jnp.float32)


def bf16(*shape):
    return pltpu.VMEM(shape, jnp.bfloat16)


def call_solve(n_wide, n_narrow, table, fields):
    per_owner, n_fields, cells = fields.shape
    owners = n_wide * n_narrow
    slots = owners * CAPACITY
    X3, Y3 = dims(LEVELS)
    levels = [(level, *dims(level)) for level in range(LEVELS)]
    faces = [f32(X + 2 * HALO[l], Y + 2 * EDGE, Z) for l, X, Y in levels]
    moves = 2 * LEVELS
    packs = {
        "solved": bf16(slots, SOLVED, cells),
        "carried": bf16(slots, n_fields - SOLVED, cells),
    }
    dma = pltpu.SemaphoreType.DMA
    scratch = [
        pltpu.VMEM(table.shape, jnp.int32),
        bf16(*fields.shape),
        packs["solved"],
        packs["carried"],
        packs["solved"],
        packs["carried"],
        pltpu.VMEM((CAPACITY, owners, Z), jnp.int32),
        pltpu.VMEM((per_owner, Z), jnp.int32),
        pltpu.SMEM((CAPACITY, owners, Z), jnp.int32),
        pltpu.SMEM((per_owner, Z), jnp.int32),
        f32(64, Z),
        f32(Y0 + 2 * PAD, Z),
        [f32(X0 + 2 * h, Y0 + 2 * PAD, Z) for h in FIELD_HALO],
        bf16(2, HALO_PLANES, Y0, Z),
        bf16(2, HALO_PLANES, Y0, Z),
        bf16(2, 2 * X0, PAD, Z),
        bf16(2, 2 * X0, PAD, Z),
        bf16(4, 2 * CORNER, PAD, Z),
        bf16(4, 2 * CORNER, PAD, Z),
        [f32(4, X + 2 * HX[l], Y + 2 * PAD, Z) for l, X, Y in levels],
        [f32(2, 2, X * ROWS[l] // PAD, PAD, Z) for l, X, Y in levels],
        [f32(2, 2, X * ROWS[l] // PAD, PAD, Z) for l, X, Y in levels],
        [f32(X + 2 * HALO[l] + 1, Y + 2 * EDGE, Z) for l, X, Y in levels],
        [f32(X + 2 * HALO[l], Y + 2 * EDGE + 8, Z) for l, X, Y in levels],
        faces,
        faces,
        faces,
        faces,
        faces,
        faces,
        [f32(X0 + 2 * HX[0], Y0 + 2 * EDGE, Z)] + [f32(X, Y, Z) for l, X, Y in levels[1:]],
        [f32(*dims(level), Z) for level in range(LEVELS + 1)],
        f32(dims(1)[0] + 2, dims(1)[1] + 2 * PAD, Z),
        f32(n_narrow, 5 * X3 + 1, Y3, Z),
        f32(n_narrow, X3, Y3, Z),
        f32(8, n_narrow * X3, Y3, Z),
        dma((moves, 8)),
        dma((moves, 8)),
        dma((2, n_narrow - 1)),
        dma((2, n_narrow - 1)),
        dma((owners,)),
        dma((owners,)),
        dma((owners,)),
        dma((owners,)),
        dma((4,)),
    ]
    anywhere = pl.BlockSpec(memory_space=pl.ANY)
    return pl.pallas_call(
        functools.partial(solve_kernel, n_wide, n_narrow),
        out_shape=(
            jax.ShapeDtypeStruct(fields.shape, fields.dtype),
            jax.ShapeDtypeStruct((X0, Y0, Z), jnp.float32),
        ),
        in_specs=[anywhere, anywhere],
        out_specs=(pl.BlockSpec(memory_space=pltpu.VMEM),) * 2,
        scratch_shapes=scratch,
        compiler_params=pltpu.CompilerParams(
            collective_id=0, has_side_effects=True, vmem_limit_bytes=min(60, 46 + owners // 8) * 1024 * 1024
        ),
        cost_estimate=pl.CostEstimate(
            flops=200_000_000, bytes_accessed=200_000_000, transcendentals=0
        ),
    )(table, fields)


def hand_over_kernel(migrated_ref, pressure_ref, migrated_out, pressure_out, sem):
    copies = []
    for n, (src, dst) in enumerate(((migrated_ref, migrated_out), (pressure_ref, pressure_out))):
        size = src.shape[0] // PIECES
        for g in range(PIECES):
            piece = pl.ds(g * size, size)
            copies.append(pltpu.make_async_copy(src.at[piece], dst.at[piece], sem.at[n, g]))
    for copy in copies:
        copy.start()
    for copy in copies:
        copy.wait()


def hand_over(migrated, pressure):
    anywhere = pl.BlockSpec(memory_space=pl.ANY)
    return pl.pallas_call(
        hand_over_kernel,
        out_shape=tuple(jax.ShapeDtypeStruct(a.shape, a.dtype) for a in (migrated, pressure)),
        in_specs=[anywhere, anywhere],
        out_specs=(anywhere, anywhere),
        scratch_shapes=[pltpu.SemaphoreType.DMA((2, PIECES))],
        compiler_params=pltpu.CompilerParams(vmem_limit_bytes=1024 * 1024),
    )(migrated, pressure)


def shards(n_wide, n_narrow, target_slot, fields):
    return hand_over(*call_solve(n_wide, n_narrow, target_slot.reshape(-1, Z), fields))


def solution(mesh):
    body = functools.partial(shards, mesh.shape["wide"], mesh.shape["narrow"])
    in_specs = (P(), P(("wide", "narrow"), None, None))
    out_specs = (P(("wide", "narrow"), None, None), P("narrow", "wide", None))
    return jax.shard_map(body, mesh=mesh, in_specs=in_specs, out_specs=out_specs, check_vma=False)
```

```python
import functools

import jax
import jax.numpy as jnp
from jax import lax
from jax.experimental import pallas as pl
from jax.experimental.pallas import tpu as pltpu
from jax.sharding import PartitionSpec as P

PATCH = 16
BYP = 4
BZP = 8
LEVELS = 3
BOTTOM = 16
DAMPING = 0.8
KEEP = 1.0 - DAMPING
SOLVED = 4
CAPACITY = 2
PER_OWNER = 32
X0 = PATCH
Y0 = PATCH * BYP
Z = PATCH * BZP
PAD = 8
EDGE = 4
HX = (2, 3, 2)
ROWS = (2, 4, 2)
CORNER_PLANES = (1, 3, 1)
HALO = (4, 2, 1)
FIELD_HALO = (3, 2, 2, 5)
HALO_PLANES = sum(FIELD_HALO)
CORNER = max(FIELD_HALO)
MESH = pl.DeviceIdType.MESH
FAR = (5, 0, 1, 2, 1, 1, 1, 1, 1, 3)
NEAR = (9, 0, 0, 1, 1, 1, 1, 1, 1, 0)
PIECES = 8
SIDES = tuple((dx, dy) for dx in (-1, 0, 1) for dy in (-1, 0, 1) if dx or dy)


def dims(level):
    return X0 >> level, Y0 >> level


def solve_kernel(
    n_wide,
    n_narrow,
    target_ref,
    fields_ref,
    merged,
    pressure,
    target,
    fields,
    solved,
    carried,
    arrived,
    moved,
    send_index_v,
    receive_index_v,
    send_index,
    receive_index,
    turn,
    tmp,
    grids,
    sent_x,
    got_x,
    sent_y,
    got_y,
    sent_c,
    got_c,
    iterates,
    sent_rows,
    got_rows,
    face_x,
    face_y,
    face_zl,
    face_zh,
    inner_zl,
    inner_zh,
    diag,
    weight,
    source,
    answer,
    near_answer,
    gather_faces,
    gather_source,
    coef,
    send_sem,
    recv_sem,
    gsend_sem,
    grecv_sem,
    carry_send_sem,
    carry_recv_sem,
    solved_send_sem,
    solved_recv_sem,
    local_sem,
):
    wide = lax.axis_index("wide")
    narrow = lax.axis_index("narrow")
    owners = n_wide * n_narrow
    me = wide * n_narrow + narrow
    low = {-1: narrow > 0, 1: narrow < n_narrow - 1, 0: None}
    side_y = {-1: wide > 0, 1: wide < n_wide - 1, 0: None}

    def has(side):
        dx, dy = side
        if dx == 0:
            return side_y[dy]
        if dy == 0:
            return low[dx]
        return jnp.logical_and(low[dx], side_y[dy])

    def peer(side):
        return (wide + side[1], narrow + side[0])

    def back(side):
        return (-side[0], -side[1])

    others = [(wide, lax.rem(narrow + d, n_narrow)) for d in range(1, n_narrow)]

    target_copy = pltpu.make_async_copy(target_ref, target, local_sem.at[0])
    target_copy.start()
    fields_copy = pltpu.make_async_copy(fields_ref, fields, local_sem.at[1])
    fields_copy.start()

    def at_distance(distance):
        owner = jnp.bitwise_xor(me, distance)
        return owner, (owner // n_narrow, lax.rem(owner, n_narrow))

    def partner(k):
        return at_distance(jnp.where(lax.rem(k, 2) == 1, owners // 2 + k // 2, k // 2))

    barrier = pltpu.get_barrier_semaphore()

    def greet(k, carry):
        _, device = partner(k)
        pl.semaphore_signal(barrier, inc=1, device_id=device, device_id_type=MESH)
        return carry

    lax.fori_loop(1, owners, greet, 0)

    target_copy.wait()
    segments = Z // PER_OWNER
    own_row = target[pl.ds(me // segments, 1), :]
    lane_d = lax.broadcasted_iota(jnp.int32, (owners, Z), 1)
    owner_d = lax.broadcasted_iota(jnp.int32, (owners, Z), 0)
    mine = jnp.logical_and(
        lane_d // PER_OWNER == lax.rem(me, segments), own_row // PER_OWNER == owner_d
    )
    place = lax.rem(lane_d, PER_OWNER)
    low_place = jnp.min(jnp.where(mine, place, PER_OWNER - 1), axis=1, keepdims=True)
    high_place = jnp.max(jnp.where(mine, place, 0), axis=1, keepdims=True)
    send_index_v[0] = jnp.broadcast_to(low_place, (owners, Z))
    send_index_v[1] = jnp.broadcast_to(high_place, (owners, Z))
    index_copy = pltpu.make_async_copy(send_index_v, send_index, local_sem.at[2])
    index_copy.start()

    index_copy.wait()
    fields_copy.wait()
    pl.semaphore_wait(barrier, owners - 1)

    def block(owner):
        return pl.ds(owner * CAPACITY, CAPACITY)

    def bulk(whom, packed, landed, send, recv, k, incoming=False):
        owner, device = whom(k)
        return pltpu.make_async_remote_copy(
            src_ref=packed.at[block(me if incoming else owner)],
            dst_ref=landed.at[block(owner if incoming else me)],
            send_sem=send.at[k],
            recv_sem=recv.at[k],
            device_id=device,
            device_id_type=MESH,
        )

    solved_bulk = functools.partial(bulk, partner, solved, arrived, solved_send_sem, solved_recv_sem)
    carried_bulk = functools.partial(bulk, at_distance, carried, moved, carry_send_sem, carry_recv_sem)

    def pack_solved(k, carry):
        owner, _ = partner(k)
        for r in range(CAPACITY):
            solved[owner * CAPACITY + r] = fields[send_index[r, owner, 0], :SOLVED]
        solved_bulk(k).start()
        return carry

    def pack_carried(k, carry):
        owner, _ = at_distance(k)
        for r in range(CAPACITY):
            carried[owner * CAPACITY + r] = fields[send_index[r, owner, 0], SOLVED:]
        return carry

    lax.fori_loop(1, owners, pack_solved, 0)
    for r in range(CAPACITY):
        patch = fields[send_index[r, me, 0]]
        arrived[me * CAPACITY + r] = patch[:SOLVED]
        moved[me * CAPACITY + r] = patch[SOLVED:]
    lax.fori_loop(1, owners, pack_carried, 0)

    table = target[...]
    t_rows = table.shape[0]
    t_lane = lax.broadcasted_iota(jnp.int32, (t_rows, Z), 1)
    t_owner = lax.broadcasted_iota(jnp.int32, (t_rows, Z), 0) * segments + t_lane // PER_OWNER
    t_place = lax.rem(t_lane, PER_OWNER)
    seen = jnp.where(table // PER_OWNER == me, 1, 0)
    step = 1
    while step < PER_OWNER:
        seen = jnp.maximum(seen, jnp.where(t_place >= step, pltpu.roll(seen, step, 1), 0))
        step *= 2
    rank = jnp.where(t_place >= 1, pltpu.roll(seen, 1, 1), 0)
    slot = t_owner * CAPACITY + rank
    for q in range(PER_OWNER):
        hit = jnp.where(table == me * PER_OWNER + q, slot, 0)
        receive_index_v[q : q + 1, :] = jnp.max(hit, axis=0, keepdims=True)
    slots_q = jnp.max(receive_index_v[...], axis=1, keepdims=True)
    receive_index_v[...] = jnp.broadcast_to(slots_q, (PER_OWNER, Z))
    receive_copy = pltpu.make_async_copy(receive_index_v, receive_index, local_sem.at[3])
    receive_copy.start()

    half_way = owners // 2

    def cuts(shares, first, end):
        return [first + (end - first) * sum(shares[:k]) // sum(shares) for k in range(len(shares) + 1)]

    far = cuts(FAR, half_way, owners)
    near = cuts(NEAR, 1, half_way)
    pushed = []

    def begin(k, carry):
        carried_bulk(k).start()
        return carry

    def push():
        turn_now = len(pushed)
        pushed.append(turn_now)
        for bounds in (near, far):
            if bounds[turn_now] < bounds[turn_now + 1]:
                lax.fori_loop(bounds[turn_now], bounds[turn_now + 1], begin, 0)

    push()
    for level in range(LEVELS):
        X, Y = dims(level)
        p = iterates[level]
        hx = HX[level]
        for e in (2,) if level == 0 else (0, 2):

            @pl.when(jnp.logical_not(low[-1]))
            def _(p=p, e=e, Y=Y, hx=hx):
                p[e, :hx] = jnp.zeros((hx, Y + 2 * PAD, Z), jnp.float32)

            @pl.when(jnp.logical_not(low[1]))
            def _(p=p, e=e, X=X, Y=Y, hx=hx):
                p[e, hx + X :] = jnp.zeros((hx, Y + 2 * PAD, Z), jnp.float32)

            @pl.when(jnp.logical_not(side_y[-1]))
            def _(p=p, e=e, X=X, Y=Y, hx=hx):
                p[e, :, :PAD] = jnp.zeros((X + 2 * hx, PAD, Z), jnp.float32)

            @pl.when(jnp.logical_not(side_y[1]))
            def _(p=p, e=e, X=X, Y=Y, hx=hx):
                p[e, :, PAD + Y :] = jnp.zeros((X + 2 * hx, PAD, Z), jnp.float32)

    receive_copy.wait()

    def solved_arrive(k, carry):
        solved_bulk(k, incoming=True).wait_recv()
        return carry

    lax.fori_loop(1, owners, solved_arrive, 0)
    push()

    lane = lax.broadcasted_iota(jnp.int32, (8, Z), 1)
    block_lane = lane // PATCH
    lower_bits = [(block_lane // s) % 2 == 1 for s in (1, 2, 4)]

    def to_grid(step, carry):
        b = step // X0
        i = step % X0
        at = pl.multiple_of(i * 2 * Z, 2 * Z)
        rows = []
        for c in range(BZP):
            both = arrived[receive_index[b * BZP + c, 0], :, pl.ds(at, 2 * Z)].astype(
                jnp.float32
            )
            rows.append(jnp.concatenate([both[:, :Z], both[:, Z:]], axis=0))
        for bit, s in zip(lower_bits, (1, 2, 4)):
            new = list(rows)
            for c in range(BZP):
                if c & s == 0:
                    lower, upper = rows[c], rows[c + s]
                    new[c] = jnp.where(bit, pltpu.roll(upper, PATCH * s, 1), lower)
                    new[c + s] = jnp.where(bit, upper, pltpu.roll(lower, Z - PATCH * s, 1))
            rows = new
        for j in range(8):
            turn[8 * j : 8 * j + 8, :] = rows[j]
        for half in range(2):
            y = pl.multiple_of(b * PATCH + half * 8, 8)
            for f, ref in enumerate(grids):
                values = turn[pl.ds(half * SOLVED + f, 8, stride=8), :]
                ref[i + FIELD_HALO[f], pl.ds(PAD + y, 8), :] = values
        return carry

    lax.fori_loop(0, BYP * X0, to_grid, 0, unroll=8)

    def known(side, values):
        return jnp.where(has(side), values.astype(jnp.float32), 0.0)

    planes = []
    for f, h in enumerate(FIELD_HALO):
        planes += [(f, h, j) for j in range(h)]
    for n, (f, h, j) in enumerate(planes):
        for side, x in ((0, j), (1, X0 - h + j)):
            sent_x[side, n] = grids[f][h + x, PAD : PAD + Y0, :].astype(jnp.bfloat16)
    at_row = lax.broadcasted_iota(jnp.int32, (PAD, Z), 0)

    def end_rows(end, x):
        y = (0, Y0 - PAD)[end]
        u, v, w, r = (
            grids[f][h + x, PAD + y : PAD + y + PAD, :] for f, h in enumerate(FIELD_HALO)
        )
        if end == 0:
            uvw = jnp.where(
                at_row < 2, u, jnp.where(at_row < 5, pltpu.roll(v, 2, 0), pltpu.roll(w, 5, 0))
            )
        else:
            uvw = jnp.where(
                at_row > 5, u, jnp.where(at_row > 2, pltpu.roll(v, 6, 0), pltpu.roll(w, 3, 0))
            )
        return r.astype(jnp.bfloat16), uvw.astype(jnp.bfloat16)

    def keep_rows(end, x, uvw, r):
        y = (0, PAD + Y0)[end]
        u, v, w = (
            (uvw, pltpu.roll(uvw, 2, 0), pltpu.roll(uvw, 5, 0)),
            (uvw, pltpu.roll(uvw, 6, 0), pltpu.roll(uvw, 3, 0)),
        )[end]
        for f, values in enumerate((u, v, w, r)):
            h = FIELD_HALO[f]
            if -h <= x < X0 + h:
                grids[f][h + x, y : y + PAD, :] = values

    for end in range(2):
        for i in range(X0):
            sent_y[end, i], sent_y[end, X0 + i] = end_rows(end, i)
        for j in range(CORNER):
            for side, x in ((0, j), (1, X0 - CORNER + j)):
                (
                    sent_c[2 * side + end, j],
                    sent_c[2 * side + end, CORNER + j],
                ) = end_rows(end, x)

    def field_refs(side):
        dx, dy = side
        if dy == 0:
            return sent_x.at[(dx + 1) // 2], got_x.at[(1 - dx) // 2]
        if dx == 0:
            return sent_y.at[(dy + 1) // 2], got_y.at[(1 - dy) // 2]
        return sent_c.at[dx + 1 + (dy + 1) // 2], got_c.at[1 - dx + (1 - dy) // 2]

    def level_refs(level, e, into):
        X, Y = dims(level)
        p = iterates[level]
        hx = HX[level]

        def refs(side):
            dx, dy = side
            if dx == 0:
                which = into // 2
                return (
                    sent_rows[level].at[which, (dy + 1) // 2],
                    got_rows[level].at[which, (1 - dy) // 2],
                )
            h = hx if dy == 0 else CORNER_PLANES[level]
            src_x, dst_x, n_x = {
                -1: (hx, hx + X, h),
                0: (hx, hx, X),
                1: (hx + X - h, hx - h, h),
            }[dx]
            src_y, dst_y, n_y = {
                -1: (PAD, PAD + Y, PAD),
                0: (PAD, PAD, Y),
                1: (Y, 0, PAD),
            }[dy]
            return (
                p.at[e, pl.ds(src_x, n_x), pl.ds(src_y, n_y)],
                p.at[into, pl.ds(dst_x, n_x), pl.ds(dst_y, n_y)],
            )

        return refs

    def pack_rows(level, e, into):
        X, Y = dims(level)
        p, n = iterates[level], ROWS[level]
        per = PAD // n
        for end, y, first_row in ((0, PAD, 0), (1, Y, PAD - n)):
            for g in range(X // per):
                tile = None
                for k in range(per):
                    rows = p[e, HX[level] + per * g + k, y : y + PAD, :]
                    shift = (n * k - first_row) % PAD
                    rows = pltpu.roll(rows, shift, 0) if shift else rows
                    tile = rows if tile is None else jnp.where(at_row >= n * k, rows, tile)
                sent_rows[level][into // 2, end, g] = tile

    def unpack_rows(level, into):
        X, Y = dims(level)
        p, n = iterates[level], ROWS[level]
        per = PAD // n
        for end, y, first_row in ((0, 0, PAD - n), (1, PAD + Y, 0)):
            for g in range(X // per):
                tile = known((0, 2 * end - 1), got_rows[level][into // 2, end, g])
                for k in range(per):
                    shift = (first_row - n * k) % PAD
                    p[into, HX[level] + per * g + k, y : y + PAD, :] = (
                        pltpu.roll(tile, shift, 0) if shift else tile
                    )

    drains = []

    def exchange(refs, move):
        def copy(side, incoming=False):
            src, dst = refs(back(side) if incoming else side)
            return pltpu.make_async_remote_copy(
                src_ref=src,
                dst_ref=dst,
                send_sem=send_sem.at[move, SIDES.index(side)],
                recv_sem=recv_sem.at[move, SIDES.index(side if incoming else back(side))],
                device_id=peer(side),
                device_id_type=MESH,
            )

        def each(act):
            for side in SIDES:

                @pl.when(has(side))
                def _(side=side):
                    act(side)

        drains.append(lambda: each(lambda side: copy(side).wait_send()))
        return (
            lambda: each(lambda side: copy(side).start()),
            lambda: each(lambda side: copy(side, incoming=True).wait_recv()),
        )

    def level_exchange(level, e, into, move):
        pack_rows(level, e, into)
        start, arrive = exchange(level_refs(level, e, into), move)
        start()

        def finish():
            arrive()
            unpack_rows(level, into)

        return finish

    def lanes(values):
        return lax.broadcasted_iota(jnp.int32, values.shape, 1)

    def z_low(values, step):
        return jnp.where(lanes(values) < step, 0.0, pltpu.roll(values, step, 1))

    def z_high(values, step):
        return jnp.where(lanes(values) >= Z - step, 0.0, pltpu.roll(values, Z - step, 1))

    def keep_inner(level, i, at, zl, zh):
        step = 1 << level
        inner_zl[level][i, at, :] = jnp.where(lanes(zl) < step, 0.0, zl)
        inner_zh[level][i, at, :] = jnp.where(lanes(zh) >= Z - step, 0.0, zh)

    grid_u, grid_v, grid_w, grid_r = grids
    rows0 = Y0 + 2 * EDGE
    win0 = pl.ds(PAD - EDGE, rows0)

    def face(a, b):
        return 2.0 / jnp.maximum(a + b, 0.5)

    def faces(i, row=0, rows=rows0):
        at, start = pl.ds(row, rows), row + PAD - EDGE
        here = grid_r[i + 1, pl.ds(start, rows), :]
        face_x[0][i, at, :] = face(grid_r[i, pl.ds(start, rows), :], here)
        face_y[0][i, at, :] = face(grid_r[i + 1, pl.ds(start - 1, rows), :], here)
        if row + rows == rows0:
            last = PAD + EDGE + Y0
            face_y[0][i, rows0 : rows0 + EDGE, :] = face(
                grid_r[i + 1, last - 1 : last + EDGE - 1, :], grid_r[i + 1, last : last + EDGE, :]
            )
        zl, zh = face(z_low(here, 1), here), face(z_high(here, 1), here)
        face_zl[0][i, at, :] = zl
        face_zh[0][i, at, :] = zh
        keep_inner(0, i, at, zl, zh)

    def inside_rows(level, row, rows):
        Y = dims(level)[1]
        at = lax.broadcasted_iota(jnp.int32, (rows, Z), 0) + row
        return jnp.logical_and(
            jnp.logical_or(side_y[-1], at >= EDGE), jnp.logical_or(side_y[1], at < EDGE + Y)
        )

    def weigh(level, i, row=0, rows=None):
        X, Y = dims(level)
        h, rows = HALO[level], rows or Y + 2 * EDGE
        at = pl.ds(row, rows)
        total = face_x[level][i, at, :] + face_x[level][i + 1, at, :]
        total += face_y[level][i, at, :] + face_y[level][i, pl.ds(row + 1, rows), :]
        total += face_zl[level][i, at, :] + face_zh[level][i, at, :]
        inside = jnp.logical_and(
            jnp.logical_or(low[-1], i >= h), jnp.logical_or(low[1], i < h + X)
        )
        w = jnp.where(jnp.logical_and(inside_rows(level, row, rows), inside), DAMPING / total, 0.0)
        diag[level][i, at, :] = total
        weight[level][i, at, :] = w
        return w

    def first(j, row=0, rows=rows0):
        at, start = pl.ds(row, rows), row + PAD - EDGE
        mid = pl.ds(start, rows)
        w = weigh(0, j + HALO[0] - HX[0], row, rows)
        wz = grid_w[j + FIELD_HALO[2] - HX[0], mid, :]
        u_at, v_at = j + FIELD_HALO[0] - HX[0], j + FIELD_HALO[1] - HX[0]
        du = grid_u[u_at + 1, mid, :] - grid_u[u_at - 1, mid, :]
        dv = grid_v[v_at, pl.ds(start + 1, rows), :] - grid_v[v_at, pl.ds(start - 1, rows), :]
        b = -0.5 * ((du + dv) + (z_high(wz, 1) - z_low(wz, 1)))
        source[0][j, at, :] = b
        iterates[0][0, j, mid, :] = w * b

    def planes_of(act, low_j, high_j, edges_only=False, unroll=2):
        def one(j, carry):
            if edges_only:
                act(j, 0, PAD)
                act(j, rows0 - PAD, PAD)
            else:
                act(j)
            return carry

        lax.fori_loop(low_j, high_j, one, 0, unroll=unroll)

    n_faces, n_first = X0 + 2 * HALO[0], X0 + 2 * HX[0]
    face_from, face_to = HALO[0] + 1, HALO[0] + X0 - 1
    first_from, first_to = HX[0] + 1, HX[0] + X0 - 2
    field_start, field_arrive = exchange(field_refs, 0)
    field_start()
    push()

    def solved_end(k, carry):
        solved_bulk(k).wait_send()
        return carry

    lax.fori_loop(1, owners, solved_end, 0, unroll=False)
    planes_of(faces, face_from, face_to)
    planes_of(first, first_from, first_to)
    field_arrive()

    for n, (f, h, j) in enumerate(planes):
        for dx, x in ((-1, j), (1, h + X0 + j)):
            at = (dx + 1) // 2
            grids[f][x, PAD : PAD + Y0, :] = known((dx, 0), got_x[at, n])
    for end, dy in ((0, -1), (1, 1)):
        for i in range(X0):
            r, uvw = (known((0, dy), got_y[end, k * X0 + i]) for k in range(2))
            keep_rows(end, i, uvw, r)
        for j in range(CORNER):
            for side, dx, x in ((0, -1, j - CORNER), (1, 1, X0 + j)):
                r, uvw = (
                    known((dx, dy), got_c[2 * side + end, k * CORNER + j]) for k in range(2)
                )
                keep_rows(end, x, uvw, r)

    push()
    planes_of(faces, 0, face_from)
    planes_of(faces, face_to, n_faces)
    planes_of(faces, face_from, face_to, edges_only=True)
    face_x[0][n_faces] = face(grid_r[n_faces, win0, :], grid_r[n_faces + 1, win0, :])
    planes_of(first, 0, first_from, unroll=3)
    planes_of(first, first_to, n_first, unroll=4)
    planes_of(first, first_from, first_to, edges_only=True)

    def z_bit(values, level):
        return (lanes(values) // (1 << level)) % 2 == 1

    def z_pair(values, level):
        step = 1 << level
        return values + jnp.where(
            z_bit(values, level), pltpu.roll(values, step, 1), pltpu.roll(values, Z - step, 1)
        )

    def z_even(values, level):
        return jnp.where(z_bit(values, level), pltpu.roll(values, 1 << level, 1), values)

    def z_odd(values, level):
        return jnp.where(z_bit(values, level), values, pltpu.roll(values, Z - (1 << level), 1))

    def coarse_faces(level, base, start, count, more=0):
        even = pl.ds(start, count, stride=2)
        even_y = pl.ds(start, count + more, stride=2)
        odd = pl.ds(start + 1, count, stride=2)
        after = pl.ds(start + 2, count, stride=2)
        fx, fy, zl, zh = (f[level] for f in (face_x, face_y, face_zl, face_zh))

        def cx(x):
            i = base + 2 * x
            return 0.25 * z_pair(fx[i, even, :] + fx[i, odd, :], level)

        def cy(x, rows):
            i = base + 2 * x
            return 0.25 * z_pair(fy[i, rows, :] + fy[i + 1, rows, :], level)

        def four(f, x):
            i = base + 2 * x
            return 0.25 * (
                (f[i, even, :] + f[i, odd, :]) + (f[i + 1, even, :] + f[i + 1, odd, :])
            )

        return (
            cx,
            lambda x: cy(x, even_y),
            lambda x: cy(x, after),
            lambda x: z_even(four(zl, x), level),
            lambda x: z_odd(four(zh, x), level),
        )

    for level in range(LEVELS - 1):
        X, Y = dims(level + 1)
        count = Y + EDGE
        n_planes = X + 2 * HALO[level + 1]
        cx, cyl, _, czl, czh = coarse_faces(level, 0, 0, count, more=1)
        rows = pl.ds(EDGE // 2, count)

        def coarsen(i, carry, level=level, rows=rows, count=count, cx=cx, cyl=cyl, czl=czl, czh=czh):
            face_x[level + 1][i, rows, :] = cx(i)
            face_y[level + 1][i, pl.ds(EDGE // 2, count + 1), :] = cyl(i)
            zl, zh = czl(i), czh(i)
            face_zl[level + 1][i, rows, :] = zl
            face_zh[level + 1][i, rows, :] = zh
            step = 1 << (level + 1)
            inner_zl[level + 1][i, rows, :] = jnp.where(lanes(zl) < step, 0.0, zl)
            inner_zh[level + 1][i, rows, :] = jnp.where(lanes(zh) >= Z - step, 0.0, zh)
            return carry

        lax.fori_loop(0, n_planes, coarsen, 0, unroll=3)
        face_x[level + 1][n_planes, rows, :] = cx(n_planes)

        def weigh_plane(i, carry, level=level):
            weigh(level + 1, i)
            return carry

        lax.fori_loop(0, n_planes, weigh_plane, 0, unroll=3)

    X, Y = dims(LEVELS)
    cx, cyl, cyh, czl, czh = coarse_faces(LEVELS - 1, HALO[LEVELS - 1], EDGE, Y)
    for x in range(X + 1):
        gather_faces[narrow, x] = cx(x)
    for x in range(X):
        for k, part in enumerate((cyl, cyh, czl, czh)):
            gather_faces[narrow, X + 1 + k * X + x] = part(x)

    def gather(ref, which):
        def copy(d, incoming=False):
            came = lax.rem(narrow + n_narrow - d, n_narrow) if incoming else narrow
            return pltpu.make_async_remote_copy(
                src_ref=ref.at[narrow],
                dst_ref=ref.at[came],
                send_sem=gsend_sem.at[which, d - 1],
                recv_sem=grecv_sem.at[which, d - 1],
                device_id=others[d - 1],
                device_id_type=MESH,
            )

        def start():
            for d in range(1, n_narrow):
                copy(d).start()

        def finish():
            for d in range(1, n_narrow):
                copy(d, incoming=True).wait_recv()

        def drain():
            for d in range(1, n_narrow):
                copy(d).wait_send()

        return start, finish, drain

    face_start, face_finish, face_drain = gather(gather_faces, 0)
    source_start, source_finish, source_drain = gather(gather_source, 1)
    face_start()

    def neighbour_sum(level, e, x, own):
        Y = dims(level)[1]
        p = iterates[level]
        step = 1 << level
        edge = 0 if own else EDGE
        start, rows = PAD - edge, Y + 2 * edge
        at = pl.ds(EDGE - edge, rows)
        i, j = x + HALO[level], x + HX[level]
        here = p[e, j, pl.ds(start, rows), :]
        total = (
            face_x[level][i, at, :] * p[e, j - 1, pl.ds(start, rows), :]
            + face_x[level][i + 1, at, :] * p[e, j + 1, pl.ds(start, rows), :]
        )
        total += face_y[level][i, at, :] * p[e, j, pl.ds(start - 1, rows), :]
        total += face_y[level][i, pl.ds(EDGE - edge + 1, rows), :] * p[
            e, j, pl.ds(start + 1, rows), :
        ]
        total += inner_zl[level][i, at, :] * pltpu.roll(here, step, 1)
        total += inner_zh[level][i, at, :] * pltpu.roll(here, Z - step, 1)
        return here, total

    def sweep(level, e, x, own):
        Y = dims(level)[1]
        edge = 0 if own else EDGE
        here, total = neighbour_sum(level, e, x, own)
        w = weight[level][x + HALO[level], pl.ds(EDGE - edge, Y + 2 * edge), :]
        if e == 0:
            return (1.0 + KEEP) * here + w * total
        start = iterates[level][0, x + HX[level], pl.ds(PAD - edge, Y + 2 * edge), :]
        return (KEEP * here + start) + w * total

    def wide_sweep(level, e, halo):
        X, Y = dims(level)

        def plane(j, carry):
            x = j - halo
            iterates[level][e + 1, x + HX[level], pl.ds(PAD - EDGE, Y + 2 * EDGE), :] = sweep(
                level, e, x, False
            )
            return carry

        lax.fori_loop(0, X + 2 * halo, plane, 0, unroll=3 if X + 2 * halo == 18 else 2)

    finish_first = None
    for level in range(LEVELS):
        X, Y = dims(level)
        if level > 0:
            finish = level_exchange(level, 0, 0, level)
            push()
            finish()
        wide_sweep(level, 0, 1)
        if level == 0:
            finish_first = level_exchange(0, 1, 2, LEVELS)
        h, half, last = HALO[level], Y // 2, level + 1 == LEVELS
        own_rows = pl.ds(EDGE, Y)

        def restrict(x, carry, level=level, Y=Y, h=h, half=half, last=last, own_rows=own_rows):
            both = None
            for k in range(2):
                fine = 2 * x + k
                here, total = neighbour_sum(level, 1, fine, True)
                b = source[0][fine + HX[0], own_rows, :] if level == 0 else source[level][fine]
                left = (b - diag[level][fine + h, own_rows, :] * here) + total
                both = left if both is None else both + left
            tmp[:Y, :] = both
            summed = (
                tmp[pl.ds(0, half, stride=2), :] + tmp[pl.ds(1, half, stride=2), :]
            )
            summed = 0.5 * z_pair(summed, level)
            if last:
                gather_source[narrow, x] = summed
            else:
                source[level + 1][x] = summed
                w = weight[level + 1][x + HALO[level + 1], pl.ds(EDGE, half), :]
                iterates[level + 1][0, x + HX[level + 1], pl.ds(PAD, half), :] = w * summed
            return carry

        if last:
            for x in range(X // 2):
                restrict(x, 0)
        else:
            lax.fori_loop(0, X // 2, restrict, 0, unroll=4)

    source_start()
    push()
    face_finish()
    source_finish()
    X, Y = dims(LEVELS)
    step = 1 << LEVELS
    row = lax.broadcasted_iota(jnp.int32, (Y, Z), 0)
    col = lax.broadcasted_iota(jnp.int32, (Y, Z), 1)
    for n in range(n_narrow):
        for x in range(X):
            fxl, fxh = gather_faces[n, x], gather_faces[n, x + 1]
            fyl, fyh, fzl, fzh = (gather_faces[n, X + 1 + k * X + x] for k in range(4))
            total = ((fxl + fxh) + (fyl + fyh)) + (fzl + fzh)
            w = DAMPING / total
            at = n * X + x
            coef[0, at] = w * fxl
            coef[1, at] = w * fxh
            coef[2, at] = jnp.where(row == 0, 0.0, w * fyl)
            coef[3, at] = jnp.where(row == Y - 1, 0.0, w * fyh)
            coef[4, at] = jnp.where(col < step, 0.0, w * fzl)
            coef[5, at] = jnp.where(col >= Z - step, 0.0, w * fzh)
            coef[6, at] = w * gather_source[n, x]

    zero_plane = jnp.zeros((1, Y, Z), jnp.float32)

    def bottom(k, cur):
        new = KEEP * cur + coef[6]
        new += coef[0] * jnp.concatenate([zero_plane, cur[:-1]], axis=0)
        new += coef[1] * jnp.concatenate([cur[1:], zero_plane], axis=0)
        new += coef[2] * pltpu.roll(cur, 1, 1)
        new += coef[3] * pltpu.roll(cur, Y - 1, 1)
        new += coef[4] * pltpu.roll(cur, step, 2)
        new += coef[5] * pltpu.roll(cur, Z - step, 2)
        return new

    push()
    coef[7] = lax.fori_loop(0, BOTTOM - 1, bottom, coef[6], unroll=15)
    for x in range(X):
        answer[LEVELS][x] = coef[7, narrow * X + x]

    def repeat_rows(e, count):
        tmp[pl.ds(0, count, stride=2), :] = e
        tmp[pl.ds(1, count, stride=2), :] = e
        return tmp[: 2 * count, :]

    for level in reversed(range(1, LEVELS)):
        X, Y = dims(level)
        half = Y // 2

        def raised(x, carry, level=level, Y=Y, half=half):
            e = repeat_rows(answer[level + 1][x // 2], half)
            at = x + HX[level]
            iterates[level][2, at, PAD : PAD + Y, :] = (
                iterates[level][1, at, PAD : PAD + Y, :] + e
            )
            return carry

        lax.fori_loop(0, X, raised, 0, unroll=4)
        finish = level_exchange(level, 2, 2, LEVELS + level)
        push()
        finish()
        out_halo = 1 if level == 1 else 0
        wide_sweep(level, 2, 1 + out_halo)

        def close(j, carry, level=level, out_halo=out_halo):
            if out_halo:
                near_answer[j, pl.ds(PAD - EDGE, dims(level)[1] + 2 * EDGE), :] = sweep(
                    level, 3, j - out_halo, False
                )
            else:
                answer[level][j] = sweep(level, 3, j, True)
            return carry

        lax.fori_loop(0, X + 2 * out_halo, close, 0, unroll=2)

    for x in range(X0):
        iterates[0][2, x + HX[0], PAD : PAD + Y0, :] = iterates[0][1, x + HX[0], PAD : PAD + Y0, :]
    finish_first()
    coarse_rows = pl.ds(PAD - EDGE // 2, Y0 // 2 + EDGE)

    def raise_first(j, carry):
        e = repeat_rows(near_answer[j // 2, coarse_rows, :], Y0 // 2 + EDGE)
        iterates[0][2, j, win0, :] = iterates[0][2, j, win0, :] + e
        return carry

    lax.fori_loop(0, X0 + 2 * HX[0], raise_first, 0, unroll=4)
    wide_sweep(0, 2, 1)

    def close_first(x, carry):
        pressure[x] = sweep(0, 3, x, True)
        return carry

    lax.fori_loop(0, X0, close_first, 0, unroll=4)

    assert len(pushed) == len(FAR)

    def merge_solved(q, carry):
        merged[q, :SOLVED] = arrived[receive_index[q, 0]]
        return carry

    lax.fori_loop(0, PER_OWNER, merge_solved, 0, unroll=4)
    face_drain()
    source_drain()
    for drain in drains:
        drain()

    def carried_end(k, carry):
        carried_bulk(k).wait_send()
        carried_bulk(k, incoming=True).wait_recv()
        return carry

    lax.fori_loop(1, owners, carried_end, 0)

    def merge_carried(q, carry):
        merged[q, SOLVED:] = moved[receive_index[q, 0]]
        return carry

    lax.fori_loop(0, PER_OWNER, merge_carried, 0, unroll=8)


def f32(*shape):
    return pltpu.VMEM(shape, jnp.float32)


def bf16(*shape):
    return pltpu.VMEM(shape, jnp.bfloat16)


def call_solve(n_wide, n_narrow, table, fields):
    per_owner, n_fields, cells = fields.shape
    owners = n_wide * n_narrow
    slots = owners * CAPACITY
    X3, Y3 = dims(LEVELS)
    levels = [(level, *dims(level)) for level in range(LEVELS)]
    faces = [f32(X + 2 * HALO[l], Y + 2 * EDGE, Z) for l, X, Y in levels]
    moves = 2 * LEVELS
    packs = {
        "solved": bf16(slots, SOLVED, cells),
        "carried": bf16(slots, n_fields - SOLVED, cells),
    }
    dma = pltpu.SemaphoreType.DMA
    scratch = [
        pltpu.VMEM(table.shape, jnp.int32),
        bf16(*fields.shape),
        packs["solved"],
        packs["carried"],
        packs["solved"],
        packs["carried"],
        pltpu.VMEM((CAPACITY, owners, Z), jnp.int32),
        pltpu.VMEM((per_owner, Z), jnp.int32),
        pltpu.SMEM((CAPACITY, owners, Z), jnp.int32),
        pltpu.SMEM((per_owner, Z), jnp.int32),
        f32(64, Z),
        f32(Y0 + 2 * PAD, Z),
        [f32(X0 + 2 * h, Y0 + 2 * PAD, Z) for h in FIELD_HALO],
        bf16(2, HALO_PLANES, Y0, Z),
        bf16(2, HALO_PLANES, Y0, Z),
        bf16(2, 2 * X0, PAD, Z),
        bf16(2, 2 * X0, PAD, Z),
        bf16(4, 2 * CORNER, PAD, Z),
        bf16(4, 2 * CORNER, PAD, Z),
        [f32(4, X + 2 * HX[l], Y + 2 * PAD, Z) for l, X, Y in levels],
        [f32(2, 2, X * ROWS[l] // PAD, PAD, Z) for l, X, Y in levels],
        [f32(2, 2, X * ROWS[l] // PAD, PAD, Z) for l, X, Y in levels],
        [f32(X + 2 * HALO[l] + 1, Y + 2 * EDGE, Z) for l, X, Y in levels],
        [f32(X + 2 * HALO[l], Y + 2 * EDGE + 8, Z) for l, X, Y in levels],
        faces,
        faces,
        faces,
        faces,
        faces,
        faces,
        [f32(X0 + 2 * HX[0], Y0 + 2 * EDGE, Z)] + [f32(X, Y, Z) for l, X, Y in levels[1:]],
        [f32(*dims(level), Z) for level in range(LEVELS + 1)],
        f32(dims(1)[0] + 2, dims(1)[1] + 2 * PAD, Z),
        f32(n_narrow, 5 * X3 + 1, Y3, Z),
        f32(n_narrow, X3, Y3, Z),
        f32(8, n_narrow * X3, Y3, Z),
        dma((moves, 8)),
        dma((moves, 8)),
        dma((2, n_narrow - 1)),
        dma((2, n_narrow - 1)),
        dma((owners,)),
        dma((owners,)),
        dma((owners,)),
        dma((owners,)),
        dma((4,)),
    ]
    anywhere = pl.BlockSpec(memory_space=pl.ANY)
    return pl.pallas_call(
        functools.partial(solve_kernel, n_wide, n_narrow),
        out_shape=(
            jax.ShapeDtypeStruct(fields.shape, fields.dtype),
            jax.ShapeDtypeStruct((X0, Y0, Z), jnp.float32),
        ),
        in_specs=[anywhere, anywhere],
        out_specs=(pl.BlockSpec(memory_space=pltpu.VMEM),) * 2,
        scratch_shapes=scratch,
        compiler_params=pltpu.CompilerParams(
            collective_id=0, has_side_effects=True, vmem_limit_bytes=min(60, 46 + owners // 8) * 1024 * 1024
        ),
        cost_estimate=pl.CostEstimate(
            flops=200_000_000, bytes_accessed=200_000_000, transcendentals=0
        ),
    )(table, fields)


def hand_over_kernel(migrated_ref, pressure_ref, migrated_out, pressure_out, sem):
    copies = []
    for n, (src, dst) in enumerate(((migrated_ref, migrated_out), (pressure_ref, pressure_out))):
        size = src.shape[0] // PIECES
        for g in range(PIECES):
            piece = pl.ds(g * size, size)
            copies.append(pltpu.make_async_copy(src.at[piece], dst.at[piece], sem.at[n, g]))
    for copy in copies:
        copy.start()
    for copy in copies:
        copy.wait()


def hand_over(migrated, pressure):
    anywhere = pl.BlockSpec(memory_space=pl.ANY)
    return pl.pallas_call(
        hand_over_kernel,
        out_shape=tuple(jax.ShapeDtypeStruct(a.shape, a.dtype) for a in (migrated, pressure)),
        in_specs=[anywhere, anywhere],
        out_specs=(anywhere, anywhere),
        scratch_shapes=[pltpu.SemaphoreType.DMA((2, PIECES))],
        compiler_params=pltpu.CompilerParams(vmem_limit_bytes=1024 * 1024),
    )(migrated, pressure)


def shards(n_wide, n_narrow, target_slot, fields):
    return hand_over(*call_solve(n_wide, n_narrow, target_slot.reshape(-1, Z), fields))


def solution(mesh):
    body = functools.partial(shards, mesh.shape["wide"], mesh.shape["narrow"])
    in_specs = (P(), P(("wide", "narrow"), None, None))
    out_specs = (P(("wide", "narrow"), None, None), P("narrow", "wide", None))
    return jax.shard_map(body, mesh=mesh, in_specs=in_specs, out_specs=out_specs, check_vma=False)
```

```python
import functools

import jax
import jax.numpy as jnp
from jax import lax
from jax.experimental import pallas as pl
from jax.experimental.pallas import tpu as pltpu
from jax.sharding import PartitionSpec as P

PATCH = 16
BYP = 4
BZP = 8
LEVELS = 3
BOTTOM = 16
DAMPING = 0.8
KEEP = 1.0 - DAMPING
SOLVED = 4
CAPACITY = 2
PER_OWNER = 32
X0 = PATCH
Y0 = PATCH * BYP
Z = PATCH * BZP
PAD = 8
EDGE = 4
HX = (2, 3, 2)
ROWS = (2, 4, 2)
CORNER_PLANES = (1, 3, 1)
HALO = (4, 2, 1)
FIELD_HALO = (3, 2, 2, 5)
HALO_PLANES = sum(FIELD_HALO)
CORNER = max(FIELD_HALO)
MESH = pl.DeviceIdType.MESH
FAR = (5, 0, 1, 2, 1, 1, 1, 1, 1, 3)
NEAR = (9, 0, 1, 0, 1, 1, 1, 1, 1, 0)
PIECES = 8
SIDES = tuple((dx, dy) for dx in (-1, 0, 1) for dy in (-1, 0, 1) if dx or dy)


def dims(level):
    return X0 >> level, Y0 >> level


def solve_kernel(
    n_wide,
    n_narrow,
    target_ref,
    fields_ref,
    merged,
    pressure,
    target,
    fields,
    solved,
    carried,
    arrived,
    moved,
    send_index_v,
    receive_index_v,
    send_index,
    receive_index,
    turn,
    tmp,
    grids,
    sent_x,
    got_x,
    sent_y,
    got_y,
    sent_c,
    got_c,
    iterates,
    sent_rows,
    got_rows,
    face_x,
    face_y,
    face_zl,
    face_zh,
    inner_zl,
    inner_zh,
    diag,
    weight,
    source,
    answer,
    near_answer,
    gather_faces,
    gather_source,
    coef,
    send_sem,
    recv_sem,
    gsend_sem,
    grecv_sem,
    carry_send_sem,
    carry_recv_sem,
    solved_send_sem,
    solved_recv_sem,
    local_sem,
):
    wide = lax.axis_index("wide")
    narrow = lax.axis_index("narrow")
    owners = n_wide * n_narrow
    me = wide * n_narrow + narrow
    low = {-1: narrow > 0, 1: narrow < n_narrow - 1, 0: None}
    side_y = {-1: wide > 0, 1: wide < n_wide - 1, 0: None}

    def has(side):
        dx, dy = side
        if dx == 0:
            return side_y[dy]
        if dy == 0:
            return low[dx]
        return jnp.logical_and(low[dx], side_y[dy])

    def peer(side):
        return (wide + side[1], narrow + side[0])

    def back(side):
        return (-side[0], -side[1])

    others = [(wide, lax.rem(narrow + d, n_narrow)) for d in range(1, n_narrow)]

    target_copy = pltpu.make_async_copy(target_ref, target, local_sem.at[0])
    target_copy.start()
    fields_copy = pltpu.make_async_copy(fields_ref, fields, local_sem.at[1])
    fields_copy.start()

    def at_distance(distance):
        owner = jnp.bitwise_xor(me, distance)
        return owner, (owner // n_narrow, lax.rem(owner, n_narrow))

    def partner(k):
        return at_distance(jnp.where(lax.rem(k, 2) == 1, owners // 2 + k // 2, k // 2))

    barrier = pltpu.get_barrier_semaphore()

    def greet(k, carry):
        _, device = partner(k)
        pl.semaphore_signal(barrier, inc=1, device_id=device, device_id_type=MESH)
        return carry

    lax.fori_loop(1, owners, greet, 0)

    target_copy.wait()
    segments = Z // PER_OWNER
    own_row = target[pl.ds(me // segments, 1), :]
    lane_d = lax.broadcasted_iota(jnp.int32, (owners, Z), 1)
    owner_d = lax.broadcasted_iota(jnp.int32, (owners, Z), 0)
    mine = jnp.logical_and(
        lane_d // PER_OWNER == lax.rem(me, segments), own_row // PER_OWNER == owner_d
    )
    place = lax.rem(lane_d, PER_OWNER)
    low_place = jnp.min(jnp.where(mine, place, PER_OWNER - 1), axis=1, keepdims=True)
    high_place = jnp.max(jnp.where(mine, place, 0), axis=1, keepdims=True)
    send_index_v[0] = jnp.broadcast_to(low_place, (owners, Z))
    send_index_v[1] = jnp.broadcast_to(high_place, (owners, Z))
    index_copy = pltpu.make_async_copy(send_index_v, send_index, local_sem.at[2])
    index_copy.start()

    table = target[...]
    t_rows = table.shape[0]
    t_lane = lax.broadcasted_iota(jnp.int32, (t_rows, Z), 1)
    t_owner = lax.broadcasted_iota(jnp.int32, (t_rows, Z), 0) * segments + t_lane // PER_OWNER
    t_place = lax.rem(t_lane, PER_OWNER)
    seen = jnp.where(table // PER_OWNER == me, 1, 0)
    step = 1
    while step < PER_OWNER:
        seen = jnp.maximum(seen, jnp.where(t_place >= step, pltpu.roll(seen, step, 1), 0))
        step *= 2
    rank = jnp.where(t_place >= 1, pltpu.roll(seen, 1, 1), 0)
    slot = t_owner * CAPACITY + rank
    for q in range(PER_OWNER):
        hit = jnp.where(table == me * PER_OWNER + q, slot, 0)
        receive_index_v[q : q + 1, :] = jnp.max(hit, axis=0, keepdims=True)
    slots_q = jnp.max(receive_index_v[...], axis=1, keepdims=True)
    receive_index_v[...] = jnp.broadcast_to(slots_q, (PER_OWNER, Z))
    receive_copy = pltpu.make_async_copy(receive_index_v, receive_index, local_sem.at[3])
    receive_copy.start()

    index_copy.wait()
    fields_copy.wait()
    pl.semaphore_wait(barrier, owners - 1)

    def block(owner):
        return pl.ds(owner * CAPACITY, CAPACITY)

    def bulk(whom, packed, landed, send, recv, k, incoming=False):
        owner, device = whom(k)
        return pltpu.make_async_remote_copy(
            src_ref=packed.at[block(me if incoming else owner)],
            dst_ref=landed.at[block(owner if incoming else me)],
            send_sem=send.at[k],
            recv_sem=recv.at[k],
            device_id=device,
            device_id_type=MESH,
        )

    solved_bulk = functools.partial(bulk, partner, solved, arrived, solved_send_sem, solved_recv_sem)
    carried_bulk = functools.partial(bulk, at_distance, carried, moved, carry_send_sem, carry_recv_sem)

    def pack_solved(k, carry):
        owner, _ = partner(k)
        for r in range(CAPACITY):
            solved[owner * CAPACITY + r] = fields[send_index[r, owner, 0], :SOLVED]
        solved_bulk(k).start()
        return carry

    def pack_carried(k, carry):
        owner, _ = at_distance(k)
        for r in range(CAPACITY):
            carried[owner * CAPACITY + r] = fields[send_index[r, owner, 0], SOLVED:]
        return carry

    lax.fori_loop(1, owners, pack_solved, 0)
    for r in range(CAPACITY):
        patch = fields[send_index[r, me, 0]]
        arrived[me * CAPACITY + r] = patch[:SOLVED]
        moved[me * CAPACITY + r] = patch[SOLVED:]
    lax.fori_loop(1, owners, pack_carried, 0)

    half_way = owners // 2

    def cuts(shares, first, end):
        return [first + (end - first) * sum(shares[:k]) // sum(shares) for k in range(len(shares) + 1)]

    far = cuts(FAR, half_way, owners)
    near = cuts(NEAR, 1, half_way)
    pushed = []

    def begin(k, carry):
        carried_bulk(k).start()
        return carry

    def push():
        turn_now = len(pushed)
        pushed.append(turn_now)
        for bounds in (near, far):
            if bounds[turn_now] < bounds[turn_now + 1]:
                lax.fori_loop(bounds[turn_now], bounds[turn_now + 1], begin, 0)

    push()
    for level in range(LEVELS):
        X, Y = dims(level)
        p = iterates[level]
        hx = HX[level]
        for e in (2,) if level == 0 else (0, 2):

            @pl.when(jnp.logical_not(low[-1]))
            def _(p=p, e=e, Y=Y, hx=hx):
                p[e, :hx] = jnp.zeros((hx, Y + 2 * PAD, Z), jnp.float32)

            @pl.when(jnp.logical_not(low[1]))
            def _(p=p, e=e, X=X, Y=Y, hx=hx):
                p[e, hx + X :] = jnp.zeros((hx, Y + 2 * PAD, Z), jnp.float32)

            @pl.when(jnp.logical_not(side_y[-1]))
            def _(p=p, e=e, X=X, Y=Y, hx=hx):
                p[e, :, :PAD] = jnp.zeros((X + 2 * hx, PAD, Z), jnp.float32)

            @pl.when(jnp.logical_not(side_y[1]))
            def _(p=p, e=e, X=X, Y=Y, hx=hx):
                p[e, :, PAD + Y :] = jnp.zeros((X + 2 * hx, PAD, Z), jnp.float32)

    receive_copy.wait()

    def solved_arrive(k, carry):
        solved_bulk(k, incoming=True).wait_recv()
        return carry

    lax.fori_loop(1, owners, solved_arrive, 0)
    push()

    lane = lax.broadcasted_iota(jnp.int32, (8, Z), 1)
    block_lane = lane // PATCH
    lower_bits = [(block_lane // s) % 2 == 1 for s in (1, 2, 4)]

    def to_grid(step, carry):
        b = step // X0
        i = step % X0
        at = pl.multiple_of(i * 2 * Z, 2 * Z)
        rows = []
        for c in range(BZP):
            both = arrived[receive_index[b * BZP + c, 0], :, pl.ds(at, 2 * Z)].astype(
                jnp.float32
            )
            rows.append(jnp.concatenate([both[:, :Z], both[:, Z:]], axis=0))
        for bit, s in zip(lower_bits, (1, 2, 4)):
            new = list(rows)
            for c in range(BZP):
                if c & s == 0:
                    lower, upper = rows[c], rows[c + s]
                    new[c] = jnp.where(bit, pltpu.roll(upper, PATCH * s, 1), lower)
                    new[c + s] = jnp.where(bit, upper, pltpu.roll(lower, Z - PATCH * s, 1))
            rows = new
        for j in range(8):
            turn[8 * j : 8 * j + 8, :] = rows[j]
        for half in range(2):
            y = pl.multiple_of(b * PATCH + half * 8, 8)
            for f, ref in enumerate(grids):
                values = turn[pl.ds(half * SOLVED + f, 8, stride=8), :]
                ref[i + FIELD_HALO[f], pl.ds(PAD + y, 8), :] = values
        return carry

    lax.fori_loop(0, BYP * X0, to_grid, 0, unroll=8)

    def known(side, values):
        return jnp.where(has(side), values.astype(jnp.float32), 0.0)

    planes = []
    for f, h in enumerate(FIELD_HALO):
        planes += [(f, h, j) for j in range(h)]
    for n, (f, h, j) in enumerate(planes):
        for side, x in ((0, j), (1, X0 - h + j)):
            sent_x[side, n] = grids[f][h + x, PAD : PAD + Y0, :].astype(jnp.bfloat16)
    at_row = lax.broadcasted_iota(jnp.int32, (PAD, Z), 0)

    def end_rows(end, x):
        y = (0, Y0 - PAD)[end]
        u, v, w, r = (
            grids[f][h + x, PAD + y : PAD + y + PAD, :] for f, h in enumerate(FIELD_HALO)
        )
        if end == 0:
            uvw = jnp.where(
                at_row < 2, u, jnp.where(at_row < 5, pltpu.roll(v, 2, 0), pltpu.roll(w, 5, 0))
            )
        else:
            uvw = jnp.where(
                at_row > 5, u, jnp.where(at_row > 2, pltpu.roll(v, 6, 0), pltpu.roll(w, 3, 0))
            )
        return r.astype(jnp.bfloat16), uvw.astype(jnp.bfloat16)

    def keep_rows(end, x, uvw, r):
        y = (0, PAD + Y0)[end]
        u, v, w = (
            (uvw, pltpu.roll(uvw, 2, 0), pltpu.roll(uvw, 5, 0)),
            (uvw, pltpu.roll(uvw, 6, 0), pltpu.roll(uvw, 3, 0)),
        )[end]
        for f, values in enumerate((u, v, w, r)):
            h = FIELD_HALO[f]
            if -h <= x < X0 + h:
                grids[f][h + x, y : y + PAD, :] = values

    for end in range(2):
        for i in range(X0):
            sent_y[end, i], sent_y[end, X0 + i] = end_rows(end, i)
        for j in range(CORNER):
            for side, x in ((0, j), (1, X0 - CORNER + j)):
                (
                    sent_c[2 * side + end, j],
                    sent_c[2 * side + end, CORNER + j],
                ) = end_rows(end, x)

    def field_refs(side):
        dx, dy = side
        if dy == 0:
            return sent_x.at[(dx + 1) // 2], got_x.at[(1 - dx) // 2]
        if dx == 0:
            return sent_y.at[(dy + 1) // 2], got_y.at[(1 - dy) // 2]
        return sent_c.at[dx + 1 + (dy + 1) // 2], got_c.at[1 - dx + (1 - dy) // 2]

    def level_refs(level, e, into):
        X, Y = dims(level)
        p = iterates[level]
        hx = HX[level]

        def refs(side):
            dx, dy = side
            if dx == 0:
                which = into // 2
                return (
                    sent_rows[level].at[which, (dy + 1) // 2],
                    got_rows[level].at[which, (1 - dy) // 2],
                )
            h = hx if dy == 0 else CORNER_PLANES[level]
            src_x, dst_x, n_x = {
                -1: (hx, hx + X, h),
                0: (hx, hx, X),
                1: (hx + X - h, hx - h, h),
            }[dx]
            src_y, dst_y, n_y = {
                -1: (PAD, PAD + Y, PAD),
                0: (PAD, PAD, Y),
                1: (Y, 0, PAD),
            }[dy]
            return (
                p.at[e, pl.ds(src_x, n_x), pl.ds(src_y, n_y)],
                p.at[into, pl.ds(dst_x, n_x), pl.ds(dst_y, n_y)],
            )

        return refs

    def pack_rows(level, e, into):
        X, Y = dims(level)
        p, n = iterates[level], ROWS[level]
        per = PAD // n
        for end, y, first_row in ((0, PAD, 0), (1, Y, PAD - n)):
            for g in range(X // per):
                tile = None
                for k in range(per):
                    rows = p[e, HX[level] + per * g + k, y : y + PAD, :]
                    shift = (n * k - first_row) % PAD
                    rows = pltpu.roll(rows, shift, 0) if shift else rows
                    tile = rows if tile is None else jnp.where(at_row >= n * k, rows, tile)
                sent_rows[level][into // 2, end, g] = tile

    def unpack_rows(level, into):
        X, Y = dims(level)
        p, n = iterates[level], ROWS[level]
        per = PAD // n
        for end, y, first_row in ((0, 0, PAD - n), (1, PAD + Y, 0)):
            for g in range(X // per):
                tile = known((0, 2 * end - 1), got_rows[level][into // 2, end, g])
                for k in range(per):
                    shift = (first_row - n * k) % PAD
                    p[into, HX[level] + per * g + k, y : y + PAD, :] = (
                        pltpu.roll(tile, shift, 0) if shift else tile
                    )

    drains = []

    def exchange(refs, move):
        def copy(side, incoming=False):
            src, dst = refs(back(side) if incoming else side)
            return pltpu.make_async_remote_copy(
                src_ref=src,
                dst_ref=dst,
                send_sem=send_sem.at[move, SIDES.index(side)],
                recv_sem=recv_sem.at[move, SIDES.index(side if incoming else back(side))],
                device_id=peer(side),
                device_id_type=MESH,
            )

        def each(act):
            for side in SIDES:

                @pl.when(has(side))
                def _(side=side):
                    act(side)

        drains.append(lambda: each(lambda side: copy(side).wait_send()))
        return (
            lambda: each(lambda side: copy(side).start()),
            lambda: each(lambda side: copy(side, incoming=True).wait_recv()),
        )

    def level_exchange(level, e, into, move):
        pack_rows(level, e, into)
        start, arrive = exchange(level_refs(level, e, into), move)
        start()

        def finish():
            arrive()
            unpack_rows(level, into)

        return finish

    def lanes(values):
        return lax.broadcasted_iota(jnp.int32, values.shape, 1)

    def z_low(values, step):
        return jnp.where(lanes(values) < step, 0.0, pltpu.roll(values, step, 1))

    def z_high(values, step):
        return jnp.where(lanes(values) >= Z - step, 0.0, pltpu.roll(values, Z - step, 1))

    def keep_inner(level, i, at, zl, zh):
        step = 1 << level
        inner_zl[level][i, at, :] = jnp.where(lanes(zl) < step, 0.0, zl)
        inner_zh[level][i, at, :] = jnp.where(lanes(zh) >= Z - step, 0.0, zh)

    grid_u, grid_v, grid_w, grid_r = grids
    rows0 = Y0 + 2 * EDGE
    win0 = pl.ds(PAD - EDGE, rows0)

    def face(a, b):
        return 2.0 / jnp.maximum(a + b, 0.5)

    def faces(i, row=0, rows=rows0):
        at, start = pl.ds(row, rows), row + PAD - EDGE
        here = grid_r[i + 1, pl.ds(start, rows), :]
        face_x[0][i, at, :] = face(grid_r[i, pl.ds(start, rows), :], here)
        face_y[0][i, at, :] = face(grid_r[i + 1, pl.ds(start - 1, rows), :], here)
        if row + rows == rows0:
            last = PAD + EDGE + Y0
            face_y[0][i, rows0 : rows0 + EDGE, :] = face(
                grid_r[i + 1, last - 1 : last + EDGE - 1, :], grid_r[i + 1, last : last + EDGE, :]
            )
        zl, zh = face(z_low(here, 1), here), face(z_high(here, 1), here)
        face_zl[0][i, at, :] = zl
        face_zh[0][i, at, :] = zh
        keep_inner(0, i, at, zl, zh)

    def inside_rows(level, row, rows):
        Y = dims(level)[1]
        at = lax.broadcasted_iota(jnp.int32, (rows, Z), 0) + row
        return jnp.logical_and(
            jnp.logical_or(side_y[-1], at >= EDGE), jnp.logical_or(side_y[1], at < EDGE + Y)
        )

    def weigh(level, i, row=0, rows=None):
        X, Y = dims(level)
        h, rows = HALO[level], rows or Y + 2 * EDGE
        at = pl.ds(row, rows)
        total = face_x[level][i, at, :] + face_x[level][i + 1, at, :]
        total += face_y[level][i, at, :] + face_y[level][i, pl.ds(row + 1, rows), :]
        total += face_zl[level][i, at, :] + face_zh[level][i, at, :]
        inside = jnp.logical_and(
            jnp.logical_or(low[-1], i >= h), jnp.logical_or(low[1], i < h + X)
        )
        w = jnp.where(jnp.logical_and(inside_rows(level, row, rows), inside), DAMPING / total, 0.0)
        diag[level][i, at, :] = total
        weight[level][i, at, :] = w
        return w

    def first(j, row=0, rows=rows0):
        at, start = pl.ds(row, rows), row + PAD - EDGE
        mid = pl.ds(start, rows)
        w = weigh(0, j + HALO[0] - HX[0], row, rows)
        wz = grid_w[j + FIELD_HALO[2] - HX[0], mid, :]
        u_at, v_at = j + FIELD_HALO[0] - HX[0], j + FIELD_HALO[1] - HX[0]
        du = grid_u[u_at + 1, mid, :] - grid_u[u_at - 1, mid, :]
        dv = grid_v[v_at, pl.ds(start + 1, rows), :] - grid_v[v_at, pl.ds(start - 1, rows), :]
        b = -0.5 * ((du + dv) + (z_high(wz, 1) - z_low(wz, 1)))
        source[0][j, at, :] = b
        iterates[0][0, j, mid, :] = w * b

    def planes_of(act, low_j, high_j, edges_only=False, unroll=2):
        def one(j, carry):
            if edges_only:
                act(j, 0, PAD)
                act(j, rows0 - PAD, PAD)
            else:
                act(j)
            return carry

        lax.fori_loop(low_j, high_j, one, 0, unroll=unroll)

    n_faces, n_first = X0 + 2 * HALO[0], X0 + 2 * HX[0]
    face_from, face_to = HALO[0] + 1, HALO[0] + X0 - 1
    first_from, first_to = HX[0] + 1, HX[0] + X0 - 2
    field_start, field_arrive = exchange(field_refs, 0)
    field_start()
    push()

    def solved_end(k, carry):
        solved_bulk(k).wait_send()
        return carry

    lax.fori_loop(1, owners, solved_end, 0, unroll=False)
    planes_of(faces, face_from, face_to)
    planes_of(first, first_from, first_to)
    field_arrive()

    for n, (f, h, j) in enumerate(planes):
        for dx, x in ((-1, j), (1, h + X0 + j)):
            at = (dx + 1) // 2
            grids[f][x, PAD : PAD + Y0, :] = known((dx, 0), got_x[at, n])
    for end, dy in ((0, -1), (1, 1)):
        for i in range(X0):
            r, uvw = (known((0, dy), got_y[end, k * X0 + i]) for k in range(2))
            keep_rows(end, i, uvw, r)
        for j in range(CORNER):
            for side, dx, x in ((0, -1, j - CORNER), (1, 1, X0 + j)):
                r, uvw = (
                    known((dx, dy), got_c[2 * side + end, k * CORNER + j]) for k in range(2)
                )
                keep_rows(end, x, uvw, r)

    push()
    planes_of(faces, 0, face_from)
    planes_of(faces, face_to, n_faces)
    planes_of(faces, face_from, face_to, edges_only=True)
    face_x[0][n_faces] = face(grid_r[n_faces, win0, :], grid_r[n_faces + 1, win0, :])
    planes_of(first, 0, first_from, unroll=3)
    planes_of(first, first_to, n_first, unroll=4)
    planes_of(first, first_from, first_to, edges_only=True)

    def z_bit(values, level):
        return (lanes(values) // (1 << level)) % 2 == 1

    def z_pair(values, level):
        step = 1 << level
        return values + jnp.where(
            z_bit(values, level), pltpu.roll(values, step, 1), pltpu.roll(values, Z - step, 1)
        )

    def z_even(values, level):
        return jnp.where(z_bit(values, level), pltpu.roll(values, 1 << level, 1), values)

    def z_odd(values, level):
        return jnp.where(z_bit(values, level), values, pltpu.roll(values, Z - (1 << level), 1))

    def coarse_faces(level, base, start, count, more=0):
        even = pl.ds(start, count, stride=2)
        even_y = pl.ds(start, count + more, stride=2)
        odd = pl.ds(start + 1, count, stride=2)
        after = pl.ds(start + 2, count, stride=2)
        fx, fy, zl, zh = (f[level] for f in (face_x, face_y, face_zl, face_zh))

        def cx(x):
            i = base + 2 * x
            return 0.25 * z_pair(fx[i, even, :] + fx[i, odd, :], level)

        def cy(x, rows):
            i = base + 2 * x
            return 0.25 * z_pair(fy[i, rows, :] + fy[i + 1, rows, :], level)

        def four(f, x):
            i = base + 2 * x
            return 0.25 * (
                (f[i, even, :] + f[i, odd, :]) + (f[i + 1, even, :] + f[i + 1, odd, :])
            )

        return (
            cx,
            lambda x: cy(x, even_y),
            lambda x: cy(x, after),
            lambda x: z_even(four(zl, x), level),
            lambda x: z_odd(four(zh, x), level),
        )

    for level in range(LEVELS - 1):
        X, Y = dims(level + 1)
        count = Y + EDGE
        n_planes = X + 2 * HALO[level + 1]
        cx, cyl, _, czl, czh = coarse_faces(level, 0, 0, count, more=1)
        rows = pl.ds(EDGE // 2, count)

        def coarsen(i, carry, level=level, rows=rows, count=count, cx=cx, cyl=cyl, czl=czl, czh=czh):
            face_x[level + 1][i, rows, :] = cx(i)
            face_y[level + 1][i, pl.ds(EDGE // 2, count + 1), :] = cyl(i)
            zl, zh = czl(i), czh(i)
            face_zl[level + 1][i, rows, :] = zl
            face_zh[level + 1][i, rows, :] = zh
            step = 1 << (level + 1)
            inner_zl[level + 1][i, rows, :] = jnp.where(lanes(zl) < step, 0.0, zl)
            inner_zh[level + 1][i, rows, :] = jnp.where(lanes(zh) >= Z - step, 0.0, zh)
            return carry

        lax.fori_loop(0, n_planes, coarsen, 0, unroll=3)
        face_x[level + 1][n_planes, rows, :] = cx(n_planes)

        def weigh_plane(i, carry, level=level):
            weigh(level + 1, i)
            return carry

        lax.fori_loop(0, n_planes, weigh_plane, 0, unroll=3)

    X, Y = dims(LEVELS)
    cx, cyl, cyh, czl, czh = coarse_faces(LEVELS - 1, HALO[LEVELS - 1], EDGE, Y)
    for x in range(X + 1):
        gather_faces[narrow, x] = cx(x)
    for x in range(X):
        for k, part in enumerate((cyl, cyh, czl, czh)):
            gather_faces[narrow, X + 1 + k * X + x] = part(x)

    def gather(ref, which):
        def copy(d, incoming=False):
            came = lax.rem(narrow + n_narrow - d, n_narrow) if incoming else narrow
            return pltpu.make_async_remote_copy(
                src_ref=ref.at[narrow],
                dst_ref=ref.at[came],
                send_sem=gsend_sem.at[which, d - 1],
                recv_sem=grecv_sem.at[which, d - 1],
                device_id=others[d - 1],
                device_id_type=MESH,
            )

        def start():
            for d in range(1, n_narrow):
                copy(d).start()

        def finish():
            for d in range(1, n_narrow):
                copy(d, incoming=True).wait_recv()

        def drain():
            for d in range(1, n_narrow):
                copy(d).wait_send()

        return start, finish, drain

    face_start, face_finish, face_drain = gather(gather_faces, 0)
    source_start, source_finish, source_drain = gather(gather_source, 1)
    face_start()

    def neighbour_sum(level, e, x, own):
        Y = dims(level)[1]
        p = iterates[level]
        step = 1 << level
        edge = 0 if own else EDGE
        start, rows = PAD - edge, Y + 2 * edge
        at = pl.ds(EDGE - edge, rows)
        i, j = x + HALO[level], x + HX[level]
        here = p[e, j, pl.ds(start, rows), :]
        total = (
            face_x[level][i, at, :] * p[e, j - 1, pl.ds(start, rows), :]
            + face_x[level][i + 1, at, :] * p[e, j + 1, pl.ds(start, rows), :]
        )
        total += face_y[level][i, at, :] * p[e, j, pl.ds(start - 1, rows), :]
        total += face_y[level][i, pl.ds(EDGE - edge + 1, rows), :] * p[
            e, j, pl.ds(start + 1, rows), :
        ]
        total += inner_zl[level][i, at, :] * pltpu.roll(here, step, 1)
        total += inner_zh[level][i, at, :] * pltpu.roll(here, Z - step, 1)
        return here, total

    def sweep(level, e, x, own):
        Y = dims(level)[1]
        edge = 0 if own else EDGE
        here, total = neighbour_sum(level, e, x, own)
        w = weight[level][x + HALO[level], pl.ds(EDGE - edge, Y + 2 * edge), :]
        if e == 0:
            return (1.0 + KEEP) * here + w * total
        start = iterates[level][0, x + HX[level], pl.ds(PAD - edge, Y + 2 * edge), :]
        return (KEEP * here + start) + w * total

    def wide_sweep(level, e, halo):
        X, Y = dims(level)

        def plane(j, carry):
            x = j - halo
            iterates[level][e + 1, x + HX[level], pl.ds(PAD - EDGE, Y + 2 * EDGE), :] = sweep(
                level, e, x, False
            )
            return carry

        lax.fori_loop(0, X + 2 * halo, plane, 0, unroll=3 if X + 2 * halo == 18 else 2)

    finish_first = None
    for level in range(LEVELS):
        X, Y = dims(level)
        if level > 0:
            finish = level_exchange(level, 0, 0, level)
            push()
            finish()
        wide_sweep(level, 0, 1)
        if level == 0:
            finish_first = level_exchange(0, 1, 2, LEVELS)
        h, half, last = HALO[level], Y // 2, level + 1 == LEVELS
        own_rows = pl.ds(EDGE, Y)

        def restrict(x, carry, level=level, Y=Y, h=h, half=half, last=last, own_rows=own_rows):
            both = None
            for k in range(2):
                fine = 2 * x + k
                here, total = neighbour_sum(level, 1, fine, True)
                b = source[0][fine + HX[0], own_rows, :] if level == 0 else source[level][fine]
                left = (b - diag[level][fine + h, own_rows, :] * here) + total
                both = left if both is None else both + left
            tmp[:Y, :] = both
            summed = (
                tmp[pl.ds(0, half, stride=2), :] + tmp[pl.ds(1, half, stride=2), :]
            )
            summed = 0.5 * z_pair(summed, level)
            if last:
                gather_source[narrow, x] = summed
            else:
                source[level + 1][x] = summed
                w = weight[level + 1][x + HALO[level + 1], pl.ds(EDGE, half), :]
                iterates[level + 1][0, x + HX[level + 1], pl.ds(PAD, half), :] = w * summed
            return carry

        if last:
            for x in range(X // 2):
                restrict(x, 0)
        else:
            lax.fori_loop(0, X // 2, restrict, 0, unroll=4)

    source_start()
    push()
    face_finish()
    source_finish()
    X, Y = dims(LEVELS)
    step = 1 << LEVELS
    row = lax.broadcasted_iota(jnp.int32, (Y, Z), 0)
    col = lax.broadcasted_iota(jnp.int32, (Y, Z), 1)
    for n in range(n_narrow):
        for x in range(X):
            fxl, fxh = gather_faces[n, x], gather_faces[n, x + 1]
            fyl, fyh, fzl, fzh = (gather_faces[n, X + 1 + k * X + x] for k in range(4))
            total = ((fxl + fxh) + (fyl + fyh)) + (fzl + fzh)
            w = DAMPING / total
            at = n * X + x
            coef[0, at] = w * fxl
            coef[1, at] = w * fxh
            coef[2, at] = jnp.where(row == 0, 0.0, w * fyl)
            coef[3, at] = jnp.where(row == Y - 1, 0.0, w * fyh)
            coef[4, at] = jnp.where(col < step, 0.0, w * fzl)
            coef[5, at] = jnp.where(col >= Z - step, 0.0, w * fzh)
            coef[6, at] = w * gather_source[n, x]

    zero_plane = jnp.zeros((1, Y, Z), jnp.float32)

    def bottom(k, cur):
        new = KEEP * cur + coef[6]
        new += coef[0] * jnp.concatenate([zero_plane, cur[:-1]], axis=0)
        new += coef[1] * jnp.concatenate([cur[1:], zero_plane], axis=0)
        new += coef[2] * pltpu.roll(cur, 1, 1)
        new += coef[3] * pltpu.roll(cur, Y - 1, 1)
        new += coef[4] * pltpu.roll(cur, step, 2)
        new += coef[5] * pltpu.roll(cur, Z - step, 2)
        return new

    push()
    coef[7] = lax.fori_loop(0, BOTTOM - 1, bottom, coef[6], unroll=15)
    for x in range(X):
        answer[LEVELS][x] = coef[7, narrow * X + x]

    def repeat_rows(e, count):
        tmp[pl.ds(0, count, stride=2), :] = e
        tmp[pl.ds(1, count, stride=2), :] = e
        return tmp[: 2 * count, :]

    for level in reversed(range(1, LEVELS)):
        X, Y = dims(level)
        half = Y // 2

        def raised(x, carry, level=level, Y=Y, half=half):
            e = repeat_rows(answer[level + 1][x // 2], half)
            at = x + HX[level]
            iterates[level][2, at, PAD : PAD + Y, :] = (
                iterates[level][1, at, PAD : PAD + Y, :] + e
            )
            return carry

        lax.fori_loop(0, X, raised, 0, unroll=4)
        finish = level_exchange(level, 2, 2, LEVELS + level)
        push()
        finish()
        out_halo = 1 if level == 1 else 0
        wide_sweep(level, 2, 1 + out_halo)

        def close(j, carry, level=level, out_halo=out_halo):
            if out_halo:
                near_answer[j, pl.ds(PAD - EDGE, dims(level)[1] + 2 * EDGE), :] = sweep(
                    level, 3, j - out_halo, False
                )
            else:
                answer[level][j] = sweep(level, 3, j, True)
            return carry

        lax.fori_loop(0, X + 2 * out_halo, close, 0, unroll=2)

    for x in range(X0):
        iterates[0][2, x + HX[0], PAD : PAD + Y0, :] = iterates[0][1, x + HX[0], PAD : PAD + Y0, :]
    finish_first()
    coarse_rows = pl.ds(PAD - EDGE // 2, Y0 // 2 + EDGE)

    def raise_first(j, carry):
        e = repeat_rows(near_answer[j // 2, coarse_rows, :], Y0 // 2 + EDGE)
        iterates[0][2, j, win0, :] = iterates[0][2, j, win0, :] + e
        return carry

    lax.fori_loop(0, X0 + 2 * HX[0], raise_first, 0, unroll=4)
    wide_sweep(0, 2, 1)

    def close_first(x, carry):
        pressure[x] = sweep(0, 3, x, True)
        return carry

    lax.fori_loop(0, X0, close_first, 0, unroll=4)

    assert len(pushed) == len(FAR)

    def merge_solved(q, carry):
        merged[q, :SOLVED] = arrived[receive_index[q, 0]]
        return carry

    lax.fori_loop(0, PER_OWNER, merge_solved, 0, unroll=4)
    face_drain()
    source_drain()
    for drain in drains:
        drain()

    def carried_end(k, carry):
        carried_bulk(k).wait_send()
        carried_bulk(k, incoming=True).wait_recv()
        return carry

    lax.fori_loop(1, owners, carried_end, 0)

    def merge_carried(q, carry):
        merged[q, SOLVED:] = moved[receive_index[q, 0]]
        return carry

    lax.fori_loop(0, PER_OWNER, merge_carried, 0, unroll=8)


def f32(*shape):
    return pltpu.VMEM(shape, jnp.float32)


def bf16(*shape):
    return pltpu.VMEM(shape, jnp.bfloat16)


def call_solve(n_wide, n_narrow, table, fields):
    per_owner, n_fields, cells = fields.shape
    owners = n_wide * n_narrow
    slots = owners * CAPACITY
    X3, Y3 = dims(LEVELS)
    levels = [(level, *dims(level)) for level in range(LEVELS)]
    faces = [f32(X + 2 * HALO[l], Y + 2 * EDGE, Z) for l, X, Y in levels]
    moves = 2 * LEVELS
    packs = {
        "solved": bf16(slots, SOLVED, cells),
        "carried": bf16(slots, n_fields - SOLVED, cells),
    }
    dma = pltpu.SemaphoreType.DMA
    scratch = [
        pltpu.VMEM(table.shape, jnp.int32),
        bf16(*fields.shape),
        packs["solved"],
        packs["carried"],
        packs["solved"],
        packs["carried"],
        pltpu.VMEM((CAPACITY, owners, Z), jnp.int32),
        pltpu.VMEM((per_owner, Z), jnp.int32),
        pltpu.SMEM((CAPACITY, owners, Z), jnp.int32),
        pltpu.SMEM((per_owner, Z), jnp.int32),
        f32(64, Z),
        f32(Y0 + 2 * PAD, Z),
        [f32(X0 + 2 * h, Y0 + 2 * PAD, Z) for h in FIELD_HALO],
        bf16(2, HALO_PLANES, Y0, Z),
        bf16(2, HALO_PLANES, Y0, Z),
        bf16(2, 2 * X0, PAD, Z),
        bf16(2, 2 * X0, PAD, Z),
        bf16(4, 2 * CORNER, PAD, Z),
        bf16(4, 2 * CORNER, PAD, Z),
        [f32(4, X + 2 * HX[l], Y + 2 * PAD, Z) for l, X, Y in levels],
        [f32(2, 2, X * ROWS[l] // PAD, PAD, Z) for l, X, Y in levels],
        [f32(2, 2, X * ROWS[l] // PAD, PAD, Z) for l, X, Y in levels],
        [f32(X + 2 * HALO[l] + 1, Y + 2 * EDGE, Z) for l, X, Y in levels],
        [f32(X + 2 * HALO[l], Y + 2 * EDGE + 8, Z) for l, X, Y in levels],
        faces,
        faces,
        faces,
        faces,
        faces,
        faces,
        [f32(X0 + 2 * HX[0], Y0 + 2 * EDGE, Z)] + [f32(X, Y, Z) for l, X, Y in levels[1:]],
        [f32(*dims(level), Z) for level in range(LEVELS + 1)],
        f32(dims(1)[0] + 2, dims(1)[1] + 2 * PAD, Z),
        f32(n_narrow, 5 * X3 + 1, Y3, Z),
        f32(n_narrow, X3, Y3, Z),
        f32(8, n_narrow * X3, Y3, Z),
        dma((moves, 8)),
        dma((moves, 8)),
        dma((2, n_narrow - 1)),
        dma((2, n_narrow - 1)),
        dma((owners,)),
        dma((owners,)),
        dma((owners,)),
        dma((owners,)),
        dma((4,)),
    ]
    anywhere = pl.BlockSpec(memory_space=pl.ANY)
    return pl.pallas_call(
        functools.partial(solve_kernel, n_wide, n_narrow),
        out_shape=(
            jax.ShapeDtypeStruct(fields.shape, fields.dtype),
            jax.ShapeDtypeStruct((X0, Y0, Z), jnp.float32),
        ),
        in_specs=[anywhere, anywhere],
        out_specs=(pl.BlockSpec(memory_space=pltpu.VMEM),) * 2,
        scratch_shapes=scratch,
        compiler_params=pltpu.CompilerParams(
            collective_id=0, has_side_effects=True, vmem_limit_bytes=min(60, 46 + owners // 8) * 1024 * 1024
        ),
        cost_estimate=pl.CostEstimate(
            flops=200_000_000, bytes_accessed=200_000_000, transcendentals=0
        ),
    )(table, fields)


def hand_over_kernel(migrated_ref, pressure_ref, migrated_out, pressure_out, sem):
    copies = []
    for n, (src, dst) in enumerate(((migrated_ref, migrated_out), (pressure_ref, pressure_out))):
        size = src.shape[0] // PIECES
        for g in range(PIECES):
            piece = pl.ds(g * size, size)
            copies.append(pltpu.make_async_copy(src.at[piece], dst.at[piece], sem.at[n, g]))
    for copy in copies:
        copy.start()
    for copy in copies:
        copy.wait()


def hand_over(migrated, pressure):
    anywhere = pl.BlockSpec(memory_space=pl.ANY)
    return pl.pallas_call(
        hand_over_kernel,
        out_shape=tuple(jax.ShapeDtypeStruct(a.shape, a.dtype) for a in (migrated, pressure)),
        in_specs=[anywhere, anywhere],
        out_specs=(anywhere, anywhere),
        scratch_shapes=[pltpu.SemaphoreType.DMA((2, PIECES))],
        compiler_params=pltpu.CompilerParams(vmem_limit_bytes=1024 * 1024),
    )(migrated, pressure)


def shards(n_wide, n_narrow, target_slot, fields):
    return hand_over(*call_solve(n_wide, n_narrow, target_slot.reshape(-1, Z), fields))


def solution(mesh):
    body = functools.partial(shards, mesh.shape["wide"], mesh.shape["narrow"])
    in_specs = (P(), P(("wide", "narrow"), None, None))
    out_specs = (P(("wide", "narrow"), None, None), P("narrow", "wide", None))
    return jax.shard_map(body, mesh=mesh, in_specs=in_specs, out_specs=out_specs, check_vma=False)
```
